512 devices in a mesh: row: 16 (over z_lo, core), col: 8 (over z_hi, x), feat: 4 (over y).
Axes of the slice: x: 4, y: 4, z: 16 (z_hi: 2, z_lo: 8; z = z_hi * 8 + z_lo), core: 2. Of those that a mesh axis runs over, the one named last changes fastest.
Arguments:
- snapshots: bfloat16 [2048, 32768], P(('row', 'col'), 'feat'), may hold values from -6 to 6
- start_block: float32 [2048, 32], P('row'), may hold values from -6 to 6
Outputs:
- eigen_basis: float32 [2048, 32], P('row')
The draws below stay inside these ranges and needn't reach their ends.
All inputs are finite; a program needn't handle non-finite values.
Results may differ from the reference program's by a relative error of at most 0.0003.
Values may be sent and summed in bfloat16 or wider, within the bound.
A program may use at most 64 MiB of HBM per device.

```python
import math
import jax
import jax.numpy as jnp
from jax import lax

BLOCK = 128
PTS = 32768
LAGS = 128
VECS = 32
ITERS = 6
SNAPS = 2048


def draw_snapshots(key, part):
    keys = jax.random.split(key, 9)
    period = BLOCK * 10.0 / 7.0
    duration = period / 2.0
    event_count = max(2, SNAPS // (2 * BLOCK))
    amp_low = 0.2
    amp_high = 3.0
    innovations = jax.random.normal(keys[0], (SNAPS, PTS), jnp.float32)
    noise = jax.random.normal(keys[1], (SNAPS, PTS), jnp.float32)
    event_gain = 1.5
    amplitude = jnp.exp(jax.random.uniform(keys[2], (PTS,), jnp.float32, math.log(amp_low), math.log(amp_high)))
    amplitude = amplitude / jnp.sqrt(jnp.mean(amplitude * amplitude))
    phase = jax.random.uniform(keys[3], (PTS,), jnp.float32, -math.pi, math.pi)
    horizon = jnp.exp(jax.random.uniform(keys[4], (PTS,), jnp.float32, math.log(BLOCK / 50.0), math.log(2.0 * BLOCK)))
    memory = jnp.exp(-1.0 / horizon)
    drive = jnp.sqrt(1.0 - memory * memory)
    begin = jax.random.normal(keys[5], (PTS,), jnp.float32)

    def advance(state, innovation):
        fresh = memory * state + drive * innovation
        return (fresh, fresh)
    unused, anomaly = lax.scan(advance, begin, innovations)
    times = jnp.arange(SNAPS, dtype=jnp.float32)
    starts = jax.random.uniform(keys[6], (event_count,), jnp.float32, -duration, float(SNAPS))
    offset = times[:, None] - starts[None, :]
    inside = jnp.logical_and(offset >= 0.0, offset < duration)
    bump = jnp.where(inside, jnp.sin(math.pi * offset / duration) ** 2, 0.0)
    centres = jax.random.uniform(keys[7], (event_count,), jnp.float32, 0.0, float(PTS))
    points = jnp.arange(PTS, dtype=jnp.float32)
    distance_along = jnp.mod(points[None, :] - centres[:, None], float(PTS))
    patch = (distance_along < PTS / 8.0).astype(jnp.float32)
    strength = jnp.exp(jax.random.uniform(keys[8], (event_count, PTS), jnp.float32, math.log(0.5), math.log(2.0)))
    pattern = patch * strength
    event_term = jnp.dot(bump, pattern, precision=lax.Precision.HIGHEST)
    envelope = 1.0 + jnp.sum(bump, axis=1)
    cycle = math.sqrt(2.0) * jnp.cos(2.0 * math.pi * times[:, None] / period + phase[None, :])
    core = math.sqrt(0.6) * cycle + math.sqrt(0.25) * envelope[:, None] * anomaly + math.sqrt(0.15) * noise
    field = amplitude[None, :] * core + event_gain * event_term
    return jnp.clip(field, -6.0, 6.0).astype(jnp.bfloat16)


def block_levels(own_key, extent, cuts, least, high):
    loudness = 1.0
    for axis_at, blocks in cuts:
        heights = jax.random.uniform(jax.random.fold_in(jax.random.fold_in(own_key, 6), axis_at), (blocks,), jnp.float32, least / len(cuts), high / len(cuts))
        loudness = loudness * jnp.repeat(jnp.exp(heights), extent[axis_at] // blocks).reshape((-1,) + (1,) * (len(extent) - 1 - axis_at))
    return loudness


def bell_draw(key, shape, width, bound, cuts=(), kind=jnp.bfloat16):
    array = jax.random.normal(key, shape, jnp.float32) * width
    if len(cuts) > 0:
        array = block_levels(key, shape, cuts, -0.22, 0.18) * array
    return jnp.clip(array, min=-bound, max=bound).astype(kind)


def setup_inputs(seed: int = 0) -> dict:
    seeds = jax.random.split(jax.random.key(seed), 3)
    return {
        "snapshots": draw_snapshots(jax.random.fold_in(seeds[2], 71), 0),
        "start_block": bell_draw(seeds[1], (SNAPS, VECS), 1.0, 6.0, ((0, 16),), jnp.float32),
    }


kernel_spread = 0.25
highest = lax.Precision.HIGHEST

def lag_window(distance):
    rim = LAGS - 1
    padded = jnp.pad(distance, ((rim, 0), (rim, 0)))
    running = jnp.zeros_like(distance)
    size_now = distance.shape[0]
    for lag_index in range(LAGS):
        begin = rim - lag_index
        running = running + padded[begin:begin + size_now, begin:begin + size_now]
    return running

def reference(snapshots, start_block):
    field = snapshots.astype(jnp.float32)
    norms = lax.optimization_barrier(jnp.sum(field * field, axis=1))
    gram = jnp.dot(field.astype(jnp.float32), field.T.astype(jnp.float32), precision=highest, preferred_element_type=jnp.float32)
    distance = norms[:, None] + norms[None, :] - 2.0 * gram
    lagged = lag_window(distance)
    idents = jnp.arange(SNAPS, dtype=jnp.int32)
    counts = jnp.minimum(jnp.minimum(idents[:, None], idents[None, :]), LAGS - 1) + 1
    kernel = jnp.exp(-(lagged / (counts.astype(jnp.float32) * PTS)) / kernel_spread)
    degrees = lax.optimization_barrier(jnp.sum(kernel, axis=1))
    scales = lax.rsqrt(degrees)
    markov = kernel * scales[:, None] * scales[None, :]
    basis = start_block
    for rounds in range(ITERS):
        product = jnp.dot(markov.astype(jnp.float32), basis.astype(jnp.float32), precision=highest, preferred_element_type=jnp.float32)
        small = jnp.dot(product.T.astype(jnp.float32), product.astype(jnp.float32), precision=highest, preferred_element_type=jnp.float32)
        factor = jnp.linalg.cholesky(small)
        basis = jax.scipy.linalg.solve_triangular(factor, product.T, lower=True).T
    return basis * math.sqrt(SNAPS)
```

```python
import functools
import math

import jax
import jax.numpy as jnp
from jax import lax
from jax.experimental import pallas as pl
from jax.experimental.pallas import tpu as pltpu
from jax.sharding import PartitionSpec as P

PTS = 32768
LAGS = 128
SNAPS = 2048
MESH = pl.DeviceIdType.MESH
HIGH = lax.Precision.HIGHEST
F32 = jnp.float32
BF16 = jnp.bfloat16


def place():
    row, col, y = lax.axis_index("row"), lax.axis_index("col"), lax.axis_index("feat")
    x, z_hi = lax.rem(col, 4), lax.div(col, 4)
    core, z_lo = lax.rem(row, 2), lax.div(row, 2)
    return x, y, z_hi * 8 + z_lo, core


def device(x, y, z, core):
    return (lax.rem(z, 8) * 2 + core, lax.div(z, 8) * 4 + x, y)


def send(src, dst, send_sem, recv_sem, target):
    copy = pltpu.make_async_remote_copy(
        src_ref=src, dst_ref=dst, send_sem=send_sem, recv_sem=recv_sem,
        device_id=target, device_id_type=MESH,
    )
    copy.start()
    return copy


def greet(targets):
    barrier = pltpu.get_barrier_semaphore()
    for target in targets:
        pl.semaphore_signal(barrier, inc=1, device_id=target, device_id_type=MESH)
    pl.semaphore_wait(barrier, len(targets))


def dot(a, b, dims, precision=None):
    return lax.dot_general(
        a, b, (dims, ((), ())), precision=precision, preferred_element_type=F32
    )


def distance_kernel(
    x_ref, start_ref, dist_ref, basis_ref,
    zbuf, abuf, bbuf, part, sib, own, upbuf, downbuf, stage,
    z_send, z_recv, plane_send, plane_recv, gather_send, gather_recv,
    sib_send, sib_recv, up_send, up_recv, down_send, down_recv,
    agu_send, agu_recv, agd_send, agd_recv, st_send, st_recv,
):
    x, y, z, core = place()
    me = z * 2 + core
    row = lax.rem(z, 8) * 2 + core

    def line(t):
        return device(x, y, lax.div(t, 2), lax.rem(t, 2))

    def along_x(k):
        return device(lax.rem(x + k, 4), y, z, core)

    def along_y(k):
        return device(x, lax.rem(y + k, 4), z, core)

    sibling = device(x, y, z, 1 - core)
    above = device(x, y, lax.rem(z + 1, 16), core)
    below = device(x, y, lax.rem(z + 15, 16), core)
    greet([line(lax.rem(me + o, 32)) for o in range(1, 32)]
          + [along_x(k) for k in (1, 2, 3)] + [along_y(k) for k in (1, 2, 3)])

    def slot(t):
        z_from, core_from = lax.div(t, 2), lax.rem(t, 2)
        z_lo, z_hi = lax.rem(z_from, 8), lax.div(z_from, 8)
        return lax.div(z_lo, 2), lax.rem(z_lo, 2) * 4 + core_from * 2 + z_hi

    def columns(t):
        return pl.ds(pl.multiple_of(t * 256, 256), 256)

    big, small = slot(me)
    copies = []
    for o in range(1, 32):
        t = lax.rem(me + o, 32)
        copies.append(send(x_ref.at[:, columns(t)], zbuf.at[big, small],
                           z_send.at[o], z_recv.at[o], line(t)))
    zbuf[big, small] = x_ref[:, columns(me)]
    for copy in copies:
        copy.wait()

    giver = lax.div(row, 4) == y
    basis_slot = lax.rem(row, 4)

    def basis_copy(o):
        t = lax.rem(row + o, 16)
        return pltpu.make_async_remote_copy(
            src_ref=start_ref, dst_ref=basis_ref.at[basis_slot],
            send_sem=st_send.at[o], recv_sem=st_recv.at[basis_slot],
            device_id=(t, lax.axis_index("col"), y), device_id_type=MESH)

    @pl.when(giver)
    def _():
        for o in range(1, 16):
            basis_copy(o).start()
        basis_ref[basis_slot] = start_ref[...]

    a_copies, b_copies = [], []
    for k in (1, 2, 3):
        a_copies.append(send(zbuf.at[lax.rem(x + k, 4)], abuf.at[y, :, x],
                             plane_send.at[0, k], plane_recv.at[0, k], along_x(k)))
        b_copies.append(send(zbuf.at[lax.rem(y + k, 4)], bbuf.at[y, :, x],
                             plane_send.at[1, k], plane_recv.at[1, k], along_y(k)))
    abuf[y, :, x] = zbuf[x]
    bbuf[y, :, x] = zbuf[y]
    gathers = []
    for copy in a_copies:
        copy.wait()
    for k in (1, 2, 3):
        gathers.append(send(abuf.at[y], abuf.at[y],
                            gather_send.at[0, k], gather_recv.at[0, k], along_y(k)))
    for copy in b_copies:
        copy.wait()
    for k in (1, 2, 3):
        gathers.append(send(bbuf.at[:, :, x], bbuf.at[:, :, x],
                            gather_send.at[1, k], gather_recv.at[1, k], along_x(k)))
    for copy in gathers:
        copy.wait()

    products = jnp.zeros((512, 512), F32)
    a_norm = jnp.zeros((512, 1), F32)
    b_norm = jnp.zeros((8, 512), F32)
    for q in range(4):
        a = abuf[q].reshape(512, 256)
        b = bbuf[q].reshape(512, 256)
        products += dot(a, b, ((1,), (1,)))
        a_wide, b_wide = a.astype(F32), b.astype(F32)
        a_norm += jnp.sum(a_wide * a_wide, axis=1, keepdims=True)
        b_norm += dot(jnp.ones((8, 256), F32), b_wide * b_wide, ((1,), (1,)), HIGH)
    part[...] = (a_norm + b_norm[0:1] - 2.0 * products).reshape(2, 16, 16, 512)

    copy = send(part.at[1 - core], sib, sib_send, sib_recv, sibling)
    copy.wait()
    own[...] = part[core] + sib[...]

    def chunk(q):
        return lax.rem(q + 32, 16)

    ups, downs = [], []
    for s in range(8):
        q = chunk(z + 8 - s)
        if s == 0:
            source = own.at[q]
        else:
            ups[-1].wait_recv()
            stage[0, s] = upbuf[s - 1] + own[q]
            source = stage.at[0, s]
        ups.append(send(source, upbuf.at[s], up_send.at[s], up_recv.at[s], above))
        if s < 7:
            q = chunk(z - 7 + s)
            if s == 0:
                source = own.at[q]
            else:
                downs[-1].wait_recv()
                stage[1, s] = downbuf[s - 1] + own[q]
                source = stage.at[1, s]
            downs.append(send(source, downbuf.at[s], down_send.at[s], down_recv.at[s], below))
    ups[-1].wait_recv()
    downs[-1].wait_recv()
    dist_ref[z] = own[z] + upbuf[7] + downbuf[6]
    ag_up, ag_down = [], []
    for s in range(8):
        if s:
            ag_up[-1].wait_recv()
        q = chunk(z - s)
        ag_up.append(send(dist_ref.at[q], dist_ref.at[q], agu_send.at[s], agu_recv.at[s], above))
        if s < 7:
            if s:
                ag_down[-1].wait_recv()
            q = chunk(z + s)
            ag_down.append(send(dist_ref.at[q], dist_ref.at[q], agd_send.at[s], agd_recv.at[s], below))
    ag_up[-1].wait_recv()
    ag_down[-1].wait_recv()
    for copy in ups + downs + ag_up + ag_down:
        copy.wait_send()

    @pl.when(giver)
    def _():
        for o in range(1, 16):
            basis_copy(o).wait_send()

    for k in range(4):
        @pl.when(row != 4 * y + k)
        def _():
            pltpu.make_async_remote_copy(
                src_ref=start_ref, dst_ref=basis_ref.at[k],
                send_sem=st_send.at[0], recv_sem=st_recv.at[k],
                device_id=sibling, device_id_type=MESH).wait_recv()


def inverse_factor(gram):
    rows = lax.broadcasted_iota(jnp.int32, (32, 128), 0)
    lanes = lax.broadcasted_iota(jnp.int32, (32, 128), 1)
    work = jnp.where(lanes < 32, gram, jnp.where(lanes - 32 == rows, 1.0, 0.0))
    for k in range(31):
        top = work[k:k + 1, :]
        ratio = work[:, k:k + 1] / top[:, k:k + 1]
        work = work - jnp.where(rows > k, ratio, 0.0) * top
    diagonal = jnp.sum(jnp.where(lanes == rows, work, 0.0), axis=1, keepdims=True)
    return work[:, 32:64] / jnp.sqrt(diagonal)


def basis_kernel(
    dist_ref, start_ref, out_ref,
    ext, kern, deg, wide, outgo, income, final,
    halo_send, halo_recv, sib_send, sib_recv, deg_send, deg_recv,
    step_send, step_recv, fin_send, fin_recv,
):
    x, y, z, core = place()
    z_lo = lax.rem(z, 8)
    x_next = lax.rem(x + core, 4)

    def along_x(k):
        return device(lax.rem(x + k, 4), y, z, core)

    def along_y(k):
        return device(x, lax.rem(y + k, 4), z, core)

    y_next = lax.rem(y + 1, 4)
    sibling = device(x, y, z, 1 - core)
    down = device(x_next, y, z, 1 - core)
    right = device(x, y_next, z, core)
    diagonal = device(x_next, y_next, z, 1 - core)
    x_prev, y_prev = lax.rem(x + 3 + core, 4), lax.rem(y + 3, 4)
    up = device(x_prev, y, z, 1 - core)
    up_left = device(x_prev, y_prev, z, 1 - core)
    greet([sibling, down, up, diagonal, up_left]
          + [along_x(k) for k in (1, 2, 3)] + [along_y(k) for k in (1, 2, 3)])

    copies = [
        send(dist_ref.at[pl.ds(128, 128), :], ext.at[pl.ds(0, 128), pl.ds(128, 512)],
             halo_send.at[0], halo_recv.at[0], down),
        send(dist_ref.at[:, pl.ds(384, 128)], ext.at[pl.ds(128, 256), pl.ds(0, 128)],
             halo_send.at[1], halo_recv.at[1], right),
        send(dist_ref.at[pl.ds(128, 128), pl.ds(384, 128)], ext.at[pl.ds(0, 128), pl.ds(0, 128)],
             halo_send.at[2], halo_recv.at[2], diagonal),
    ]
    ext[128:384, 128:640] = dist_ref[...]
    for copy in copies:
        copy.wait()
    rows = lax.broadcasted_iota(jnp.int32, (384, 640), 0)
    lanes = lax.broadcasted_iota(jnp.int32, (384, 640), 1)
    first_row = jnp.where(2 * x + core == 0, 128, 0)
    first_lane = jnp.where(y == 0, 128, 0)
    run = jnp.where((rows >= first_row) & (lanes >= first_lane), ext[...], 0.0)
    stride = 1
    while stride < LAGS:
        run = run + pltpu.roll(pltpu.roll(run, stride, 0), stride, 1)
        stride *= 2
    lagged = run[128:, 128:]
    i = lax.broadcasted_iota(jnp.int32, (256, 512), 0) + (x * 512 + core * 256)
    j = lax.broadcasted_iota(jnp.int32, (256, 512), 1) + y * 512
    counts = (jnp.minimum(jnp.minimum(i, j), LAGS - 1) + 1).astype(F32)
    kern[core] = jnp.exp(-(lagged / (counts * (PTS * 0.25))))
    copy = send(kern.at[core], kern.at[core], sib_send, sib_recv, sibling)
    copy.wait()
    tile = kern[...].reshape(512, 512)

    ones = jnp.ones((8, 512), F32)
    deg[0, y] = dot(ones, tile, ((1,), (1,)), HIGH)
    deg[1, x] = dot(ones, tile, ((1,), (0,)), HIGH)
    copies = []
    for k in (1, 2, 3):
        copies.append(send(deg.at[0, y], deg.at[0, y], deg_send.at[0, k], deg_recv.at[0, k], along_y(k)))
        copies.append(send(deg.at[1, x], deg.at[1, x], deg_send.at[1, k], deg_recv.at[1, k], along_x(k)))
    for copy in copies:
        copy.wait()

    def four(ref):
        return (ref[0] + ref[1]) + (ref[2] + ref[3])

    scale_row = 1.0 / jnp.sqrt(four(deg.at[0])[0:1])
    scale_col = 1.0 / jnp.sqrt(four(deg.at[1])[0:1])

    wide[...] = jnp.zeros_like(wide)

    def gram_of(block):
        wide[0:32, :] = block
        return dot(block, wide[...], ((1,), (1,)), HIGH)

    basis = jnp.concatenate([start_ref[q] for q in range(4)], axis=1)
    pending = jnp.zeros((32, 128), F32)
    inverse = None
    for step in range(6):
        over_y = step % 2 == 0
        mine = y if over_y else x
        if over_y:
            product = dot(basis * scale_col, tile, ((1,), (1,)), HIGH) * scale_row
        else:
            product = dot(basis * scale_row, tile, ((1,), (0,)), HIGH) * scale_col
        send_gram = step in (2, 4)
        width = 640 if send_gram else 512
        income[step, mine, :, 0:512] = product
        if send_gram:
            income[step, mine, :, 512:640] = pending
        copies = []
        for k in (1, 2, 3):
            view = income.at[step, mine, :, pl.ds(0, width)]
            copies.append(send(view, view, step_send.at[step, k], step_recv.at[step, k],
                               along_y(k) if over_y else along_x(k)))
        if step in (3, 5):
            inverse = inverse_factor(gram)
        for copy in copies:
            copy.wait()
        total = four(income.at[step, :, :, pl.ds(0, width)])
        basis = total[:, :512]
        if send_gram:
            gram = total[:, 512:]
        if step in (3, 5):
            basis = dot(inverse, basis, ((1,), (0,)), HIGH)
        if step in (1, 3, 5):
            pending = gram_of(basis)

    owner = lax.div(z_lo, 2)
    final[0, y] = pending
    copies = []
    for k in (1, 2, 3):
        copies.append(send(final.at[0, y], final.at[0, y], fin_send.at[k], fin_recv.at[k], along_y(k)))

    def row_copy(k):
        return pltpu.make_async_remote_copy(
            src_ref=final.at[1, 0], dst_ref=final.at[1, 0],
            send_sem=fin_send.at[3 + k], recv_sem=fin_recv.at[0],
            device_id=along_y(k), device_id_type=MESH)

    @pl.when(y == owner)
    def _():
        for q in range(4):
            @pl.when(lax.rem(z_lo, 2) * 2 + core == q)
            def _():
                final[1, 0] = basis[:, q * 128:(q + 1) * 128]
        for k in (1, 2, 3):
            row_copy(k).start()
        for k in (1, 2, 3):
            row_copy(k).wait_send()

    for copy in copies:
        copy.wait()
    inverse = inverse_factor(four(final.at[0]))

    @pl.when(y != owner)
    def _():
        row_copy(1).wait_recv()

    out_ref[...] = dot(inverse, final[1, 0], ((1,), (0,)), HIGH) * math.sqrt(SNAPS)


VMEM = pl.BlockSpec(memory_space=pltpu.VMEM)
DMA = pltpu.SemaphoreType.DMA


def body(snapshots, start_block):
    dist, start = pl.pallas_call(
        distance_kernel,
        out_shape=(jax.ShapeDtypeStruct((16, 16, 512), F32),
                   jax.ShapeDtypeStruct((4, 32, 128), F32)),
        in_specs=[VMEM, VMEM],
        out_specs=(VMEM, VMEM),
        scratch_shapes=[
            pltpu.VMEM((4, 8, 16, 256), BF16),
            pltpu.VMEM((4, 8, 4, 16, 256), BF16),
            pltpu.VMEM((4, 8, 4, 16, 256), BF16),
            pltpu.VMEM((2, 16, 16, 512), F32),
            pltpu.VMEM((16, 16, 512), F32),
            pltpu.VMEM((16, 16, 512), F32),
            pltpu.VMEM((8, 16, 512), F32),
            pltpu.VMEM((7, 16, 512), F32),
            pltpu.VMEM((2, 8, 16, 512), F32),
            DMA((32,)), DMA((32,)), DMA((2, 4)), DMA((2, 4)), DMA((2, 4)), DMA((2, 4)),
            DMA, DMA, DMA((8,)), DMA((8,)), DMA((7,)), DMA((7,)),
            DMA((8,)), DMA((8,)), DMA((7,)), DMA((7,)), DMA((16,)), DMA((4,)),
        ],
        compiler_params=pltpu.CompilerParams(
            collective_id=1, has_side_effects=True, vmem_limit_bytes=40 << 20),
        name="distances",
    )(snapshots, start_block.T)
    out = pl.pallas_call(
        basis_kernel,
        out_shape=jax.ShapeDtypeStruct((32, 128), F32),
        in_specs=[VMEM, VMEM],
        out_specs=VMEM,
        scratch_shapes=[
            pltpu.VMEM((384, 640), F32),
            pltpu.VMEM((2, 256, 512), F32),
            pltpu.VMEM((2, 4, 8, 512), F32),
            pltpu.VMEM((128, 512), F32),
            pltpu.VMEM((8, 128), F32),
            pltpu.VMEM((6, 4, 32, 640), F32),
            pltpu.VMEM((2, 4, 32, 128), F32),
            DMA((3,)), DMA((3,)), DMA, DMA, DMA((2, 4)), DMA((2, 4)),
            DMA((6, 4)), DMA((6, 4)), DMA((7,)), DMA((4,)),
        ],
        compiler_params=pltpu.CompilerParams(
            collective_id=2, has_side_effects=True, vmem_limit_bytes=40 << 20),
        name="subspace",
    )(dist.reshape(256, 512), start)
    return out.T


def solution(mesh):
    placed = (P(("row", "col"), "feat"), P("row", None))
    return jax.shard_map(
        body, mesh=mesh, in_specs=placed, out_specs=P("row", None), check_vma=False
    )
```

```python
import math

import jax
import jax.numpy as jnp
from jax import lax
from jax.experimental import pallas as pl
from jax.experimental.pallas import tpu as pltpu
from jax.sharding import PartitionSpec as P

PTS = 32768
LAGS = 128
SNAPS = 2048
PLANES = (1, 5, 9, 13)
MESH = pl.DeviceIdType.MESH
HIGH = lax.Precision.HIGHEST
F32 = jnp.float32
BF16 = jnp.bfloat16


def device(x, y, z, core):
    return (lax.rem(z, 8) * 2 + core, lax.div(z, 8) * 4 + x, y)


def remote(src, dst, send_sem, recv_sem, target):
    return pltpu.make_async_remote_copy(
        src_ref=src, dst_ref=dst, send_sem=send_sem, recv_sem=recv_sem,
        device_id=target, device_id_type=MESH,
    )


def send(*args):
    copy = remote(*args)
    copy.start()
    return copy


def dot(a, b, dims, precision=None):
    return lax.dot_general(
        a, b, (dims, ((), ())), precision=precision, preferred_element_type=F32
    )


def parts(value, count):
    out = []
    for _ in range(count):
        out.append(value.astype(BF16))
        value = value - out[-1].astype(F32)
    return out


def inverse_factor(gram):
    rows = lax.broadcasted_iota(jnp.int32, (32, 128), 0)
    lanes = lax.broadcasted_iota(jnp.int32, (32, 128), 1)
    work = jnp.where(lanes < 32, gram, jnp.where(lanes - 32 == rows, 1.0, 0.0))
    for k in range(31):
        top = work[k:k + 1, :]
        ratio = work[:, k:k + 1] / top[:, k:k + 1]
        work = work - jnp.where(rows > k, ratio, 0.0) * top
    diagonal = jnp.sum(jnp.where(lanes == rows, work, 0.0), axis=1, keepdims=True)
    return work[:, 32:64] / jnp.sqrt(diagonal)


def four(ref):
    return (ref[0] + ref[1]) + (ref[2] + ref[3])


def kernel(
    x_ref, start_ref, out_ref,
    zbuf, abuf, bbuf, part, sib, own, rsbuf, total, dist, start,
    ext, kern_hi, kern_lo, deg_row, deg_col, wide, income, grams, last, last_rows, last_grams,
    z_send, z_recv, plane_send, plane_recv, gather_send, gather_recv,
    sib_send, sib_recv, rs_send, rs_recv, ag_send, ag_recv, st_send, st_recv,
    halo_send, halo_recv, core_send, core_recv, deg_send, deg_recv,
    step_send, step_recv, gram_send, gram_recv, fin_send, fin_recv, row_send, row_recv,
):
    row, col, y = lax.axis_index("row"), lax.axis_index("col"), lax.axis_index("feat")
    x, z_hi = lax.rem(col, 4), lax.div(col, 4)
    core, z_lo = lax.rem(row, 2), lax.div(row, 2)
    z = z_hi * 8 + z_lo
    me = z * 2 + core
    group = lax.div(z, 4)
    iterates = lax.rem(z, 4) == 1

    def line(t):
        return device(x, y, lax.div(t, 2), lax.rem(t, 2))

    def along_x(k, c=core):
        return device(lax.rem(x + k, 4), y, z, c)

    def along_y(k, c=core):
        return device(x, lax.rem(y + k, 4), z, c)

    sibling = device(x, y, z, 1 - core)
    barrier = pltpu.get_barrier_semaphore()
    partners = ([line(lax.rem(me + o, 32)) for o in range(1, 32)]
                + [along_x(k) for k in (1, 2, 3)] + [along_y(k) for k in (1, 2, 3)])
    for target in partners:
        pl.semaphore_signal(barrier, inc=1, device_id=target, device_id_type=MESH)
    pl.semaphore_wait(barrier, len(partners))

    def columns(t, h):
        return pl.ds(pl.multiple_of(t * 256 + h * 128, 128), 128)

    big, small = lax.div(z_lo, 2), lax.rem(z_lo, 2) * 4 + core * 2 + z_hi
    for h in (0, 1):
        for o in range(1, 32):
            t = lax.rem(me + o, 32)
            send(x_ref.at[:, columns(t, h)], zbuf.at[h, big, small],
                 z_send.at[h, o], z_recv.at[h, o], line(t))
        zbuf[h, big, small] = x_ref[:, columns(me, h)]

    giver = lax.div(row, 4) == y
    basis_slot = lax.rem(row, 4)

    def basis_copy(n, t):
        return remote(start_ref, start.at[basis_slot], st_send.at[n], st_recv.at[basis_slot],
                      (t, col, y))

    for n, t in enumerate((2, 3, 10, 11)):
        @pl.when(giver & (row != t))
        def _():
            basis_copy(n, t).start()

    @pl.when(giver)
    def _():
        start[basis_slot] = start_ref[...]

    first = []
    for h in (0, 1):
        for o in range(1, 32):
            remote(x_ref.at[:, columns(0, h)], zbuf.at[h, 0, 0],
                   z_send.at[h, o], z_recv.at[h, o], sibling).wait()
        pairs = []
        for k in (1, 2, 3):
            pairs.append((
                send(zbuf.at[h, lax.rem(x + k, 4)], abuf.at[h, y, :, x],
                     plane_send.at[h, 0, k], plane_recv.at[h, 0, k], along_x(k)),
                send(zbuf.at[h, lax.rem(y + k, 4)], bbuf.at[h, y, :, x],
                     plane_send.at[h, 1, k], plane_recv.at[h, 1, k], along_y(k))))
        first.append(pairs)
        abuf[h, y, :, x] = zbuf[h, x]
        bbuf[h, y, :, x] = zbuf[h, y]
    gathers = []
    for h in (0, 1):
        group_copies = []
        for copy, _ in first[h]:
            copy.wait()
        for k in (1, 2, 3):
            group_copies.append(send(abuf.at[h, y], abuf.at[h, y],
                                     gather_send.at[h, 0, k], gather_recv.at[h, 0, k], along_y(k)))
        for _, copy in first[h]:
            copy.wait()
        for k in (1, 2, 3):
            group_copies.append(send(bbuf.at[h, :, :, x], bbuf.at[h, :, :, x],
                                     gather_send.at[h, 1, k], gather_recv.at[h, 1, k], along_x(k)))
        gathers.append(group_copies)

    for h in (0, 1):
        for copy in gathers[h]:
            copy.wait()
        b = jnp.concatenate([bbuf[h, q].reshape(512, 128) for q in range(4)], axis=1)
        b_wide = b.astype(F32)
        ones = jnp.ones((16, 512), BF16)
        b_norm = sum(dot(ones, p, ((1,), (1,))) for p in parts(b_wide * b_wide, 2))[0:1]
        for half in (1 - core, core):
            a = jnp.concatenate(
                [abuf[h, q, pl.ds(half * 4, 4)].reshape(256, 128) for q in range(4)], axis=1)
            a_wide = a.astype(F32)
            a_norm = jnp.sum(a_wide * a_wide, axis=1, keepdims=True)
            value = (a_norm + b_norm - 2.0 * dot(a, b, ((1,), (1,)))).reshape(4, 4, 16, 512)
            if h == 1:
                value = value + part[half]
            part[half] = value
            if h == 1 and half is not core:
                core_sums = [send(part.at[half, n], sib.at[n], sib_send.at[n], sib_recv.at[n], sibling)
                             for n in range(4)]

    def scatter(n, i, q):
        return remote(own.at[n, i], rsbuf.at[z], rs_send.at[0], rs_recv.at[0],
                      device(x, y, q, core))

    for n in range(4):
        core_sums[n].wait()
        own[n] = part[core, n] + sib[n]
        for i in range(4):
            q = n * 4 + i

            @pl.when(z != q)
            def _():
                scatter(n, i, q).start()

            @pl.when(z == q)
            def _():
                rsbuf[q] = own[n, i]
    remote(rsbuf.at[pl.ds(0, 15)], rsbuf.at[pl.ds(0, 15)], rs_send.at[0], rs_recv.at[0], sibling).wait()
    chunk = rsbuf[0]
    for q in range(1, 16):
        chunk = chunk + rsbuf[q]
    total[...] = chunk

    my_rows = pl.ds(pl.multiple_of(z * 16, 16), 16)

    def gather(n, p):
        return remote(total, dist.at[my_rows, :], ag_send.at[n], ag_recv.at[0], device(x, y, p, core))

    for n, p in enumerate(PLANES):
        @pl.when(z != p)
        def _():
            gather(n, p).start()

    @pl.when(iterates)
    def _():
        dist[my_rows, :] = total[...]
        remote(dist.at[pl.ds(0, 240), :], dist.at[pl.ds(0, 240), :],
               ag_send.at[4], ag_recv.at[0], sibling).wait_recv()

        x_next, y_next = lax.rem(x + core, 4), lax.rem(y + 1, 4)
        halo = [
            send(dist.at[pl.ds(128, 128), :], ext.at[pl.ds(0, 128), pl.ds(128, 512)],
                 halo_send.at[0], halo_recv.at[0], device(x_next, y, z, 1 - core)),
            send(dist.at[:, pl.ds(384, 128)], ext.at[pl.ds(128, 256), pl.ds(0, 128)],
                 halo_send.at[1], halo_recv.at[1], device(x, y_next, z, core)),
            send(dist.at[pl.ds(128, 128), pl.ds(384, 128)], ext.at[pl.ds(0, 128), pl.ds(0, 128)],
                 halo_send.at[2], halo_recv.at[2], device(x_next, y_next, z, 1 - core)),
        ]
        ext[128:384, 128:640] = dist[...]
        for copy in halo:
            copy.wait()
        rows = lax.broadcasted_iota(jnp.int32, (384, 640), 0)
        lanes = lax.broadcasted_iota(jnp.int32, (384, 640), 1)
        first_row = jnp.where(2 * x + core == 0, 128, 0)
        first_lane = jnp.where(y == 0, 128, 0)
        run = jnp.where((rows >= first_row) & (lanes >= first_lane), ext[...], 0.0)
        stride = 1
        while stride < LAGS:
            run = run + pltpu.roll(pltpu.roll(run, stride, 0), stride, 1)
            stride *= 2
        lagged = run[128:, 128:]
        i = lax.broadcasted_iota(jnp.int32, (256, 512), 0) + (x * 512 + core * 256)
        j = lax.broadcasted_iota(jnp.int32, (256, 512), 1) + y * 512
        counts = (jnp.minimum(jnp.minimum(i, j), LAGS - 1) + 1).astype(F32)
        half_tile = jnp.exp(-(lagged / (counts * (PTS * 0.25))))
        half_hi, half_lo = parts(half_tile, 2)
        my_half = pl.ds(pl.multiple_of(core * 256, 256), 256)
        kern_hi[my_half, :] = half_hi
        kern_lo[my_half, :] = half_lo
        swaps = [send(ref.at[my_half, :], ref.at[my_half, :], core_send.at[n], core_recv.at[n], sibling)
                 for n, ref in enumerate((kern_hi, kern_lo))]

        ones = jnp.ones((8, 512), F32)
        deg_row[core, y] = dot(ones, half_tile, ((1,), (1,)), HIGH)
        deg_col[core, x] = dot(ones[:, :256], half_tile, ((1,), (0,)), HIGH)
        copies = []
        for c in (0, 1):
            for k in range(4):
                if c == 0 and k == 0:
                    continue
                c_to = lax.rem(core + c, 2)
                view = deg_row.at[core, y]
                copies.append(send(view, view, deg_send.at[0, c, k], deg_recv.at[0, c, k], along_y(k, c_to)))
                view = deg_col.at[core, x]
                copies.append(send(view, view, deg_send.at[1, c, k], deg_recv.at[1, c, k], along_x(k, c_to)))
        for copy in swaps:
            copy.wait()
        tile_hi, tile_lo = kern_hi[...], kern_lo[...]
        for copy in copies:
            copy.wait()
        row_sums = jnp.concatenate([four(deg_row.at[0]), four(deg_row.at[1])], axis=1)[0:1]
        scale_row = 1.0 / jnp.sqrt(row_sums)
        scale_col = 1.0 / jnp.sqrt((four(deg_col.at[0]) + four(deg_col.at[1]))[0:1])
        wide[...] = jnp.zeros_like(wide)

        def gram_of(block):
            wide[0:32, :] = block
            return dot(block, wide[...], ((1,), (1,)), HIGH)

        for k in range(4):
            @pl.when(row != 4 * y + k)
            def _():
                remote(start_ref, start.at[k], st_send.at[4], st_recv.at[k], sibling).wait_recv()
        mine = [start[k] for k in range(4)]
        basis = jnp.concatenate(mine, axis=1)
        inverse = None
        gram_copies = None
        for step in range(6):
            over_y = step % 2 == 0
            at = y if over_y else x
            scaled = parts(basis * (scale_col if over_y else scale_row), 3)
            dims = ((1,), (1,)) if over_y else ((1,), (0,))
            high = dot(jnp.concatenate(scaled, axis=0), tile_hi, dims)
            low = dot(jnp.concatenate(scaled[:2], axis=0), tile_lo, dims)
            product = high[:32] + ((high[32:64] + low[:32]) + (high[64:] + low[32:]))
            income[step, at] = product * (scale_row if over_y else scale_col)
            copies = []
            for k in (1, 2, 3):
                view = income.at[step, at]
                copies.append(send(view, view, step_send.at[step, k], step_recv.at[step, k],
                                   along_y(k) if over_y else along_x(k)))
            if step in (2, 4):
                n = step // 2 - 1
                grams[n, y] = gram_of(basis)
                gram_copies = [send(grams.at[n, y], grams.at[n, y], gram_send.at[n, k],
                                    gram_recv.at[n, k], along_y(k)) for k in (1, 2, 3)]
            if step in (3, 5):
                for copy in gram_copies:
                    copy.wait()
                inverse = inverse_factor(four(grams.at[step // 2 - 1]))
            for copy in copies:
                copy.wait()
            basis = four(income.at[step])
            if step in (3, 5):
                basis = dot(inverse, basis, ((1,), (0,)), HIGH)

        last[...] = basis
        last_grams[y] = gram_of(basis)
        owner = lax.div(y, 2) == lax.rem(group, 2)
        waits = []
        for k in range(4):
            for i in range(4):
                z_to = group * 4 + lax.rem(1 + i, 4)
                target = device(x, lax.rem(y + k, 4), z_to, core)
                if k or i:
                    waits.append(send(last_grams.at[y], last_grams.at[y], fin_send.at[k, i],
                                      fin_recv.at[y], target))

        def row_copy(k, i):
            lane = pl.multiple_of((i * 2 + core) * 128, 128)
            return remote(last.at[:, pl.ds(lane, 128)], last_rows, row_send.at[k, i], row_recv.at[0],
                          device(x, lax.rem(y + k, 4), z_hi * 8 + 2 * y + i, core))

        for k in range(4):
            for i in range(2):
                to_self = (k == 0) & (z_lo == 2 * y + i)

                @pl.when(owner & jnp.logical_not(to_self))
                def _():
                    row_copy(k, i).start()

                if k == 0:
                    @pl.when(owner & to_self)
                    def _():
                        lane = pl.multiple_of((i * 2 + core) * 128, 128)
                        last_rows[...] = last[:, pl.ds(lane, 128)]
        for copy in waits:
            copy.wait_send()
        for k in range(4):
            for i in range(2):
                to_self = (k == 0) & (z_lo == 2 * y + i)

                @pl.when(owner & jnp.logical_not(to_self))
                def _():
                    row_copy(k, i).wait_send()

    for q in range(4):
        @pl.when(jnp.logical_not(iterates & (y == q)))
        def _():
            remote(last_grams.at[q], last_grams.at[q], fin_send.at[0, 0], fin_recv.at[q], sibling).wait_recv()
    inverse = inverse_factor(four(last_grams))

    @pl.when(jnp.logical_not(iterates & (y == lax.div(z_lo, 2))))
    def _():
        remote(last_rows, last_rows, row_send.at[0, 0], row_recv.at[0], sibling).wait_recv()

    out_ref[...] = dot(inverse, last_rows[...], ((1,), (0,)), HIGH) * math.sqrt(SNAPS)

    for n, t in enumerate((2, 3, 10, 11)):
        @pl.when(giver & (row != t))
        def _():
            basis_copy(n, t).wait_send()
    for n, p in enumerate(PLANES):
        @pl.when(z != p)
        def _():
            gather(n, p).wait_send()


VMEM = pl.BlockSpec(memory_space=pltpu.VMEM)
DMA = pltpu.SemaphoreType.DMA


def body(snapshots, start_block):
    out = pl.pallas_call(
        kernel,
        out_shape=jax.ShapeDtypeStruct((32, 128), F32),
        in_specs=[VMEM, VMEM],
        out_specs=VMEM,
        scratch_shapes=[
            pltpu.VMEM((2, 4, 8, 16, 128), BF16),
            pltpu.VMEM((2, 4, 8, 4, 16, 128), BF16),
            pltpu.VMEM((2, 4, 8, 4, 16, 128), BF16),
            pltpu.VMEM((2, 4, 4, 16, 512), F32),
            pltpu.VMEM((4, 4, 16, 512), F32),
            pltpu.VMEM((4, 4, 16, 512), F32),
            pltpu.VMEM((16, 16, 512), F32),
            pltpu.VMEM((16, 512), F32),
            pltpu.VMEM((256, 512), F32),
            pltpu.VMEM((4, 32, 128), F32),
            pltpu.VMEM((384, 640), F32),
            pltpu.VMEM((512, 512), BF16),
            pltpu.VMEM((512, 512), BF16),
            pltpu.VMEM((2, 4, 8, 256), F32),
            pltpu.VMEM((2, 4, 8, 512), F32),
            pltpu.VMEM((128, 512), F32),
            pltpu.VMEM((6, 4, 32, 512), F32),
            pltpu.VMEM((2, 4, 32, 128), F32),
            pltpu.VMEM((32, 512), F32),
            pltpu.VMEM((32, 128), F32),
            pltpu.VMEM((4, 32, 128), F32),
            DMA((2, 32)), DMA((2, 32)), DMA((2, 2, 4)), DMA((2, 2, 4)), DMA((2, 2, 4)), DMA((2, 2, 4)),
            DMA((4,)), DMA((4,)), DMA((1,)), DMA((1,)), DMA((5,)), DMA((1,)), DMA((5,)), DMA((4,)),
            DMA((3,)), DMA((3,)), DMA((2,)), DMA((2,)), DMA((2, 2, 4)), DMA((2, 2, 4)),
            DMA((6, 4)), DMA((6, 4)), DMA((2, 4)), DMA((2, 4)), DMA((4, 4)), DMA((4,)),
            DMA((4, 2)), DMA((1,)),
        ],
        compiler_params=pltpu.CompilerParams(
            collective_id=1, has_side_effects=True, vmem_limit_bytes=48 << 20),
        name="subspace",
    )(snapshots, start_block.T)
    return out.T


def solution(mesh):
    placed = (P(("row", "col"), "feat"), P("row", None))
    return jax.shard_map(
        body, mesh=mesh, in_specs=placed, out_specs=P("row", None), check_vma=False
    )
```

```python
import math

import jax
import jax.numpy as jnp
from jax import lax
from jax.experimental import pallas as pl
from jax.experimental.pallas import tpu as pltpu
from jax.sharding import PartitionSpec as P

PTS = 32768
LAGS = 128
SNAPS = 2048
PLANES = (1, 5, 9, 13)
MESH = pl.DeviceIdType.MESH
HIGH = lax.Precision.HIGHEST
F32 = jnp.float32
BF16 = jnp.bfloat16


def device(x, y, z, core):
    return (lax.rem(z, 8) * 2 + core, lax.div(z, 8) * 4 + x, y)


def remote(src, dst, send_sem, recv_sem, target):
    return pltpu.make_async_remote_copy(
        src_ref=src, dst_ref=dst, send_sem=send_sem, recv_sem=recv_sem,
        device_id=target, device_id_type=MESH,
    )


def send(*args):
    copy = remote(*args)
    copy.start()
    return copy


def dot(a, b, dims, precision=None):
    return lax.dot_general(
        a, b, (dims, ((), ())), precision=precision, preferred_element_type=F32
    )


def parts(value, count):
    out = []
    for _ in range(count):
        out.append(value.astype(BF16))
        value = value - out[-1].astype(F32)
    return out


def inverse_factor(gram):
    rows = lax.broadcasted_iota(jnp.int32, (32, 128), 0)
    lanes = lax.broadcasted_iota(jnp.int32, (32, 128), 1)
    work = jnp.where(lanes < 32, gram, jnp.where(lanes - 32 == rows, 1.0, 0.0))
    for k in range(0, 32, 2):
        top, next_top = work[k:k + 1, :], work[k + 1:k + 2, :]
        left, right = work[:, k:k + 1], work[:, k + 1:k + 2]
        scale = 1.0 / top[:, k:k + 1]
        ratio = left * scale
        step = next_top[:, k:k + 1] * scale
        next_top = next_top - step * top
        next_ratio = (right - ratio * top[:, k + 1:k + 2]) / next_top[:, k + 1:k + 2]
        first = jnp.where(rows > k, ratio, 0.0)
        second = jnp.where(rows > k + 1, next_ratio, 0.0)
        work = (work - first * top) - second * next_top
    diagonal = jnp.sum(jnp.where(lanes == rows, work, 0.0), axis=1, keepdims=True)
    return work[:, 32:64] / jnp.sqrt(diagonal)


def four(ref):
    return (ref[0] + ref[1]) + (ref[2] + ref[3])


def kernel(
    x_ref, start_ref, out_ref,
    zbuf, abuf, bbuf, part, sib, own, rsbuf, total, dist, start,
    ext, kern_hi, kern_lo, deg_row, deg_col, wide, income, grams, last, last_rows, last_grams,
    local_sem, z_send, z_recv, plane_send, plane_recv, gather_send, gather_recv,
    sib_send, sib_recv, rs_send, rs_recv, ag_send, ag_recv, st_send, st_recv,
    halo_send, halo_recv, core_send, core_recv, deg_send, deg_recv,
    step_send, step_recv, gram_send, gram_recv, fin_send, fin_recv, row_send, row_recv,
):
    row, col, y = lax.axis_index("row"), lax.axis_index("col"), lax.axis_index("feat")
    x, z_hi = lax.rem(col, 4), lax.div(col, 4)
    core, z_lo = lax.rem(row, 2), lax.div(row, 2)
    z = z_hi * 8 + z_lo
    me = z * 2 + core
    group = lax.div(z, 4)
    iterates = lax.rem(z, 4) == 1

    def line(t):
        return device(x, y, lax.div(t, 2), lax.rem(t, 2))

    def along_x(k, c=core):
        return device(lax.rem(x + k, 4), y, z, c)

    def along_y(k, c=core):
        return device(x, lax.rem(y + k, 4), z, c)

    sibling = device(x, y, z, 1 - core)
    barrier = pltpu.get_barrier_semaphore()
    far_first = sorted(range(1, 32), key=lambda o: -min(o, 32 - o))
    partners = ([line(lax.rem(me + o, 32)) for o in far_first]
                + [along_x(k) for k in (1, 2, 3)] + [along_y(k) for k in (1, 2, 3)])
    for target in partners:
        pl.semaphore_signal(barrier, inc=1, device_id=target, device_id_type=MESH)
    pl.semaphore_wait(barrier, len(partners))

    def columns(t, h):
        return pl.ds(pl.multiple_of(t * 256 + h * 128, 128), 128)

    big, small = lax.div(z_lo, 2), lax.rem(z_lo, 2) * 4 + core * 2 + z_hi
    halves = []
    for h in (0, 1):
        if h:
            for copy in halves[0]:
                copy.wait_send()
        copies = []
        for o in far_first:
            t = lax.rem(me + o, 32)
            copies.append(send(x_ref.at[:, columns(t, h)], zbuf.at[h, big, small],
                               z_send.at[h, o], z_recv.at[h, o], line(t)))
        halves.append(copies)
    here = [pltpu.make_async_copy(x_ref.at[:, columns(me, h)], zbuf.at[h, big, small], local_sem.at[h])
            for h in (0, 1)]
    for copy in here:
        copy.start()

    giver = lax.div(row, 4) == y
    basis_slot = lax.rem(row, 4)

    def basis_copy(n, t):
        return remote(start_ref, start.at[basis_slot], st_send.at[n], st_recv.at[basis_slot],
                      (t, col, y))

    for n, t in enumerate((2, 10)):
        @pl.when(giver & (row != t))
        def _():
            basis_copy(n, t).start()

    @pl.when(giver)
    def _():
        copy = pltpu.make_async_copy(start_ref, start.at[basis_slot], local_sem.at[2])
        copy.start()
        copy.wait()

    first = []
    for h in (0, 1):
        here[h].wait()
        for copy in halves[h]:
            if h:
                copy.wait_send()
            copy.wait_recv()
        pairs = []
        for k in (1, 2, 3):
            pairs.append((
                send(zbuf.at[h, lax.rem(x + k, 4)], abuf.at[h, y, :, x],
                     plane_send.at[h, 0, k], plane_recv.at[h, 0, k], along_x(k)),
                send(zbuf.at[h, lax.rem(y + k, 4)], bbuf.at[h, y, :, x],
                     plane_send.at[h, 1, k], plane_recv.at[h, 1, k], along_y(k))))
        first.append(pairs)
        abuf[h, y, :, x] = zbuf[h, x]
        bbuf[h, y, :, x] = zbuf[h, y]
    gathers = []
    for h in (0, 1):
        group_copies = []
        for copy, _ in first[h]:
            copy.wait()
        for k in (1, 2, 3):
            group_copies.append(send(abuf.at[h, y], abuf.at[h, y],
                                     gather_send.at[h, 0, k], gather_recv.at[h, 0, k], along_y(k)))
        for _, copy in first[h]:
            copy.wait()
        for k in (1, 2, 3):
            group_copies.append(send(bbuf.at[h, :, :, x], bbuf.at[h, :, :, x],
                                     gather_send.at[h, 1, k], gather_recv.at[h, 1, k], along_x(k)))
        gathers.append(group_copies)

    for h in (0, 1):
        for copy in gathers[h]:
            copy.wait()
        b = jnp.concatenate([bbuf[h, q].reshape(512, 128) for q in range(4)], axis=1)
        b_wide = b.astype(F32)
        ones = jnp.ones((16, 512), BF16)
        b_norm = sum(dot(ones, p, ((1,), (1,))) for p in parts(b_wide * b_wide, 2))[0:1]
        for half in (1 - core, core):
            a = jnp.concatenate(
                [abuf[h, q, pl.ds(half * 4, 4)].reshape(256, 128) for q in range(4)], axis=1)
            a_wide = a.astype(F32)
            a_norm = jnp.sum(a_wide * a_wide, axis=1, keepdims=True)
            value = (a_norm + b_norm - 2.0 * dot(a, b, ((1,), (1,)))).reshape(4, 4, 16, 512)
            if h == 1:
                value = value + part[half]
            part[half] = value
            if h == 1 and half is not core:
                core_sums = [send(part.at[half, n], sib.at[n], sib_send.at[n], sib_recv.at[n], sibling)
                             for n in range(4)]

    for n in range(4):
        core_sums[n].wait()
        own[pl.ds(n * 4, 4)] = part[core, n] + sib[n]
    for o in sorted(range(1, 16), key=lambda o: -min(o, 16 - o)):
        q = lax.rem(z + o, 16)
        send(own.at[q], rsbuf.at[z], rs_send.at[0], rs_recv.at[0], device(x, y, q, core))
    rsbuf[z] = own[z]
    remote(rsbuf.at[pl.ds(0, 15)], rsbuf.at[pl.ds(0, 15)], rs_send.at[0], rs_recv.at[0], sibling).wait()
    chunk = rsbuf[0]
    for q in range(1, 16):
        chunk = chunk + rsbuf[q]
    total[...] = chunk

    my_rows = pl.ds(pl.multiple_of(z * 16, 16), 16)

    def gather(n, p):
        return remote(total, dist.at[my_rows, :], ag_send.at[n], ag_recv.at[0], device(x, y, p, core))

    for n, p in enumerate(PLANES):
        @pl.when(z != p)
        def _():
            gather(n, p).start()

    @pl.when(iterates)
    def _():
        dist[my_rows, :] = total[...]
        remote(dist.at[pl.ds(0, 240), :], dist.at[pl.ds(0, 240), :],
               ag_send.at[4], ag_recv.at[0], sibling).wait_recv()

        x_next, y_next = lax.rem(x + core, 4), lax.rem(y + 1, 4)
        halo = [
            send(dist.at[pl.ds(128, 128), :], ext.at[pl.ds(0, 128), pl.ds(128, 512)],
                 halo_send.at[0], halo_recv.at[0], device(x_next, y, z, 1 - core)),
            send(dist.at[:, pl.ds(384, 128)], ext.at[pl.ds(128, 256), pl.ds(0, 128)],
                 halo_send.at[1], halo_recv.at[1], device(x, y_next, z, core)),
            send(dist.at[pl.ds(128, 128), pl.ds(384, 128)], ext.at[pl.ds(0, 128), pl.ds(0, 128)],
                 halo_send.at[2], halo_recv.at[2], device(x_next, y_next, z, 1 - core)),
        ]
        ext[128:384, 128:640] = dist[...]
        for copy in halo:
            copy.wait()
        rows = lax.broadcasted_iota(jnp.int32, (384, 640), 0)
        lanes = lax.broadcasted_iota(jnp.int32, (384, 640), 1)
        first_row = jnp.where(2 * x + core == 0, 128, 0)
        first_lane = jnp.where(y == 0, 128, 0)
        run = jnp.where((rows >= first_row) & (lanes >= first_lane), ext[...], 0.0)
        stride = LAGS // 2
        while stride >= 1:
            turned = pltpu.roll(run, stride, 1)
            if stride >= 8:
                run = run[stride:] + turned[:-stride]
            else:
                run = run + pltpu.roll(turned, stride, 0)
            stride //= 2
        lagged = run[8:, 128:]
        i = lax.broadcasted_iota(jnp.int32, (256, 512), 0) + (x * 512 + core * 256)
        j = lax.broadcasted_iota(jnp.int32, (256, 512), 1) + y * 512
        counts = (jnp.minimum(jnp.minimum(i, j), LAGS - 1) + 1).astype(F32)
        half_tile = jnp.exp(-(lagged / (counts * (PTS * 0.25))))
        half_hi, half_lo = parts(half_tile, 2)
        my_half = pl.ds(pl.multiple_of(core * 256, 256), 256)
        kern_hi[my_half, :] = half_hi
        kern_lo[my_half, :] = half_lo
        swaps = [remote(ref.at[my_half, :], ref.at[my_half, :], core_send.at[n], core_recv.at[n], sibling)
                 for n, ref in enumerate((kern_hi, kern_lo))]

        @pl.when(core == 1)
        def _():
            for copy in swaps:
                copy.start()

        ones = jnp.ones((8, 512), F32)
        deg_row[core, y] = dot(ones, half_tile, ((1,), (1,)), HIGH)
        deg_col[core, x] = dot(ones[:, :256], half_tile, ((1,), (0,)), HIGH)

        def degree_copies(k):
            row_view, col_view = deg_row.at[core, y], deg_col.at[core, x]
            return (remote(row_view, row_view, deg_send.at[0, k], deg_recv.at[0, core, k], along_y(k, 0)),
                    remote(col_view, col_view, deg_send.at[1, k], deg_recv.at[1, core, k], along_x(k, 0)))

        @pl.when(core == 1)
        def _():
            for k in range(4):
                for copy in degree_copies(k):
                    copy.start()
            for copy in swaps:
                copy.wait_send()
            for k in range(4):
                for copy in degree_copies(k):
                    copy.wait_send()

    @pl.when(iterates & (core == 0))
    def _():
        def degree_copy(n, c, k):
            ref = (deg_row, deg_col)[n].at[c, 0]
            return remote(ref, ref, deg_send.at[n, k], deg_recv.at[n, c, k], sibling)

        for k in (1, 2, 3):
            for n, ref, target in ((0, deg_row.at[0, y], along_y(k)), (1, deg_col.at[0, x], along_x(k))):
                remote(ref, ref, deg_send.at[n, k], deg_recv.at[n, 0, k], target).start()
        wide[...] = jnp.zeros_like(wide)

        def gram_of(block):
            wide[0:32, :] = block
            return dot(block, wide[...], ((1,), (1,)), HIGH)

        for k in range(4):
            @pl.when(row != 4 * y + k)
            def _():
                remote(start_ref, start.at[k], st_send.at[2], st_recv.at[k], sibling).wait_recv()
        mine = [start[k].T for k in range(4)]
        basis = jnp.concatenate(mine, axis=1)
        other_half = pl.ds(256, 256)
        for n, ref in enumerate((kern_hi, kern_lo)):
            remote(ref.at[other_half, :], ref.at[other_half, :], core_send.at[n], core_recv.at[n], sibling).wait_recv()
        tile_hi, tile_lo = kern_hi[...], kern_lo[...]
        for n in (0, 1):
            for k in (1, 2, 3):
                degree_copy(n, 0, k).wait()
            for k in range(4):
                degree_copy(n, 1, k).wait_recv()
        row_sums = jnp.concatenate([four(deg_row.at[0]), four(deg_row.at[1])], axis=1)[0:1]
        scale_row = 1.0 / jnp.sqrt(row_sums)
        scale_col = 1.0 / jnp.sqrt((four(deg_col.at[0]) + four(deg_col.at[1]))[0:1])
        inverse = None
        gram_copies = None
        for step in range(6):
            over_y = step % 2 == 0
            at = y if over_y else x
            scaled = parts(basis * (scale_col if over_y else scale_row), 3)
            dims = ((1,), (1,)) if over_y else ((1,), (0,))
            high = dot(jnp.concatenate(scaled, axis=0), tile_hi, dims)
            low = dot(jnp.concatenate(scaled[:2], axis=0), tile_lo, dims)
            product = high[:32] + ((high[32:64] + low[:32]) + (high[64:] + low[32:]))
            income[step, at] = product * (scale_row if over_y else scale_col)
            copies = []
            for k in (1, 2, 3):
                view = income.at[step, at]
                copies.append(send(view, view, step_send.at[step, k], step_recv.at[step, k],
                                   along_y(k) if over_y else along_x(k)))
            if step in (2, 4):
                n = step // 2 - 1
                grams[n, y] = gram_of(basis)
                gram_copies = [send(grams.at[n, y], grams.at[n, y], gram_send.at[n, k],
                                    gram_recv.at[n, k], along_y(k)) for k in (1, 2, 3)]
            if step in (3, 5):
                for copy in gram_copies:
                    copy.wait()
                inverse = inverse_factor(four(grams.at[step // 2 - 1]))
            for copy in copies:
                copy.wait()
            basis = four(income.at[step])
            if step in (3, 5):
                basis = dot(inverse, basis, ((1,), (0,)), HIGH)

        last[...] = basis
        owner = lax.div(y, 2) == lax.rem(group, 2)

        def row_copy(k, i, c):
            return remote(last.at[:, pl.ds((i * 2 + c) * 128, 128)], last_rows, row_send.at[k, i, c],
                          row_recv.at[0], device(x, lax.rem(y + k, 4), z_hi * 8 + 2 * y + i, c))

        def each_row_copy(do):
            for k in range(4):
                for i in (0, 1):
                    for c in (0, 1):
                        if k or c:
                            do(row_copy(k, i, c))
                        else:
                            @pl.when(z_lo != 2 * y + i)
                            def _():
                                do(row_copy(k, i, c))

        @pl.when(owner)
        def _():
            each_row_copy(lambda copy: copy.start())
            for i in (0, 1):
                @pl.when(z_lo == 2 * y + i)
                def _():
                    last_rows[...] = last[:, i * 256:i * 256 + 128]

        gram = gram_of(basis)
        last_grams[y] = jnp.concatenate([gram[8 * n:8 * n + 8, :32] for n in range(4)], axis=1)
        waits = []
        for k in range(4):
            for i in range(4):
                for c in (0, 1):
                    if k or i or c:
                        target = device(x, lax.rem(y + k, 4), group * 4 + lax.rem(1 + i, 4), c)
                        waits.append(send(last_grams.at[y], last_grams.at[y], fin_send.at[k, i, c],
                                          fin_recv.at[y], target))

        for copy in waits:
            copy.wait_send()

        @pl.when(owner)
        def _():
            each_row_copy(lambda copy: copy.wait_send())

    for q in range(4):
        @pl.when(jnp.logical_not(iterates & (core == 0) & (y == q)))
        def _():
            remote(last_grams.at[q], last_grams.at[q], fin_send.at[0, 0, 0], fin_recv.at[q], sibling).wait_recv()
    packed = four(last_grams)
    packed = jnp.concatenate([packed[:, 32 * n:32 * n + 32] for n in range(4)], axis=0)
    inverse = inverse_factor(jnp.concatenate([packed, jnp.zeros((32, 96), F32)], axis=1))

    @pl.when(jnp.logical_not(iterates & (core == 0) & (y == lax.div(z_lo, 2))))
    def _():
        remote(last_rows, last_rows, row_send.at[0, 0, 0], row_recv.at[0], sibling).wait_recv()

    out_ref[...] = dot(inverse, last_rows[...], ((1,), (0,)), HIGH) * math.sqrt(SNAPS)

    for n, t in enumerate((2, 10)):
        @pl.when(giver & (row != t))
        def _():
            basis_copy(n, t).wait_send()
    for n, p in enumerate(PLANES):
        @pl.when(z != p)
        def _():
            gather(n, p).wait_send()


VMEM = pl.BlockSpec(memory_space=pltpu.VMEM)
ANY = pl.BlockSpec(memory_space=pl.ANY)
DMA = pltpu.SemaphoreType.DMA


def body(snapshots, start_block):
    out = pl.pallas_call(
        kernel,
        out_shape=jax.ShapeDtypeStruct((32, 128), F32),
        in_specs=[ANY, ANY],
        out_specs=VMEM,
        scratch_shapes=[
            pltpu.VMEM((2, 4, 8, 16, 128), BF16),
            pltpu.VMEM((2, 4, 8, 4, 16, 128), BF16),
            pltpu.VMEM((2, 4, 8, 4, 16, 128), BF16),
            pltpu.VMEM((2, 4, 4, 16, 512), F32),
            pltpu.VMEM((4, 4, 16, 512), F32),
            pltpu.VMEM((16, 16, 512), F32),
            pltpu.VMEM((16, 16, 512), F32),
            pltpu.VMEM((16, 512), F32),
            pltpu.VMEM((256, 512), F32),
            pltpu.VMEM((4, 128, 32), F32),
            pltpu.VMEM((384, 640), F32),
            pltpu.VMEM((512, 512), BF16),
            pltpu.VMEM((512, 512), BF16),
            pltpu.VMEM((2, 4, 8, 256), F32),
            pltpu.VMEM((2, 4, 8, 512), F32),
            pltpu.VMEM((128, 512), F32),
            pltpu.VMEM((6, 4, 32, 512), F32),
            pltpu.VMEM((2, 4, 32, 128), F32),
            pltpu.VMEM((32, 512), F32),
            pltpu.VMEM((32, 128), F32),
            pltpu.VMEM((4, 8, 128), F32),
            DMA((3,)), DMA((2, 32)), DMA((2, 32)), DMA((2, 2, 4)), DMA((2, 2, 4)), DMA((2, 2, 4)), DMA((2, 2, 4)),
            DMA((4,)), DMA((4,)), DMA((1,)), DMA((1,)), DMA((5,)), DMA((1,)), DMA((3,)), DMA((4,)),
            DMA((3,)), DMA((3,)), DMA((2,)), DMA((2,)), DMA((2, 4)), DMA((2, 2, 4)),
            DMA((6, 4)), DMA((6, 4)), DMA((2, 4)), DMA((2, 4)), DMA((4, 4, 2)), DMA((4,)),
            DMA((4, 2, 2)), DMA((1,)),
        ],
        compiler_params=pltpu.CompilerParams(
            collective_id=1, has_side_effects=True, vmem_limit_bytes=48 << 20),
        name="subspace",
    )(snapshots, start_block)
    return out.T


def solution(mesh):
    placed = (P(("row", "col"), "feat"), P("row", None))
    return jax.shard_map(
        body, mesh=mesh, in_specs=placed, out_specs=P("row", None), check_vma=False
    )
```

```python
import math

import jax
import jax.numpy as jnp
from jax import lax
from jax.experimental import pallas as pl
from jax.experimental.pallas import tpu as pltpu
from jax.sharding import PartitionSpec as P

PTS = 32768
LAGS = 128
SNAPS = 2048
PLANES = (1, 5, 9, 13)
MESH = pl.DeviceIdType.MESH
HIGH = lax.Precision.HIGHEST
F32 = jnp.float32
BF16 = jnp.bfloat16


def device(x, y, z, core):
    return (lax.rem(z, 8) * 2 + core, lax.div(z, 8) * 4 + x, y)


def remote(src, dst, send_sem, recv_sem, target):
    return pltpu.make_async_remote_copy(
        src_ref=src, dst_ref=dst, send_sem=send_sem, recv_sem=recv_sem,
        device_id=target, device_id_type=MESH,
    )


def send(*args):
    copy = remote(*args)
    copy.start()
    return copy


def send_pieces(count, src, dst, send_sem, recv_sem, target):
    rows = src.shape[0] // count
    for n in range(count):
        piece = pl.ds(n * rows, rows)
        send(src.at[piece], dst.at[piece], send_sem, recv_sem, target)
    return remote(src, dst, send_sem, recv_sem, target)


def dot(a, b, dims, precision=None):
    return lax.dot_general(
        a, b, (dims, ((), ())), precision=precision, preferred_element_type=F32
    )


def parts(value, count):
    out = []
    for _ in range(count):
        out.append(value.astype(BF16))
        value = value - out[-1].astype(F32)
    return out


def inverse_factor(gram):
    rows = lax.broadcasted_iota(jnp.int32, (32, 128), 0)
    lanes = lax.broadcasted_iota(jnp.int32, (32, 128), 1)
    work = jnp.where(lanes < 32, gram, jnp.where(lanes - 32 == rows, 1.0, 0.0))
    for k in range(0, 32, 2):
        top, next_top = work[k:k + 1, :], work[k + 1:k + 2, :]
        left, right = work[:, k:k + 1], work[:, k + 1:k + 2]
        scale = 1.0 / top[:, k:k + 1]
        ratio = left * scale
        step = next_top[:, k:k + 1] * scale
        next_top = next_top - step * top
        next_ratio = (right - ratio * top[:, k + 1:k + 2]) / next_top[:, k + 1:k + 2]
        first = jnp.where(rows > k, ratio, 0.0)
        second = jnp.where(rows > k + 1, next_ratio, 0.0)
        work = (work - first * top) - second * next_top
    diagonal = jnp.sum(jnp.where(lanes == rows, work, 0.0), axis=1, keepdims=True)
    return work[:, 32:64] / jnp.sqrt(diagonal)


def four(ref):
    return (ref[0] + ref[1]) + (ref[2] + ref[3])


def kernel(
    x_ref, start_ref, out_ref,
    zbuf, abuf, bbuf, part, sib, own, rs_up, rs_down, rs_near, rs_sum, rs_last, total, start,
    ext, kern_hi, kern_lo, deg_row, deg_col, wide, income, grams, last, last_rows, last_grams,
    local_sem, z_send, z_recv, plane_send, plane_recv, gather_send, gather_recv,
    sib_send, sib_recv, rs_send, rs_recv, ag_send, ag_recv, st_send, st_recv,
    core_send, core_recv, deg_send, deg_recv,
    step_send, step_recv, gram_send, gram_recv, fin_send, fin_recv, row_send, row_recv,
):
    row, col, y = lax.axis_index("row"), lax.axis_index("col"), lax.axis_index("feat")
    x, z_hi = lax.rem(col, 4), lax.div(col, 4)
    core, z_lo = lax.rem(row, 2), lax.div(row, 2)
    z = z_hi * 8 + z_lo
    me = z * 2 + core
    group = lax.div(z, 4)
    iterates = lax.rem(z, 4) == 1

    def line(t):
        return device(x, y, lax.div(t, 2), lax.rem(t, 2))

    def along_x(k, c=core):
        return device(lax.rem(x + k, 4), y, z, c)

    def along_y(k, c=core):
        return device(x, lax.rem(y + k, 4), z, c)

    sibling = device(x, y, z, 1 - core)
    barrier = pltpu.get_barrier_semaphore()
    far_first = sorted(range(1, 32), key=lambda o: -min(o, 32 - o))
    partners = ([line(lax.rem(me + o, 32)) for o in far_first]
                + [along_x(k) for k in (1, 2, 3)] + [along_y(k) for k in (1, 2, 3)])
    for target in partners:
        pl.semaphore_signal(barrier, inc=1, device_id=target, device_id_type=MESH)
    pl.semaphore_wait(barrier, len(partners))

    def columns(t, h):
        return pl.ds(pl.multiple_of(t * 256 + h * 128, 128), 128)

    big, small = lax.div(z_lo, 2), lax.rem(z_lo, 2) * 4 + core * 2 + z_hi
    halves = []
    for h in (0, 1):
        if h:
            for copy in halves[0]:
                copy.wait_send()
        copies = []
        for o in far_first:
            t = lax.rem(me + o, 32)
            copies.append(send(x_ref.at[:, columns(t, h)], zbuf.at[h, big, small],
                               z_send.at[h, o], z_recv.at[h, o], line(t)))
        halves.append(copies)
    here = [pltpu.make_async_copy(x_ref.at[:, columns(me, h)], zbuf.at[h, big, small], local_sem.at[h])
            for h in (0, 1)]
    for copy in here:
        copy.start()

    giver = lax.div(row, 4) == y
    basis_slot = lax.rem(row, 4)

    def basis_copy(n, t):
        return remote(start_ref, start.at[basis_slot], st_send.at[n], st_recv.at[basis_slot],
                      (t, col, y))

    for n, t in enumerate((2, 10)):
        @pl.when(giver & (row != t))
        def _():
            basis_copy(n, t).start()

    @pl.when(giver)
    def _():
        copy = pltpu.make_async_copy(start_ref, start.at[basis_slot], local_sem.at[2])
        copy.start()
        copy.wait()

    first = []
    for h in (0, 1):
        here[h].wait()
        for copy in halves[h]:
            if h:
                copy.wait_send()
            copy.wait_recv()
        pairs = []
        for k in (1, 2, 3):
            pairs.append((
                send(zbuf.at[h, lax.rem(x + k, 4)], abuf.at[h, y, :, x],
                     plane_send.at[h, 0, k], plane_recv.at[h, 0, k], along_x(k)),
                send(zbuf.at[h, lax.rem(y + k, 4)], bbuf.at[h, y, :, x],
                     plane_send.at[h, 1, k], plane_recv.at[h, 1, k], along_y(k))))
        first.append(pairs)
        abuf[h, y, :, x] = zbuf[h, x]
        bbuf[h, y, :, x] = zbuf[h, y]
    gathers = []
    for h in (0, 1):
        group_copies = []
        for copy, _ in first[h]:
            copy.wait()
        for k in (1, 2, 3):
            group_copies.append(send_pieces(4, abuf.at[h, y], abuf.at[h, y],
                                     gather_send.at[h, 0, k], gather_recv.at[h, 0, k], along_y(k)))
        for _, copy in first[h]:
            copy.wait()
        for k in (1, 2, 3):
            group_copies.append(send_pieces(4, bbuf.at[h, :, :, x], bbuf.at[h, :, :, x],
                                     gather_send.at[h, 1, k], gather_recv.at[h, 1, k], along_x(k)))
        gathers.append(group_copies)

    for h in (0, 1):
        for copy in gathers[h]:
            copy.wait()
        b = jnp.concatenate([bbuf[h, q].reshape(512, 128) for q in range(4)], axis=1)
        b_wide = b.astype(F32)
        ones = jnp.ones((16, 512), BF16)
        b_norm = sum(dot(ones, p, ((1,), (1,))) for p in parts(b_wide * b_wide, 2))[0:1]
        for half in (1 - core, core):
            a = jnp.concatenate(
                [abuf[h, q, pl.ds(half * 4, 4)].reshape(256, 128) for q in range(4)], axis=1)
            a_wide = a.astype(F32)
            a_norm = jnp.sum(a_wide * a_wide, axis=1, keepdims=True)
            value = (a_norm + b_norm - 2.0 * dot(a, b, ((1,), (1,)))).reshape(4, 4, 16, 512)
            if h == 1:
                value = value + part[half]
            part[half] = value
            if h == 1 and half is not core:
                core_sums = [send_pieces(2, part.at[half, n], sib.at[n], sib_send.at[n], sib_recv.at[n], sibling)
                             for n in range(4)]

    for n in range(4):
        core_sums[n].wait()
        own[pl.ds(n * 4, 4)] = part[core, n] + sib[n]

    def at_plane(o):
        return device(x, y, lax.rem(z + o + 16, 16), core)

    for d in (8, 7, 6, 5):
        send(own.at[lax.rem(z + d, 16)], rs_up.at[d - 5], rs_send.at[0], rs_recv.at[0], at_plane(d - 4))
        if d < 8:
            send(own.at[lax.rem(z + 16 - d, 16)], rs_down.at[d - 5], rs_send.at[1], rs_recv.at[1], at_plane(4 - d))
    for d in (3, 2, 1):
        send(own.at[lax.rem(z + d, 16)], rs_near.at[d - 1], rs_send.at[2], rs_recv.at[2], at_plane(d))
        send(own.at[lax.rem(z + 16 - d, 16)], rs_near.at[d + 2], rs_send.at[2], rs_recv.at[2], at_plane(-d))
    remote(rs_up, rs_up, rs_send.at[0], rs_recv.at[0], sibling).wait_recv()
    rs_sum[0] = own[lax.rem(z + 4, 16)] + four(rs_up)
    last_up = send(rs_sum.at[0], rs_last.at[0], rs_send.at[3], rs_recv.at[3], at_plane(4))
    remote(rs_down, rs_down, rs_send.at[1], rs_recv.at[1], sibling).wait_recv()
    rs_sum[1] = own[lax.rem(z + 12, 16)] + (rs_down[0] + rs_down[1] + rs_down[2])
    last_down = send(rs_sum.at[1], rs_last.at[1], rs_send.at[4], rs_recv.at[4], at_plane(-4))
    remote(rs_near, rs_near, rs_send.at[2], rs_recv.at[2], sibling).wait()
    near = own[z] + ((rs_near[0] + rs_near[1]) + (rs_near[2] + rs_near[3]) + (rs_near[4] + rs_near[5]))
    last_up.wait()
    last_down.wait()
    total[...] = near + (rs_last[0] + rs_last[1])
    remote(rs_up, rs_up, rs_send.at[0], rs_recv.at[0], sibling).wait_send()
    remote(rs_down, rs_down, rs_send.at[1], rs_recv.at[1], sibling).wait_send()

    x_next, y_next = lax.rem(x + core, 4), lax.rem(y + 1, 4)

    def strip(first):
        return pl.ds(pl.multiple_of(first, 16), 16)

    def gather(n, p, part_at):
        below, right = part_at
        edge = total.at[:, pl.ds(384, 128)] if right else total
        lanes = pl.ds(0, 128) if right else pl.ds(128, 512)
        rows = strip(jnp.maximum(z - 8, 0) * 16) if below else strip(128 + z * 16)
        return remote(edge, ext.at[rows, lanes], ag_send.at[n, below, right], ag_recv.at[below, right],
                      device(x_next if below else x, y_next if right else y, p,
                             1 - core if below else core))

    def each_gather(do):
        for n, p in enumerate(PLANES):
            @pl.when(z != p)
            def _():
                do(gather(n, p, (0, 0)))

            @pl.when(z >= 8)
            def _():
                do(gather(n, p, (1, 0)))
                do(gather(n, p, (1, 1)))

            do(gather(n, p, (0, 1)))

    each_gather(lambda copy: copy.start())

    @pl.when(iterates)
    def _():
        ext[strip(128 + z * 16), 128:640] = total[...]
        for n, (rows, lanes) in enumerate((
                (pl.ds(0, 240), pl.ds(128, 512)), (pl.ds(128, 256), pl.ds(0, 128)),
                (pl.ds(0, 128), pl.ds(128, 512)), (pl.ds(0, 128), pl.ds(0, 128)))):
            view = ext.at[rows, lanes]
            remote(view, view, ag_send.at[0, 0, 0], ag_recv.at[n // 2, n % 2], sibling).wait_recv()
        rows = lax.broadcasted_iota(jnp.int32, (384, 640), 0)
        lanes = lax.broadcasted_iota(jnp.int32, (384, 640), 1)
        first_row = jnp.where(2 * x + core == 0, 128, 0)
        first_lane = jnp.where(y == 0, 128, 0)
        run = jnp.where((rows >= first_row) & (lanes >= first_lane), ext[...], 0.0)
        stride = LAGS // 2
        while stride >= 1:
            turned = pltpu.roll(run, stride, 1)
            if stride >= 8:
                run = run[stride:] + turned[:-stride]
            else:
                run = run + pltpu.roll(turned, stride, 0)
            stride //= 2
        lagged = run[8:, 128:]
        i = lax.broadcasted_iota(jnp.int32, (256, 512), 0) + (x * 512 + core * 256)
        j = lax.broadcasted_iota(jnp.int32, (256, 512), 1) + y * 512
        counts = (jnp.minimum(jnp.minimum(i, j), LAGS - 1) + 1).astype(F32)
        half_tile = jnp.exp(-(lagged / (counts * (PTS * 0.25))))
        half_hi, half_lo = parts(half_tile, 2)
        my_half = pl.ds(pl.multiple_of(core * 256, 256), 256)
        kern_hi[my_half, :] = half_hi
        kern_lo[my_half, :] = half_lo
        swaps = [remote(ref.at[my_half, :], ref.at[my_half, :], core_send.at[n], core_recv.at[n], sibling)
                 for n, ref in enumerate((kern_hi, kern_lo))]

        @pl.when(core == 1)
        def _():
            for n, ref in enumerate((kern_hi, kern_lo)):
                send_pieces(4, ref.at[my_half, :], ref.at[my_half, :], core_send.at[n], core_recv.at[n], sibling)

        ones = jnp.ones((8, 512), F32)
        deg_row[core, y] = dot(ones, half_tile, ((1,), (1,)), HIGH)
        deg_col[core, x] = dot(ones[:, :256], half_tile, ((1,), (0,)), HIGH)

        def degree_copies(k):
            row_view, col_view = deg_row.at[core, y], deg_col.at[core, x]
            return (remote(row_view, row_view, deg_send.at[0, k], deg_recv.at[0, core, k], along_y(k, 0)),
                    remote(col_view, col_view, deg_send.at[1, k], deg_recv.at[1, core, k], along_x(k, 0)))

        @pl.when(core == 1)
        def _():
            for k in range(4):
                for copy in degree_copies(k):
                    copy.start()
            for copy in swaps:
                copy.wait_send()
            for k in range(4):
                for copy in degree_copies(k):
                    copy.wait_send()

    @pl.when(iterates & (core == 0))
    def _():
        def degree_copy(n, c, k):
            ref = (deg_row, deg_col)[n].at[c, 0]
            return remote(ref, ref, deg_send.at[n, k], deg_recv.at[n, c, k], sibling)

        for k in (1, 2, 3):
            for n, ref, target in ((0, deg_row.at[0, y], along_y(k)), (1, deg_col.at[0, x], along_x(k))):
                remote(ref, ref, deg_send.at[n, k], deg_recv.at[n, 0, k], target).start()
        wide[...] = jnp.zeros_like(wide)

        def gram_of(block):
            wide[0:32, :] = block
            return dot(block, wide[...], ((1,), (1,)), HIGH)

        for k in range(4):
            @pl.when(row != 4 * y + k)
            def _():
                remote(start_ref, start.at[k], st_send.at[2], st_recv.at[k], sibling).wait_recv()
        mine = [start[k].T for k in range(4)]
        basis = jnp.concatenate(mine, axis=1)
        other_half = pl.ds(256, 256)
        for n, ref in enumerate((kern_hi, kern_lo)):
            remote(ref.at[other_half, :], ref.at[other_half, :], core_send.at[n], core_recv.at[n], sibling).wait_recv()
        tile_hi, tile_lo = kern_hi[...], kern_lo[...]
        for n in (0, 1):
            for k in (1, 2, 3):
                degree_copy(n, 0, k).wait()
            for k in range(4):
                degree_copy(n, 1, k).wait_recv()
        row_sums = jnp.concatenate([four(deg_row.at[0]), four(deg_row.at[1])], axis=1)[0:1]
        scale_row = 1.0 / jnp.sqrt(row_sums)
        scale_col = 1.0 / jnp.sqrt((four(deg_col.at[0]) + four(deg_col.at[1]))[0:1])
        inverse = None
        gram_copies = None
        for step in range(6):
            over_y = step % 2 == 0
            at = y if over_y else x
            scaled = parts(basis * (scale_col if over_y else scale_row), 3)
            dims = ((1,), (1,)) if over_y else ((1,), (0,))
            high = dot(jnp.concatenate(scaled, axis=0), tile_hi, dims)
            low = dot(jnp.concatenate(scaled[:2], axis=0), tile_lo, dims)
            product = high[:32] + ((high[32:64] + low[:32]) + (high[64:] + low[32:]))
            income[step, at] = product * (scale_row if over_y else scale_col)
            copies = []
            for k in (1, 2, 3):
                view = income.at[step, at]
                copies.append(send_pieces(2, view, view, step_send.at[step, k], step_recv.at[step, k],
                                   along_y(k) if over_y else along_x(k)))
            if step in (2, 4):
                n = step // 2 - 1
                grams[n, y] = gram_of(basis)
                gram_copies = [send(grams.at[n, y], grams.at[n, y], gram_send.at[n, k],
                                    gram_recv.at[n, k], along_y(k)) for k in (1, 2, 3)]
            if step in (3, 5):
                for copy in gram_copies:
                    copy.wait()
                inverse = inverse_factor(four(grams.at[step // 2 - 1]))
            for copy in copies:
                copy.wait()
            basis = four(income.at[step])
            if step in (3, 5):
                basis = dot(inverse, basis, ((1,), (0,)), HIGH)

        owner = lax.div(y, 2) == lax.rem(group, 2)

        def row_copy(k, i, c):
            return remote(last.at[:, pl.ds((i * 2 + c) * 128, 128)], last_rows, row_send.at[k, i, c],
                          row_recv.at[0], device(x, lax.rem(y + k, 4), z_hi * 8 + 2 * y + i, c))

        def each_row_copy(do):
            for k in range(4):
                for i in (0, 1):
                    for c in (0, 1):
                        if k or c:
                            do(row_copy(k, i, c))
                        else:
                            @pl.when(z_lo != 2 * y + i)
                            def _():
                                do(row_copy(k, i, c))

        gram = gram_of(basis)
        last_grams[y] = jnp.concatenate([gram[8 * n:8 * n + 8, :32] for n in range(4)], axis=1)
        waits = []
        for k in range(4):
            for i in range(4):
                for c in (0, 1):
                    if k or i or c:
                        target = device(x, lax.rem(y + k, 4), group * 4 + lax.rem(1 + i, 4), c)
                        waits.append(send(last_grams.at[y], last_grams.at[y], fin_send.at[k, i, c],
                                          fin_recv.at[y], target))

        last[...] = basis

        @pl.when(owner)
        def _():
            each_row_copy(lambda copy: copy.start())
            for i in (0, 1):
                @pl.when(z_lo == 2 * y + i)
                def _():
                    last_rows[...] = last[:, i * 256:i * 256 + 128]

        for copy in waits:
            copy.wait_send()

        @pl.when(owner)
        def _():
            each_row_copy(lambda copy: copy.wait_send())

    for q in range(4):
        @pl.when(jnp.logical_not(iterates & (core == 0) & (y == q)))
        def _():
            remote(last_grams.at[q], last_grams.at[q], fin_send.at[0, 0, 0], fin_recv.at[q], sibling).wait_recv()
    packed = four(last_grams)
    packed = jnp.concatenate([packed[:, 32 * n:32 * n + 32] for n in range(4)], axis=0)
    inverse = inverse_factor(jnp.concatenate([packed, jnp.zeros((32, 96), F32)], axis=1))

    @pl.when(jnp.logical_not(iterates & (core == 0) & (y == lax.div(z_lo, 2))))
    def _():
        remote(last_rows, last_rows, row_send.at[0, 0, 0], row_recv.at[0], sibling).wait_recv()

    out_ref[...] = dot(inverse, last_rows[...], ((1,), (0,)), HIGH) * math.sqrt(SNAPS)

    for n, t in enumerate((2, 10)):
        @pl.when(giver & (row != t))
        def _():
            basis_copy(n, t).wait_send()
    each_gather(lambda copy: copy.wait_send())


VMEM = pl.BlockSpec(memory_space=pltpu.VMEM)
ANY = pl.BlockSpec(memory_space=pl.ANY)
DMA = pltpu.SemaphoreType.DMA


def body(snapshots, start_block):
    out = pl.pallas_call(
        kernel,
        out_shape=jax.ShapeDtypeStruct((32, 128), F32),
        in_specs=[ANY, ANY],
        out_specs=VMEM,
        scratch_shapes=[
            pltpu.VMEM((2, 4, 8, 16, 128), BF16),
            pltpu.VMEM((2, 4, 8, 4, 16, 128), BF16),
            pltpu.VMEM((2, 4, 8, 4, 16, 128), BF16),
            pltpu.VMEM((2, 4, 4, 16, 512), F32),
            pltpu.VMEM((4, 4, 16, 512), F32),
            pltpu.VMEM((16, 16, 512), F32),
            pltpu.VMEM((4, 16, 512), F32),
            pltpu.VMEM((3, 16, 512), F32),
            pltpu.VMEM((6, 16, 512), F32),
            pltpu.VMEM((2, 16, 512), F32),
            pltpu.VMEM((2, 16, 512), F32),
            pltpu.VMEM((16, 512), F32),
            pltpu.VMEM((4, 128, 32), F32),
            pltpu.VMEM((384, 640), F32),
            pltpu.VMEM((512, 512), BF16),
            pltpu.VMEM((512, 512), BF16),
            pltpu.VMEM((2, 4, 8, 256), F32),
            pltpu.VMEM((2, 4, 8, 512), F32),
            pltpu.VMEM((128, 512), F32),
            pltpu.VMEM((6, 4, 32, 512), F32),
            pltpu.VMEM((2, 4, 32, 128), F32),
            pltpu.VMEM((32, 512), F32),
            pltpu.VMEM((32, 128), F32),
            pltpu.VMEM((4, 8, 128), F32),
            DMA((3,)), DMA((2, 32)), DMA((2, 32)), DMA((2, 2, 4)), DMA((2, 2, 4)), DMA((2, 2, 4)), DMA((2, 2, 4)),
            DMA((4,)), DMA((4,)), DMA((5,)), DMA((5,)), DMA((4, 2, 2)), DMA((2, 2)), DMA((3,)), DMA((4,)),
            DMA((2,)), DMA((2,)), DMA((2, 4)), DMA((2, 2, 4)),
            DMA((6, 4)), DMA((6, 4)), DMA((2, 4)), DMA((2, 4)), DMA((4, 4, 2)), DMA((4,)),
            DMA((4, 2, 2)), DMA((1,)),
        ],
        compiler_params=pltpu.CompilerParams(
            collective_id=1, has_side_effects=True, vmem_limit_bytes=48 << 20),
        name="subspace",
    )(snapshots, start_block)
    return out.T


def solution(mesh):
    placed = (P(("row", "col"), "feat"), P("row", None))
    return jax.shard_map(
        body, mesh=mesh, in_specs=placed, out_specs=P("row", None), check_vma=False
    )
```

```python
import math

import jax
import jax.numpy as jnp
from jax import lax
from jax.experimental import pallas as pl
from jax.experimental.pallas import tpu as pltpu
from jax.sharding import PartitionSpec as P

PTS = 32768
LAGS = 128
SNAPS = 2048
PLANES = (1, 5, 9, 13)
MESH = pl.DeviceIdType.MESH
HIGH = lax.Precision.HIGHEST
F32 = jnp.float32
BF16 = jnp.bfloat16


def device(x, y, z, core):
    return (lax.rem(z, 8) * 2 + core, lax.div(z, 8) * 4 + x, y)


def remote(src, dst, send_sem, recv_sem, target):
    return pltpu.make_async_remote_copy(
        src_ref=src, dst_ref=dst, send_sem=send_sem, recv_sem=recv_sem,
        device_id=target, device_id_type=MESH,
    )


def send(*args):
    copy = remote(*args)
    copy.start()
    return copy


def send_pieces(count, src, dst, send_sem, recv_sem, target):
    rows = src.shape[0] // count
    for n in range(count):
        piece = pl.ds(n * rows, rows)
        send(src.at[piece], dst.at[piece], send_sem, recv_sem, target)
    return remote(src, dst, send_sem, recv_sem, target)


def dot(a, b, dims, precision=None):
    return lax.dot_general(
        a, b, (dims, ((), ())), precision=precision, preferred_element_type=F32
    )


def parts(value, count):
    out = []
    for _ in range(count):
        out.append(value.astype(BF16))
        value = value - out[-1].astype(F32)
    return out


def inverse_factor(gram):
    rows = lax.broadcasted_iota(jnp.int32, (32, 128), 0)
    lanes = lax.broadcasted_iota(jnp.int32, (32, 128), 1)
    work = jnp.where(lanes < 32, gram, jnp.where(lanes - 32 == rows, 1.0, 0.0))
    for k in range(0, 32, 2):
        top, next_top = work[k:k + 1, :], work[k + 1:k + 2, :]
        left, right = work[:, k:k + 1], work[:, k + 1:k + 2]
        scale = 1.0 / top[:, k:k + 1]
        ratio = left * scale
        step = next_top[:, k:k + 1] * scale
        next_top = next_top - step * top
        next_ratio = (right - ratio * top[:, k + 1:k + 2]) / next_top[:, k + 1:k + 2]
        first = jnp.where(rows > k, ratio, 0.0)
        second = jnp.where(rows > k + 1, next_ratio, 0.0)
        work = (work - first * top) - second * next_top
    diagonal = jnp.sum(jnp.where(lanes == rows, work, 0.0), axis=1, keepdims=True)
    return work[:, 32:64] / jnp.sqrt(diagonal)


def four(ref):
    return (ref[0] + ref[1]) + (ref[2] + ref[3])


def kernel(
    x_ref, start_ref, out_ref,
    zbuf, abuf, bbuf, part, sib, own, rs_up, rs_down, rs_near, rs_sum, rs_last, total, start,
    ext, kern_hi, kern_lo, deg_row, deg_col, wide, income, grams, last, last_rows, last_grams,
    local_sem, z_send, z_recv, plane_send, plane_recv, gather_send, gather_recv,
    sib_send, sib_recv, rs_send, rs_recv, ag_send, ag_recv, st_send, st_recv,
    halo_send, halo_recv, core_send, core_recv, deg_send, deg_recv,
    step_send, step_recv, gram_send, gram_recv, fin_send, fin_recv, row_send, row_recv,
):
    row, col, y = lax.axis_index("row"), lax.axis_index("col"), lax.axis_index("feat")
    x, z_hi = lax.rem(col, 4), lax.div(col, 4)
    core, z_lo = lax.rem(row, 2), lax.div(row, 2)
    z = z_hi * 8 + z_lo
    me = z * 2 + core
    group = lax.div(z, 4)
    iterates = lax.rem(z, 4) == 1

    def line(t):
        return device(x, y, lax.div(t, 2), lax.rem(t, 2))

    def along_x(k, c=core):
        return device(lax.rem(x + k, 4), y, z, c)

    def along_y(k, c=core):
        return device(x, lax.rem(y + k, 4), z, c)

    sibling = device(x, y, z, 1 - core)
    barrier = pltpu.get_barrier_semaphore()
    far_first = sorted(range(1, 32), key=lambda o: -min(o, 32 - o))
    partners = ([line(lax.rem(me + o, 32)) for o in far_first]
                + [along_x(k) for k in (1, 2, 3)] + [along_y(k) for k in (1, 2, 3)])
    for target in partners:
        pl.semaphore_signal(barrier, inc=1, device_id=target, device_id_type=MESH)
    pl.semaphore_wait(barrier, len(partners))

    def columns(t, h):
        return pl.ds(pl.multiple_of(t * 256 + h * 128, 128), 128)

    big, small = lax.div(z_lo, 2), lax.rem(z_lo, 2) * 4 + core * 2 + z_hi
    halves = []
    for h in (0, 1):
        if h:
            for copy in halves[0]:
                copy.wait_send()
        copies = []
        for o in far_first:
            t = lax.rem(me + o, 32)
            copies.append(send(x_ref.at[:, columns(t, h)], zbuf.at[h, big, small],
                               z_send.at[h, o], z_recv.at[h, o], line(t)))
        halves.append(copies)
    here = [pltpu.make_async_copy(x_ref.at[:, columns(me, h)], zbuf.at[h, big, small], local_sem.at[h])
            for h in (0, 1)]
    for copy in here:
        copy.start()

    giver = lax.div(row, 4) == y
    basis_slot = lax.rem(row, 4)

    def basis_copy(n, t):
        return remote(start_ref, start.at[basis_slot], st_send.at[n], st_recv.at[basis_slot],
                      (t, col, y))

    for n, t in enumerate((2, 10)):
        @pl.when(giver & (row != t))
        def _():
            basis_copy(n, t).start()

    @pl.when(giver)
    def _():
        copy = pltpu.make_async_copy(start_ref, start.at[basis_slot], local_sem.at[2])
        copy.start()
        copy.wait()

    first = []
    for h in (0, 1):
        here[h].wait()
        for copy in halves[h]:
            if h:
                copy.wait_send()
            copy.wait_recv()
        pairs = []
        for k in (1, 2, 3):
            pairs.append((
                send(zbuf.at[h, lax.rem(x + k, 4)], abuf.at[h, y, :, x],
                     plane_send.at[h, 0, k], plane_recv.at[h, 0, k], along_x(k)),
                send(zbuf.at[h, lax.rem(y + k, 4)], bbuf.at[h, y, :, x],
                     plane_send.at[h, 1, k], plane_recv.at[h, 1, k], along_y(k))))
        first.append(pairs)
        abuf[h, y, :, x] = zbuf[h, x]
        bbuf[h, y, :, x] = zbuf[h, y]
    gathers = []
    for h in (0, 1):
        group_copies = []
        for copy, _ in first[h]:
            copy.wait()
        for k in (1, 2, 3):
            group_copies.append(send_pieces(4, abuf.at[h, y], abuf.at[h, y],
                                     gather_send.at[h, 0, k], gather_recv.at[h, 0, k], along_y(k)))
        for _, copy in first[h]:
            copy.wait()
        for k in (1, 2, 3):
            group_copies.append(send_pieces(4, bbuf.at[h, :, :, x], bbuf.at[h, :, :, x],
                                     gather_send.at[h, 1, k], gather_recv.at[h, 1, k], along_x(k)))
        gathers.append(group_copies)

    for h in (0, 1):
        for copy in gathers[h]:
            copy.wait()
        b = jnp.concatenate([bbuf[h, q].reshape(512, 128) for q in range(4)], axis=1)
        b_wide = b.astype(F32)
        ones = jnp.ones((16, 512), BF16)
        b_norm = sum(dot(ones, p, ((1,), (1,))) for p in parts(b_wide * b_wide, 2))[0:1]
        for half in (1 - core, core):
            a = jnp.concatenate(
                [abuf[h, q, pl.ds(half * 4, 4)].reshape(256, 128) for q in range(4)], axis=1)
            a_wide = a.astype(F32)
            a_norm = jnp.sum(a_wide * a_wide, axis=1, keepdims=True)
            value = (a_norm + b_norm - 2.0 * dot(a, b, ((1,), (1,)))).reshape(4, 4, 16, 512)
            if h == 1:
                value = value + part[half]
            part[half] = value
            if h == 1 and half is not core:
                core_sums = [send_pieces(2, part.at[half, n], sib.at[n], sib_send.at[n], sib_recv.at[n], sibling)
                             for n in range(4)]

    for n in range(4):
        core_sums[n].wait()
        own[pl.ds(n * 4, 4)] = part[core, n] + sib[n]

    def at_plane(o):
        return device(x, y, lax.rem(z + o + 16, 16), core)

    for d in (8, 7, 6, 5):
        send(own.at[lax.rem(z + d, 16)], rs_up.at[d - 5], rs_send.at[0], rs_recv.at[0], at_plane(d - 4))
        if d < 8:
            send(own.at[lax.rem(z + 16 - d, 16)], rs_down.at[d - 5], rs_send.at[1], rs_recv.at[1], at_plane(4 - d))
    for d in (3, 2, 1):
        send(own.at[lax.rem(z + d, 16)], rs_near.at[d - 1], rs_send.at[2], rs_recv.at[2], at_plane(d))
        send(own.at[lax.rem(z + 16 - d, 16)], rs_near.at[d + 2], rs_send.at[2], rs_recv.at[2], at_plane(-d))
    remote(rs_up, rs_up, rs_send.at[0], rs_recv.at[0], sibling).wait_recv()
    rs_sum[0] = own[lax.rem(z + 4, 16)] + four(rs_up)
    last_up = send(rs_sum.at[0], rs_last.at[0], rs_send.at[3], rs_recv.at[3], at_plane(4))
    remote(rs_down, rs_down, rs_send.at[1], rs_recv.at[1], sibling).wait_recv()
    rs_sum[1] = own[lax.rem(z + 12, 16)] + (rs_down[0] + rs_down[1] + rs_down[2])
    last_down = send(rs_sum.at[1], rs_last.at[1], rs_send.at[4], rs_recv.at[4], at_plane(-4))
    remote(rs_near, rs_near, rs_send.at[2], rs_recv.at[2], sibling).wait()
    near = own[z] + ((rs_near[0] + rs_near[1]) + (rs_near[2] + rs_near[3]) + (rs_near[4] + rs_near[5]))
    last_up.wait()
    last_down.wait()
    total[...] = near + (rs_last[0] + rs_last[1])
    remote(rs_up, rs_up, rs_send.at[0], rs_recv.at[0], sibling).wait_send()
    remote(rs_down, rs_down, rs_send.at[1], rs_recv.at[1], sibling).wait_send()

    my_rows = pl.ds(pl.multiple_of(128 + z * 16, 16), 16)

    def gather(n, p):
        return remote(total, ext.at[my_rows, pl.ds(128, 512)], ag_send.at[n], ag_recv.at[0],
                      device(x, y, p, core))

    def each_gather(do):
        for n, p in enumerate(PLANES):
            @pl.when(z != p)
            def _():
                do(gather(n, p))

    each_gather(lambda copy: copy.start())

    @pl.when(iterates)
    def _():
        ext[my_rows, 128:640] = total[...]
        view = ext.at[pl.ds(0, 240), pl.ds(128, 512)]
        remote(view, view, ag_send.at[0], ag_recv.at[0], sibling).wait_recv()

        x_next, y_next = lax.rem(x + core, 4), lax.rem(y + 1, 4)
        below, right, both = (
            device(x_next, y, z, 1 - core), device(x, y_next, z, core), device(x_next, y_next, z, 1 - core))
        bottom, inner, edge = pl.ds(256, 128), pl.ds(128, 512), pl.ds(512, 128)
        halo = [
            send_pieces(4, ext.at[bottom, inner], ext.at[pl.ds(0, 128), inner],
                        halo_send.at[0], halo_recv.at[0], below),
            send_pieces(2, ext.at[bottom, edge], ext.at[pl.ds(0, 128), pl.ds(0, 128)],
                        halo_send.at[2], halo_recv.at[2], both),
            send_pieces(4, ext.at[pl.ds(128, 256), edge], ext.at[pl.ds(128, 256), pl.ds(0, 128)],
                        halo_send.at[1], halo_recv.at[1], right),
        ]
        for copy in halo:
            copy.wait()
        rows = lax.broadcasted_iota(jnp.int32, (384, 640), 0)
        lanes = lax.broadcasted_iota(jnp.int32, (384, 640), 1)
        first_row = jnp.where(2 * x + core == 0, 128, 0)
        first_lane = jnp.where(y == 0, 128, 0)
        run = jnp.where((rows >= first_row) & (lanes >= first_lane), ext[...], 0.0)
        stride = LAGS // 2
        while stride >= 1:
            turned = pltpu.roll(run, stride, 1)
            if stride >= 8:
                run = run[stride:] + turned[:-stride]
            else:
                run = run + pltpu.roll(turned, stride, 0)
            stride //= 2
        lagged = run[8:, 128:]
        i = lax.broadcasted_iota(jnp.int32, (256, 512), 0) + (x * 512 + core * 256)
        j = lax.broadcasted_iota(jnp.int32, (256, 512), 1) + y * 512
        counts = (jnp.minimum(jnp.minimum(i, j), LAGS - 1) + 1).astype(F32)
        half_tile = jnp.exp(-(lagged / (counts * (PTS * 0.25))))
        half_hi, half_lo = parts(half_tile, 2)
        my_half = pl.ds(pl.multiple_of(core * 256, 256), 256)
        kern_hi[my_half, :] = half_hi
        kern_lo[my_half, :] = half_lo
        swaps = [remote(ref.at[my_half, :], ref.at[my_half, :], core_send.at[n], core_recv.at[n], sibling)
                 for n, ref in enumerate((kern_hi, kern_lo))]

        @pl.when(core == 1)
        def _():
            for n, ref in enumerate((kern_hi, kern_lo)):
                send_pieces(4, ref.at[my_half, :], ref.at[my_half, :], core_send.at[n], core_recv.at[n], sibling)

        ones = jnp.ones((16, 512), BF16)
        deg_row[core, y] = (dot(ones, half_hi, ((1,), (1,))) + dot(ones, half_lo, ((1,), (1,))))[:8]
        deg_col[core, x] = (dot(ones[:, :256], half_hi, ((1,), (0,)))
                            + dot(ones[:, :256], half_lo, ((1,), (0,))))[:8]

        def degree_copies(k):
            row_view, col_view = deg_row.at[core, y], deg_col.at[core, x]
            return (remote(row_view, row_view, deg_send.at[0, k], deg_recv.at[0, core, k], along_y(k, 0)),
                    remote(col_view, col_view, deg_send.at[1, k], deg_recv.at[1, core, k], along_x(k, 0)))

        @pl.when(core == 1)
        def _():
            for k in range(4):
                for copy in degree_copies(k):
                    copy.start()
            for copy in swaps:
                copy.wait_send()
            for k in range(4):
                for copy in degree_copies(k):
                    copy.wait_send()

    @pl.when(iterates & (core == 0))
    def _():
        def degree_copy(n, c, k):
            ref = (deg_row, deg_col)[n].at[c, 0]
            return remote(ref, ref, deg_send.at[n, k], deg_recv.at[n, c, k], sibling)

        for k in (1, 2, 3):
            for n, ref, target in ((0, deg_row.at[0, y], along_y(k)), (1, deg_col.at[0, x], along_x(k))):
                remote(ref, ref, deg_send.at[n, k], deg_recv.at[n, 0, k], target).start()
        wide[...] = jnp.zeros_like(wide)

        def gram_of(block):
            wide[0:32, :] = block
            return dot(block, wide[...], ((1,), (1,)), HIGH)

        for k in range(4):
            @pl.when(row != 4 * y + k)
            def _():
                remote(start_ref, start.at[k], st_send.at[2], st_recv.at[k], sibling).wait_recv()
        mine = [start[k].T for k in range(4)]
        basis = jnp.concatenate(mine, axis=1)
        other_half = pl.ds(256, 256)
        for n, ref in enumerate((kern_hi, kern_lo)):
            remote(ref.at[other_half, :], ref.at[other_half, :], core_send.at[n], core_recv.at[n], sibling).wait_recv()
        tile_hi, tile_lo = kern_hi[...], kern_lo[...]
        for n in (0, 1):
            for k in (1, 2, 3):
                degree_copy(n, 0, k).wait()
            for k in range(4):
                degree_copy(n, 1, k).wait_recv()
        row_sums = jnp.concatenate([four(deg_row.at[0]), four(deg_row.at[1])], axis=1)[0:1]
        scale_row = 1.0 / jnp.sqrt(row_sums)
        scale_col = 1.0 / jnp.sqrt((four(deg_col.at[0]) + four(deg_col.at[1]))[0:1])
        inverse = None
        gram_copies = None
        for step in range(6):
            over_y = step % 2 == 0
            at = y if over_y else x
            scaled = parts(basis * (scale_col if over_y else scale_row), 3)
            dims = ((1,), (1,)) if over_y else ((1,), (0,))
            high = dot(jnp.concatenate(scaled, axis=0), tile_hi, dims)
            low = dot(jnp.concatenate(scaled[:2], axis=0), tile_lo, dims)
            product = high[:32] + ((high[32:64] + low[:32]) + (high[64:] + low[32:]))
            income[step, at] = product * (scale_row if over_y else scale_col)
            copies = []
            for k in (1, 2, 3):
                view = income.at[step, at]
                copies.append(send_pieces(2, view, view, step_send.at[step, k], step_recv.at[step, k],
                                   along_y(k) if over_y else along_x(k)))
            if step in (2, 4):
                n = step // 2 - 1
                grams[n, y] = gram_of(basis)
                gram_copies = [send(grams.at[n, y], grams.at[n, y], gram_send.at[n, k],
                                    gram_recv.at[n, k], along_y(k)) for k in (1, 2, 3)]
            if step in (3, 5):
                for copy in gram_copies:
                    copy.wait()
                inverse = inverse_factor(four(grams.at[step // 2 - 1]))
            for copy in copies:
                copy.wait()
            basis = four(income.at[step])
            if step in (3, 5):
                basis = dot(inverse, basis, ((1,), (0,)), HIGH)

        owner = lax.div(y, 2) == lax.rem(group, 2)

        def row_copy(k, i, c):
            return remote(last.at[:, pl.ds((i * 2 + c) * 128, 128)], last_rows, row_send.at[k, i, c],
                          row_recv.at[0], device(x, lax.rem(y + k, 4), z_hi * 8 + 2 * y + i, c))

        def each_row_copy(do):
            for k in range(4):
                for i in (0, 1):
                    for c in (0, 1):
                        if k or c:
                            do(row_copy(k, i, c))
                        else:
                            @pl.when(z_lo != 2 * y + i)
                            def _():
                                do(row_copy(k, i, c))

        gram = gram_of(basis)
        last_grams[y] = jnp.concatenate([gram[8 * n:8 * n + 8, :32] for n in range(4)], axis=1)
        waits = []
        for k in range(4):
            for i in range(4):
                for c in (0, 1):
                    if k or i or c:
                        target = device(x, lax.rem(y + k, 4), group * 4 + lax.rem(1 + i, 4), c)
                        waits.append(send(last_grams.at[y], last_grams.at[y], fin_send.at[k, i, c],
                                          fin_recv.at[y], target))

        last[...] = basis

        @pl.when(owner)
        def _():
            each_row_copy(lambda copy: copy.start())
            for i in (0, 1):
                @pl.when(z_lo == 2 * y + i)
                def _():
                    last_rows[...] = last[:, i * 256:i * 256 + 128]

        for copy in waits:
            copy.wait_send()

        @pl.when(owner)
        def _():
            each_row_copy(lambda copy: copy.wait_send())

    for q in range(4):
        @pl.when(jnp.logical_not(iterates & (core == 0) & (y == q)))
        def _():
            remote(last_grams.at[q], last_grams.at[q], fin_send.at[0, 0, 0], fin_recv.at[q], sibling).wait_recv()
    packed = four(last_grams)
    packed = jnp.concatenate([packed[:, 32 * n:32 * n + 32] for n in range(4)], axis=0)
    inverse = inverse_factor(jnp.concatenate([packed, jnp.zeros((32, 96), F32)], axis=1))

    @pl.when(jnp.logical_not(iterates & (core == 0) & (y == lax.div(z_lo, 2))))
    def _():
        remote(last_rows, last_rows, row_send.at[0, 0, 0], row_recv.at[0], sibling).wait_recv()

    out_ref[...] = dot(inverse, last_rows[...], ((1,), (0,)), HIGH) * math.sqrt(SNAPS)

    for n, t in enumerate((2, 10)):
        @pl.when(giver & (row != t))
        def _():
            basis_copy(n, t).wait_send()
    each_gather(lambda copy: copy.wait_send())


VMEM = pl.BlockSpec(memory_space=pltpu.VMEM)
ANY = pl.BlockSpec(memory_space=pl.ANY)
DMA = pltpu.SemaphoreType.DMA


def body(snapshots, start_block):
    out = pl.pallas_call(
        kernel,
        out_shape=jax.ShapeDtypeStruct((32, 128), F32),
        in_specs=[ANY, ANY],
        out_specs=VMEM,
        scratch_shapes=[
            pltpu.VMEM((2, 4, 8, 16, 128), BF16),
            pltpu.VMEM((2, 4, 8, 4, 16, 128), BF16),
            pltpu.VMEM((2, 4, 8, 4, 16, 128), BF16),
            pltpu.VMEM((2, 4, 4, 16, 512), F32),
            pltpu.VMEM((4, 4, 16, 512), F32),
            pltpu.VMEM((16, 16, 512), F32),
            pltpu.VMEM((4, 16, 512), F32),
            pltpu.VMEM((3, 16, 512), F32),
            pltpu.VMEM((6, 16, 512), F32),
            pltpu.VMEM((2, 16, 512), F32),
            pltpu.VMEM((2, 16, 512), F32),
            pltpu.VMEM((16, 512), F32),
            pltpu.VMEM((4, 128, 32), F32),
            pltpu.VMEM((384, 640), F32),
            pltpu.VMEM((512, 512), BF16),
            pltpu.VMEM((512, 512), BF16),
            pltpu.VMEM((2, 4, 8, 256), F32),
            pltpu.VMEM((2, 4, 8, 512), F32),
            pltpu.VMEM((128, 512), F32),
            pltpu.VMEM((6, 4, 32, 512), F32),
            pltpu.VMEM((2, 4, 32, 128), F32),
            pltpu.VMEM((32, 512), F32),
            pltpu.VMEM((32, 128), F32),
            pltpu.VMEM((4, 8, 128), F32),
            DMA((3,)), DMA((2, 32)), DMA((2, 32)), DMA((2, 2, 4)), DMA((2, 2, 4)), DMA((2, 2, 4)), DMA((2, 2, 4)),
            DMA((4,)), DMA((4,)), DMA((5,)), DMA((5,)), DMA((4,)), DMA((1,)), DMA((3,)), DMA((4,)),
            DMA((3,)), DMA((3,)), DMA((2,)), DMA((2,)), DMA((2, 4)), DMA((2, 2, 4)),
            DMA((6, 4)), DMA((6, 4)), DMA((2, 4)), DMA((2, 4)), DMA((4, 4, 2)), DMA((4,)),
            DMA((4, 2, 2)), DMA((1,)),
        ],
        compiler_params=pltpu.CompilerParams(
            collective_id=1, has_side_effects=True, vmem_limit_bytes=48 << 20),
        name="subspace",
    )(snapshots, start_block)
    return out.T


def solution(mesh):
    placed = (P(("row", "col"), "feat"), P("row", None))
    return jax.shard_map(
        body, mesh=mesh, in_specs=placed, out_specs=P("row", None), check_vma=False
    )
```

```python
import math

import jax
import jax.numpy as jnp
from jax import lax
from jax.experimental import pallas as pl
from jax.experimental.pallas import tpu as pltpu
from jax.sharding import PartitionSpec as P

PTS = 32768
LAGS = 128
SNAPS = 2048
PLANES = (1, 5, 9, 13)
MESH = pl.DeviceIdType.MESH
HIGH = lax.Precision.HIGHEST
F32 = jnp.float32
BF16 = jnp.bfloat16


def device(x, y, z, core):
    return (lax.rem(z, 8) * 2 + core, lax.div(z, 8) * 4 + x, y)


def remote(src, dst, send_sem, recv_sem, target):
    return pltpu.make_async_remote_copy(
        src_ref=src, dst_ref=dst, send_sem=send_sem, recv_sem=recv_sem,
        device_id=target, device_id_type=MESH,
    )


def send(*args):
    copy = remote(*args)
    copy.start()
    return copy


def send_pieces(count, src, dst, send_sem, recv_sem, target):
    rows = src.shape[0] // count
    for n in range(count):
        piece = pl.ds(n * rows, rows)
        send(src.at[piece], dst.at[piece], send_sem, recv_sem, target)
    return remote(src, dst, send_sem, recv_sem, target)


def dot(a, b, dims, precision=None):
    return lax.dot_general(
        a, b, (dims, ((), ())), precision=precision, preferred_element_type=F32
    )


def parts(value, count):
    out = []
    for _ in range(count):
        out.append(value.astype(BF16))
        value = value - out[-1].astype(F32)
    return out


def inverse_factor(gram):
    rows = lax.broadcasted_iota(jnp.int32, (32, 128), 0)
    lanes = lax.broadcasted_iota(jnp.int32, (32, 128), 1)
    work = jnp.where(lanes < 32, gram, jnp.where(lanes - 32 == rows, 1.0, 0.0))
    for k in range(0, 32, 2):
        top, next_top = work[k:k + 1, :], work[k + 1:k + 2, :]
        left, right = work[:, k:k + 1], work[:, k + 1:k + 2]
        scale = 1.0 / top[:, k:k + 1]
        ratio = left * scale
        step = next_top[:, k:k + 1] * scale
        next_top = next_top - step * top
        next_ratio = (right - ratio * top[:, k + 1:k + 2]) / next_top[:, k + 1:k + 2]
        first = jnp.where(rows > k, ratio, 0.0)
        second = jnp.where(rows > k + 1, next_ratio, 0.0)
        work = (work - first * top) - second * next_top
    diagonal = jnp.sum(jnp.where(lanes == rows, work, 0.0), axis=1, keepdims=True)
    return work[:, 32:64] / jnp.sqrt(diagonal)


def four(ref):
    return (ref[0] + ref[1]) + (ref[2] + ref[3])


def kernel(
    x_ref, start_ref, out_ref,
    zbuf, abuf, bbuf, part, sib, own, rs_up, rs_down, rs_near, rs_sum, rs_last, total, start,
    ext, kern_hi, kern_lo, deg_row, deg_col, wide, income, grams, last, last_rows, last_grams,
    local_sem, z_send, z_recv, plane_send, plane_recv, gather_send, gather_recv,
    sib_send, sib_recv, rs_send, rs_recv, ag_send, ag_recv, st_send, st_recv,
    halo_send, halo_recv, core_send, core_recv, deg_send, deg_recv,
    step_send, step_recv, gram_send, gram_recv, fin_send, fin_recv, row_send, row_recv,
):
    row, col, y = lax.axis_index("row"), lax.axis_index("col"), lax.axis_index("feat")
    x, z_hi = lax.rem(col, 4), lax.div(col, 4)
    core, z_lo = lax.rem(row, 2), lax.div(row, 2)
    z = z_hi * 8 + z_lo
    me = z * 2 + core
    group = lax.div(z, 4)
    iterates = lax.rem(z, 4) == 1

    def line(t):
        return device(x, y, lax.div(t, 2), lax.rem(t, 2))

    def along_x(k, c=core):
        return device(lax.rem(x + k, 4), y, z, c)

    def along_y(k, c=core):
        return device(x, lax.rem(y + k, 4), z, c)

    sibling = device(x, y, z, 1 - core)
    barrier = pltpu.get_barrier_semaphore()
    far_first = sorted(range(1, 32), key=lambda o: -min(o, 32 - o))
    partners = ([line(lax.rem(me + o, 32)) for o in far_first]
                + [along_x(k) for k in (1, 2, 3)] + [along_y(k) for k in (1, 2, 3)])
    for target in partners:
        pl.semaphore_signal(barrier, inc=1, device_id=target, device_id_type=MESH)
    pl.semaphore_wait(barrier, len(partners))

    def columns(t, h):
        return pl.ds(pl.multiple_of(t * 256 + h * 128, 128), 128)

    big, small = lax.div(z_lo, 2), lax.rem(z_lo, 2) * 4 + core * 2 + z_hi
    halves = []
    for h in (0, 1):
        if h:
            for copy in halves[0]:
                copy.wait_send()
        copies = []
        for o in far_first:
            t = lax.rem(me + o, 32)
            copies.append(send(x_ref.at[:, columns(t, h)], zbuf.at[h, big, small],
                               z_send.at[h, o], z_recv.at[h, o], line(t)))
        halves.append(copies)
    here = [pltpu.make_async_copy(x_ref.at[:, columns(me, h)], zbuf.at[h, big, small], local_sem.at[h])
            for h in (0, 1)]
    for copy in here:
        copy.start()

    giver = lax.div(row, 4) == y
    basis_slot = lax.rem(row, 4)

    def basis_copy(n, t):
        return remote(start_ref, start.at[basis_slot], st_send.at[n], st_recv.at[basis_slot],
                      (t, col, y))

    for n, t in enumerate((2, 10)):
        @pl.when(giver & (row != t))
        def _():
            basis_copy(n, t).start()

    @pl.when(giver)
    def _():
        copy = pltpu.make_async_copy(start_ref, start.at[basis_slot], local_sem.at[2])
        copy.start()
        copy.wait()

    first = []
    for h in (0, 1):
        here[h].wait()
        for copy in halves[h]:
            if h:
                copy.wait_send()
            copy.wait_recv()
        pairs = []
        for k in (2, 1, 3):
            pairs.append((
                send(zbuf.at[h, lax.rem(x + k, 4)], abuf.at[h, y, :, x],
                     plane_send.at[h, 0, k], plane_recv.at[h, 0, k], along_x(k)),
                send(zbuf.at[h, lax.rem(y + k, 4)], bbuf.at[h, y, :, x],
                     plane_send.at[h, 1, k], plane_recv.at[h, 1, k], along_y(k))))
        first.append(pairs)
        abuf[h, y, :, x] = zbuf[h, x]
        bbuf[h, y, :, x] = zbuf[h, y]
    gathers = []
    for h in (0, 1):
        group_copies = []
        for copy, _ in first[h]:
            copy.wait()
        for k in (2, 1, 3):
            group_copies.append(send_pieces(4, abuf.at[h, y], abuf.at[h, y],
                                     gather_send.at[h, 0, k], gather_recv.at[h, 0, k], along_y(k)))
        for _, copy in first[h]:
            copy.wait()
        for k in (2, 1, 3):
            group_copies.append(send_pieces(4, bbuf.at[h, :, :, x], bbuf.at[h, :, :, x],
                                     gather_send.at[h, 1, k], gather_recv.at[h, 1, k], along_x(k)))
        gathers.append(group_copies)

    for h in (0, 1):
        for copy in gathers[h]:
            copy.wait()
        b = jnp.concatenate([bbuf[h, q].reshape(512, 128) for q in range(4)], axis=1)
        b_wide = b.astype(F32)
        ones = jnp.ones((16, 512), BF16)
        b_norm = sum(dot(ones, p, ((1,), (1,))) for p in parts(b_wide * b_wide, 2))[0:1]
        for half in (1 - core, core):
            a = jnp.concatenate(
                [abuf[h, q, pl.ds(half * 4, 4)].reshape(256, 128) for q in range(4)], axis=1)
            a_wide = a.astype(F32)
            a_norm = jnp.sum(a_wide * a_wide, axis=1, keepdims=True)
            value = (a_norm + b_norm - 2.0 * dot(a, b, ((1,), (1,)))).reshape(4, 4, 16, 512)
            if h == 1:
                value = value + part[half]
            part[half] = value
            if h == 1 and half is not core:
                core_sums = [send_pieces(2, part.at[half, n], sib.at[n], sib_send.at[n], sib_recv.at[n], sibling)
                             for n in range(4)]

    for n in range(4):
        core_sums[n].wait()
        own[pl.ds(n * 4, 4)] = part[core, n] + sib[n]

    def at_plane(o):
        return device(x, y, lax.rem(z + o + 16, 16), core)

    for d in (8, 7, 6, 5):
        send(own.at[lax.rem(z + d, 16)], rs_up.at[d - 5], rs_send.at[0], rs_recv.at[0], at_plane(d - 4))
        if d < 8:
            send(own.at[lax.rem(z + 16 - d, 16)], rs_down.at[d - 5], rs_send.at[1], rs_recv.at[1], at_plane(4 - d))
    for d in (3, 2, 1):
        send(own.at[lax.rem(z + d, 16)], rs_near.at[d - 1], rs_send.at[2], rs_recv.at[2], at_plane(d))
        send(own.at[lax.rem(z + 16 - d, 16)], rs_near.at[d + 2], rs_send.at[2], rs_recv.at[2], at_plane(-d))
    remote(rs_up, rs_up, rs_send.at[0], rs_recv.at[0], sibling).wait_recv()
    rs_sum[0] = own[lax.rem(z + 4, 16)] + four(rs_up)
    last_up = send(rs_sum.at[0], rs_last.at[0], rs_send.at[3], rs_recv.at[3], at_plane(4))
    remote(rs_down, rs_down, rs_send.at[1], rs_recv.at[1], sibling).wait_recv()
    rs_sum[1] = own[lax.rem(z + 12, 16)] + (rs_down[0] + rs_down[1] + rs_down[2])
    last_down = send(rs_sum.at[1], rs_last.at[1], rs_send.at[4], rs_recv.at[4], at_plane(-4))
    remote(rs_near, rs_near, rs_send.at[2], rs_recv.at[2], sibling).wait()
    near = own[z] + ((rs_near[0] + rs_near[1]) + (rs_near[2] + rs_near[3]) + (rs_near[4] + rs_near[5]))
    last_up.wait()
    last_down.wait()
    total[...] = near + (rs_last[0] + rs_last[1])
    remote(rs_up, rs_up, rs_send.at[0], rs_recv.at[0], sibling).wait_send()
    remote(rs_down, rs_down, rs_send.at[1], rs_recv.at[1], sibling).wait_send()

    my_rows = pl.ds(pl.multiple_of(128 + z * 16, 16), 16)

    def gather(n, p):
        return remote(total, ext.at[my_rows, pl.ds(128, 512)], ag_send.at[n], ag_recv.at[0],
                      device(x, y, p, core))

    def each_gather(do):
        for n, p in enumerate(PLANES):
            @pl.when(z != p)
            def _():
                do(gather(n, p))

    each_gather(lambda copy: copy.start())

    @pl.when(iterates)
    def _():
        ext[my_rows, 128:640] = total[...]
        view = ext.at[pl.ds(0, 240), pl.ds(128, 512)]
        remote(view, view, ag_send.at[0], ag_recv.at[0], sibling).wait_recv()

        x_next, y_next = lax.rem(x + core, 4), lax.rem(y + 1, 4)
        below, right, both = (
            device(x_next, y, z, 1 - core), device(x, y_next, z, core), device(x_next, y_next, z, 1 - core))
        bottom, inner, edge = pl.ds(256, 128), pl.ds(128, 512), pl.ds(512, 128)
        halo = [
            send_pieces(4, ext.at[bottom, inner], ext.at[pl.ds(0, 128), inner],
                        halo_send.at[0], halo_recv.at[0], below),
            send_pieces(2, ext.at[bottom, edge], ext.at[pl.ds(0, 128), pl.ds(0, 128)],
                        halo_send.at[2], halo_recv.at[2], both),
            send_pieces(4, ext.at[pl.ds(128, 256), edge], ext.at[pl.ds(128, 256), pl.ds(0, 128)],
                        halo_send.at[1], halo_recv.at[1], right),
        ]
        for copy in halo:
            copy.wait()
        rows = lax.broadcasted_iota(jnp.int32, (384, 640), 0)
        lanes = lax.broadcasted_iota(jnp.int32, (384, 640), 1)
        first_row = jnp.where(2 * x + core == 0, 128, 0)
        first_lane = jnp.where(y == 0, 128, 0)
        run = jnp.where((rows >= first_row) & (lanes >= first_lane), ext[...], 0.0)
        stride = LAGS // 2
        while stride >= 1:
            turned = pltpu.roll(run, stride, 1)
            if stride >= 8:
                run = run[stride:] + turned[:-stride]
            else:
                run = run + pltpu.roll(turned, stride, 0)
            stride //= 2
        lagged = run[8:, 128:]
        i = lax.broadcasted_iota(jnp.int32, (256, 512), 0) + (x * 512 + core * 256)
        j = lax.broadcasted_iota(jnp.int32, (256, 512), 1) + y * 512
        counts = (jnp.minimum(jnp.minimum(i, j), LAGS - 1) + 1).astype(F32)
        half_tile = jnp.exp(-(lagged / (counts * (PTS * 0.25))))
        half_hi, half_lo = parts(half_tile, 2)
        my_half = pl.ds(pl.multiple_of(core * 256, 256), 256)
        kern_hi[my_half, :] = half_hi
        kern_lo[my_half, :] = half_lo
        swaps = [remote(ref.at[my_half, :], ref.at[my_half, :], core_send.at[n], core_recv.at[n], sibling)
                 for n, ref in enumerate((kern_hi, kern_lo))]

        @pl.when(core == 1)
        def _():
            for n, ref in enumerate((kern_hi, kern_lo)):
                send_pieces(4, ref.at[my_half, :], ref.at[my_half, :], core_send.at[n], core_recv.at[n], sibling)

        ones = jnp.ones((16, 512), BF16)
        deg_row[core, y] = (dot(ones, half_hi, ((1,), (1,))) + dot(ones, half_lo, ((1,), (1,))))[:8]
        deg_col[core, x] = (dot(ones[:, :256], half_hi, ((1,), (0,)))
                            + dot(ones[:, :256], half_lo, ((1,), (0,))))[:8]

        def degree_copies(k):
            row_view, col_view = deg_row.at[core, y], deg_col.at[core, x]
            return (remote(row_view, row_view, deg_send.at[0, k], deg_recv.at[0, core, k], along_y(k, 0)),
                    remote(col_view, col_view, deg_send.at[1, k], deg_recv.at[1, core, k], along_x(k, 0)))

        @pl.when(core == 1)
        def _():
            for k in (2, 1, 3, 0):
                for copy in degree_copies(k):
                    copy.start()
            for copy in swaps:
                copy.wait_send()
            for k in range(4):
                for copy in degree_copies(k):
                    copy.wait_send()

    @pl.when(iterates & (core == 0))
    def _():
        def degree_copy(n, c, k):
            ref = (deg_row, deg_col)[n].at[c, 0]
            return remote(ref, ref, deg_send.at[n, k], deg_recv.at[n, c, k], sibling)

        for k in (2, 1, 3):
            for n, ref, target in ((0, deg_row.at[0, y], along_y(k)), (1, deg_col.at[0, x], along_x(k))):
                remote(ref, ref, deg_send.at[n, k], deg_recv.at[n, 0, k], target).start()
        wide[...] = jnp.zeros_like(wide)

        def gram_of(block):
            wide[0:32, :] = block
            return dot(block, wide[...], ((1,), (1,)), HIGH)

        for k in range(4):
            @pl.when(row != 4 * y + k)
            def _():
                remote(start_ref, start.at[k], st_send.at[2], st_recv.at[k], sibling).wait_recv()
        mine = [start[k].T for k in range(4)]
        basis = [jnp.concatenate(mine[:2], axis=1), jnp.concatenate(mine[2:], axis=1)]
        other_half = pl.ds(256, 256)
        for n, ref in enumerate((kern_hi, kern_lo)):
            remote(ref.at[other_half, :], ref.at[other_half, :], core_send.at[n], core_recv.at[n], sibling).wait_recv()
        for n in (0, 1):
            for k in (1, 2, 3):
                degree_copy(n, 0, k).wait()
            for k in range(4):
                degree_copy(n, 1, k).wait_recv()
        row_sums = jnp.concatenate([four(deg_row.at[0]), four(deg_row.at[1])], axis=1)[0:1]
        scale_row = 1.0 / jnp.sqrt(row_sums)
        scale_col = 1.0 / jnp.sqrt((four(deg_col.at[0]) + four(deg_col.at[1]))[0:1])
        scale_row = scale_row[:, :256], scale_row[:, 256:]
        scale_col = scale_col[:, :256], scale_col[:, 256:]

        def term(over_y, n, m, block):
            n, m = pl.ds(n * 256, 256), pl.ds(m * 256, 256)
            at, dims = ((m, n), ((1,), (1,))) if over_y else ((n, m), ((1,), (0,)))
            high = dot(jnp.concatenate(block, axis=0), kern_hi[at], dims)
            low = dot(jnp.concatenate(block[:2], axis=0), kern_lo[at], dims)
            return high[:32] + ((high[32:64] + low[:32]) + (high[64:] + low[32:]))

        def arrived(step, n):
            for copy in copies[n]:
                copy.wait()
            block = four(income.at[step, n])
            return dot(inverse, block, ((1,), (0,)), HIGH) if step in (3, 5) else block

        inverse = None
        gram_copies = None
        copies = None
        for step in range(6):
            over_y = step % 2 == 0
            at = y if over_y else x
            scale_in, scale_out = (scale_col, scale_row) if over_y else (scale_row, scale_col)
            sums = None
            sent = []
            for n in (0, 1):
                if step:
                    basis[n] = arrived(step - 1, n)
                block = parts(basis[n] * scale_in[n], 3)
                if n == 0:
                    sums = [term(over_y, 0, m, block) for m in (0, 1)]
                    continue
                for m in (0, 1):
                    income[step, m, at] = (sums[m] + term(over_y, 1, m, block)) * scale_out[m]
                    view = income.at[step, m, at]
                    sent.append([send(view, view, step_send.at[step, m, k], step_recv.at[step, m, k],
                                      along_y(k) if over_y else along_x(k)) for k in (2, 1, 3)])
            copies = sent
            if step in (2, 4):
                n = step // 2 - 1
                grams[n, y] = gram_of(jnp.concatenate(basis, axis=1))
                gram_copies = [send(grams.at[n, y], grams.at[n, y], gram_send.at[n, k],
                                    gram_recv.at[n, k], along_y(k)) for k in (2, 1, 3)]
            if step in (3, 5):
                for copy in gram_copies:
                    copy.wait()
                inverse = inverse_factor(four(grams.at[step // 2 - 1]))
        basis = jnp.concatenate([arrived(5, 0), arrived(5, 1)], axis=1)

        owner = lax.div(y, 2) == lax.rem(group, 2)

        def row_copy(k, i, c):
            return remote(last.at[:, pl.ds((i * 2 + c) * 128, 128)], last_rows, row_send.at[k, i, c],
                          row_recv.at[0], device(x, lax.rem(y + k, 4), z_hi * 8 + 2 * y + i, c))

        def each_row_copy(do):
            for k in (2, 1, 3, 0):
                for i in (0, 1):
                    for c in (0, 1):
                        if k or c:
                            do(row_copy(k, i, c))
                        else:
                            @pl.when(z_lo != 2 * y + i)
                            def _():
                                do(row_copy(k, i, c))

        gram = gram_of(basis)
        last_grams[y] = jnp.concatenate([gram[8 * n:8 * n + 8, :32] for n in range(4)], axis=1)
        waits = []
        for k in (2, 1, 3, 0):
            for i in (2, 1, 3, 0):
                for c in (0, 1):
                    if k or i or c:
                        target = device(x, lax.rem(y + k, 4), group * 4 + lax.rem(1 + i, 4), c)
                        waits.append(send(last_grams.at[y], last_grams.at[y], fin_send.at[k, i, c],
                                          fin_recv.at[y], target))

        last[...] = basis

        @pl.when(owner)
        def _():
            each_row_copy(lambda copy: copy.start())
            for i in (0, 1):
                @pl.when(z_lo == 2 * y + i)
                def _():
                    last_rows[...] = last[:, i * 256:i * 256 + 128]

        for copy in waits:
            copy.wait_send()

        @pl.when(owner)
        def _():
            each_row_copy(lambda copy: copy.wait_send())

    for q in range(4):
        @pl.when(jnp.logical_not(iterates & (core == 0) & (y == q)))
        def _():
            remote(last_grams.at[q], last_grams.at[q], fin_send.at[0, 0, 0], fin_recv.at[q], sibling).wait_recv()
    packed = four(last_grams)
    packed = jnp.concatenate([packed[:, 32 * n:32 * n + 32] for n in range(4)], axis=0)
    inverse = inverse_factor(jnp.concatenate([packed, jnp.zeros((32, 96), F32)], axis=1))

    @pl.when(jnp.logical_not(iterates & (core == 0) & (y == lax.div(z_lo, 2))))
    def _():
        remote(last_rows, last_rows, row_send.at[0, 0, 0], row_recv.at[0], sibling).wait_recv()

    out_ref[...] = dot(inverse, last_rows[...], ((1,), (0,)), HIGH) * math.sqrt(SNAPS)

    for n, t in enumerate((2, 10)):
        @pl.when(giver & (row != t))
        def _():
            basis_copy(n, t).wait_send()
    each_gather(lambda copy: copy.wait_send())


VMEM = pl.BlockSpec(memory_space=pltpu.VMEM)
ANY = pl.BlockSpec(memory_space=pl.ANY)
DMA = pltpu.SemaphoreType.DMA


def body(snapshots, start_block):
    out = pl.pallas_call(
        kernel,
        out_shape=jax.ShapeDtypeStruct((32, 128), F32),
        in_specs=[ANY, ANY],
        out_specs=VMEM,
        scratch_shapes=[
            pltpu.VMEM((2, 4, 8, 16, 128), BF16),
            pltpu.VMEM((2, 4, 8, 4, 16, 128), BF16),
            pltpu.VMEM((2, 4, 8, 4, 16, 128), BF16),
            pltpu.VMEM((2, 4, 4, 16, 512), F32),
            pltpu.VMEM((4, 4, 16, 512), F32),
            pltpu.VMEM((16, 16, 512), F32),
            pltpu.VMEM((4, 16, 512), F32),
            pltpu.VMEM((3, 16, 512), F32),
            pltpu.VMEM((6, 16, 512), F32),
            pltpu.VMEM((2, 16, 512), F32),
            pltpu.VMEM((2, 16, 512), F32),
            pltpu.VMEM((16, 512), F32),
            pltpu.VMEM((4, 128, 32), F32),
            pltpu.VMEM((384, 640), F32),
            pltpu.VMEM((512, 512), BF16),
            pltpu.VMEM((512, 512), BF16),
            pltpu.VMEM((2, 4, 8, 256), F32),
            pltpu.VMEM((2, 4, 8, 512), F32),
            pltpu.VMEM((128, 512), F32),
            pltpu.VMEM((6, 2, 4, 32, 256), F32),
            pltpu.VMEM((2, 4, 32, 128), F32),
            pltpu.VMEM((32, 512), F32),
            pltpu.VMEM((32, 128), F32),
            pltpu.VMEM((4, 8, 128), F32),
            DMA((3,)), DMA((2, 32)), DMA((2, 32)), DMA((2, 2, 4)), DMA((2, 2, 4)), DMA((2, 2, 4)), DMA((2, 2, 4)),
            DMA((4,)), DMA((4,)), DMA((5,)), DMA((5,)), DMA((4,)), DMA((1,)), DMA((3,)), DMA((4,)),
            DMA((3,)), DMA((3,)), DMA((2,)), DMA((2,)), DMA((2, 4)), DMA((2, 2, 4)),
            DMA((6, 2, 4)), DMA((6, 2, 4)), DMA((2, 4)), DMA((2, 4)), DMA((4, 4, 2)), DMA((4,)),
            DMA((4, 2, 2)), DMA((1,)),
        ],
        compiler_params=pltpu.CompilerParams(
            collective_id=1, has_side_effects=True, vmem_limit_bytes=48 << 20),
        name="subspace",
    )(snapshots, start_block)
    return out.T


def solution(mesh):
    placed = (P(("row", "col"), "feat"), P("row", None))
    return jax.shard_map(
        body, mesh=mesh, in_specs=placed, out_specs=P("row", None), check_vma=False
    )
```

```python
import math

import jax
import jax.numpy as jnp
from jax import lax
from jax.experimental import pallas as pl
from jax.experimental.pallas import tpu as pltpu
from jax.sharding import PartitionSpec as P

PTS = 32768
LAGS = 128
SNAPS = 2048
MESH = pl.DeviceIdType.MESH
HIGH = lax.Precision.HIGHEST
F32 = jnp.float32
BF16 = jnp.bfloat16


def device(x, y, z, core):
    return (lax.rem(z, 8) * 2 + core, lax.div(z, 8) * 4 + x, y)


def remote(src, dst, send_sem, recv_sem, target):
    return pltpu.make_async_remote_copy(
        src_ref=src, dst_ref=dst, send_sem=send_sem, recv_sem=recv_sem,
        device_id=target, device_id_type=MESH,
    )


def send(*args):
    copy = remote(*args)
    copy.start()
    return copy


def send_pieces(count, src, dst, send_sem, recv_sem, target):
    rows = src.shape[0] // count
    for n in range(count):
        piece = pl.ds(n * rows, rows)
        send(src.at[piece], dst.at[piece], send_sem, recv_sem, target)
    return remote(src, dst, send_sem, recv_sem, target)


def dot(a, b, dims, precision=None):
    return lax.dot_general(
        a, b, (dims, ((), ())), precision=precision, preferred_element_type=F32
    )


def parts(value, count):
    out = []
    for _ in range(count):
        out.append(value.astype(BF16))
        value = value - out[-1].astype(F32)
    return out


def inverse_factor(gram):
    rows = lax.broadcasted_iota(jnp.int32, (32, 128), 0)
    lanes = lax.broadcasted_iota(jnp.int32, (32, 128), 1)
    work = jnp.where(lanes < 32, gram, jnp.where(lanes - 32 == rows, 1.0, 0.0))
    for k in range(0, 32, 16):
        tops = [work[k + n:k + n + 1, :] for n in range(16)]
        columns = [jnp.broadcast_to(work[:, k + n:k + n + 1], (32, 128)) for n in range(16)]
        for n in range(16):
            at = k + n
            ratio = columns[n] * (1.0 / columns[n][at:at + 1, :])
            for m in range(n + 1, 16):
                tops[m] = tops[m] - ratio[k + m:k + m + 1, :] * tops[n]
                columns[m] = columns[m] - ratio * columns[m][at:at + 1, :]
            work = work - jnp.where(rows > at, ratio, 0.0) * tops[n]
    diagonal = jnp.sum(jnp.where(lanes == rows, work, 0.0), axis=1, keepdims=True)
    return work[:, 32:64] / jnp.sqrt(diagonal)


def four(ref):
    return (ref[0] + ref[1]) + (ref[2] + ref[3])


def kernel(
    x_ref, start_ref, out_ref,
    zbuf, abuf, bbuf, part, sib, own, rs_up, rs_down, rs_near, rs_sum, rs_last, total, start,
    ext, kern_hi, kern_lo, deg_row, deg_col, wide, income, grams, last, last_rows, last_grams,
    local_sem, z_send, z_recv, plane_send, plane_recv, gather_send, gather_recv,
    sib_send, sib_recv, rs_send, rs_recv, ag_send, ag_recv, st_send, st_recv,
    halo_send, halo_recv, core_send, core_recv, deg_send, deg_recv,
    step_send, step_recv, gram_send, gram_recv, fin_send, fin_recv, row_send, row_recv,
):
    row, col, y = lax.axis_index("row"), lax.axis_index("col"), lax.axis_index("feat")
    x, z_hi = lax.rem(col, 4), lax.div(col, 4)
    core, z_lo = lax.rem(row, 2), lax.div(row, 2)
    z = z_hi * 8 + z_lo
    me = z * 2 + core
    group = lax.div(z, 4)
    iterates = lax.rem(z, 4) == 1

    def line(t):
        return device(x, y, lax.div(t, 2), lax.rem(t, 2))

    def along_x(k, c=core):
        return device(lax.rem(x + k, 4), y, z, c)

    def along_y(k, c=core):
        return device(x, lax.rem(y + k, 4), z, c)

    sibling = device(x, y, z, 1 - core)
    barrier = pltpu.get_barrier_semaphore()
    far_first = sorted(range(1, 32), key=lambda o: -min(o, 32 - o))
    partners = ([line(lax.rem(me + o, 32)) for o in far_first]
                + [along_x(k) for k in (1, 2, 3)] + [along_y(k) for k in (1, 2, 3)])
    for target in partners:
        pl.semaphore_signal(barrier, inc=1, device_id=target, device_id_type=MESH)
    pl.semaphore_wait(barrier, len(partners))

    def columns(t, h):
        return pl.ds(pl.multiple_of(t * 256 + h * 128, 128), 128)

    big, small = lax.div(z_lo, 2), lax.rem(z_lo, 2) * 4 + core * 2 + z_hi
    halves = []
    for h in (0, 1):
        if h:
            for copy in halves[0]:
                copy.wait_send()
        copies = []
        for o in far_first:
            t = lax.rem(me + o, 32)
            copies.append(send(x_ref.at[:, columns(t, h)], zbuf.at[h, big, small],
                               z_send.at[h, o], z_recv.at[h, o], line(t)))
        halves.append(copies)
    here = [pltpu.make_async_copy(x_ref.at[:, columns(me, h)], zbuf.at[h, big, small], local_sem.at[h])
            for h in (0, 1)]
    for copy in here:
        copy.start()

    giver = lax.div(row, 4) == y
    basis_slot = lax.rem(row, 4)

    def basis_copy(n, t):
        return remote(start_ref, start.at[basis_slot], st_send.at[n], st_recv.at[basis_slot],
                      (t, col, y))

    for n, t in enumerate((2, 10)):
        @pl.when(giver & (row != t))
        def _():
            basis_copy(n, t).start()

    @pl.when(giver)
    def _():
        copy = pltpu.make_async_copy(start_ref, start.at[basis_slot], local_sem.at[2])
        copy.start()
        copy.wait()

    first = []
    for h in (0, 1):
        here[h].wait()
        for copy in halves[h]:
            if h:
                copy.wait_send()
            copy.wait_recv()
        pairs = []
        for k in (2, 1, 3):
            pairs.append((
                send(zbuf.at[h, lax.rem(x + k, 4)], abuf.at[h, y, :, x],
                     plane_send.at[h, 0, k], plane_recv.at[h, 0, k], along_x(k)),
                send(zbuf.at[h, lax.rem(y + k, 4)], bbuf.at[h, y, :, x],
                     plane_send.at[h, 1, k], plane_recv.at[h, 1, k], along_y(k))))
        first.append(pairs)
        abuf[h, y, :, x] = zbuf[h, x]
        bbuf[h, y, :, x] = zbuf[h, y]
    gathers = []
    for h in (0, 1):
        group_copies = []
        for copy, _ in first[h]:
            copy.wait()
        for k in (2, 1, 3):
            group_copies.append(send_pieces(4, abuf.at[h, y], abuf.at[h, y],
                                     gather_send.at[h, 0, k], gather_recv.at[h, 0, k], along_y(k)))
        for _, copy in first[h]:
            copy.wait()
        for k in (2, 1, 3):
            group_copies.append(send_pieces(4, bbuf.at[h, :, :, x], bbuf.at[h, :, :, x],
                                     gather_send.at[h, 1, k], gather_recv.at[h, 1, k], along_x(k)))
        gathers.append(group_copies)

    for h in (0, 1):
        for copy in gathers[h]:
            copy.wait()
        b = jnp.concatenate([bbuf[h, q].reshape(512, 128) for q in range(4)], axis=1)
        b_wide = b.astype(F32)
        ones = jnp.ones((16, 512), BF16)
        b_norm = sum(dot(ones, p, ((1,), (1,))) for p in parts(b_wide * b_wide, 2))[0:1]
        for half in (1 - core, core):
            a = jnp.concatenate(
                [abuf[h, q, pl.ds(half * 4, 4)].reshape(256, 128) for q in range(4)], axis=1)
            a_wide = a.astype(F32)
            a_norm = jnp.sum(a_wide * a_wide, axis=1, keepdims=True)
            value = (a_norm + b_norm - 2.0 * dot(a, b, ((1,), (1,)))).reshape(4, 4, 16, 512)
            if h == 1:
                value = value + part[half]
            part[half] = value
            if h == 1 and half is not core:
                core_sums = [send_pieces(2, part.at[half, n], sib.at[n], sib_send.at[n], sib_recv.at[n], sibling)
                             for n in range(4)]

    for n in range(4):
        core_sums[n].wait()
        own[pl.ds(n * 4, 4)] = part[core, n] + sib[n]

    def at_plane(o):
        return device(x, y, lax.rem(z + o + 16, 16), core)

    for d in (8, 7, 6, 5):
        send(own.at[lax.rem(z + d, 16)], rs_up.at[d - 5], rs_send.at[0], rs_recv.at[0], at_plane(d - 4))
        if d < 8:
            send(own.at[lax.rem(z + 16 - d, 16)], rs_down.at[d - 5], rs_send.at[1], rs_recv.at[1], at_plane(4 - d))
    for d in (3, 2, 1):
        send(own.at[lax.rem(z + d, 16)], rs_near.at[d - 1], rs_send.at[2], rs_recv.at[2], at_plane(d))
        send(own.at[lax.rem(z + 16 - d, 16)], rs_near.at[d + 2], rs_send.at[2], rs_recv.at[2], at_plane(-d))
    remote(rs_up, rs_up, rs_send.at[0], rs_recv.at[0], sibling).wait_recv()
    rs_sum[0] = own[lax.rem(z + 4, 16)] + four(rs_up)
    last_up = send(rs_sum.at[0], rs_last.at[0], rs_send.at[3], rs_recv.at[3], at_plane(4))
    remote(rs_down, rs_down, rs_send.at[1], rs_recv.at[1], sibling).wait_recv()
    rs_sum[1] = own[lax.rem(z + 12, 16)] + (rs_down[0] + rs_down[1] + rs_down[2])
    last_down = send(rs_sum.at[1], rs_last.at[1], rs_send.at[4], rs_recv.at[4], at_plane(-4))
    remote(rs_near, rs_near, rs_send.at[2], rs_recv.at[2], sibling).wait()
    near = own[z] + ((rs_near[0] + rs_near[1]) + (rs_near[2] + rs_near[3]) + (rs_near[4] + rs_near[5]))
    last_up.wait()
    last_down.wait()
    total[...] = near + (rs_last[0] + rs_last[1])
    remote(rs_up, rs_up, rs_send.at[0], rs_recv.at[0], sibling).wait_send()
    remote(rs_down, rs_down, rs_send.at[1], rs_recv.at[1], sibling).wait_send()

    my_rows = pl.ds(pl.multiple_of(128 + z * 16, 16), 16)

    def gather(n, p):
        return (total, ext.at[my_rows, pl.ds(128, 512)], ag_send.at[n], ag_recv.at[0],
                device(x, y, p, core))

    def each_gather(do):
        for n in (2, 1, 3):
            do(gather(n, lax.rem(group + n, 4) * 4 + 1))

        @pl.when(jnp.logical_not(iterates))
        def _():
            do(gather(0, group * 4 + 1))

    each_gather(lambda copy: send_pieces(2, *copy))

    @pl.when(iterates)
    def _():
        ext[my_rows, 128:640] = total[...]
        view = ext.at[pl.ds(0, 240), pl.ds(128, 512)]
        remote(view, view, ag_send.at[0], ag_recv.at[0], sibling).wait_recv()

        x_next, y_next = lax.rem(x + core, 4), lax.rem(y + 1, 4)
        below, right, both = (
            device(x_next, y, z, 1 - core), device(x, y_next, z, core), device(x_next, y_next, z, 1 - core))
        bottom, inner, edge = pl.ds(256, 128), pl.ds(128, 512), pl.ds(512, 128)
        halo = [
            send_pieces(4, ext.at[bottom, inner], ext.at[pl.ds(0, 128), inner],
                        halo_send.at[0], halo_recv.at[0], below),
            send_pieces(2, ext.at[bottom, edge], ext.at[pl.ds(0, 128), pl.ds(0, 128)],
                        halo_send.at[2], halo_recv.at[2], both),
            send_pieces(4, ext.at[pl.ds(128, 256), edge], ext.at[pl.ds(128, 256), pl.ds(0, 128)],
                        halo_send.at[1], halo_recv.at[1], right),
        ]
        for copy in halo:
            copy.wait()
        rows = lax.broadcasted_iota(jnp.int32, (384, 640), 0)
        lanes = lax.broadcasted_iota(jnp.int32, (384, 640), 1)
        first_row = jnp.where(2 * x + core == 0, 128, 0)
        first_lane = jnp.where(y == 0, 128, 0)
        run = jnp.where((rows >= first_row) & (lanes >= first_lane), ext[...], 0.0)
        stride = LAGS // 2
        while stride >= 1:
            turned = pltpu.roll(run, stride, 1)
            if stride >= 8:
                run = run[stride:] + turned[:-stride]
            else:
                run = run + pltpu.roll(turned, stride, 0)
            stride //= 2
        lagged = run[8:, 128:]
        i = lax.broadcasted_iota(jnp.int32, (256, 512), 0) + (x * 512 + core * 256)
        j = lax.broadcasted_iota(jnp.int32, (256, 512), 1) + y * 512
        counts = (jnp.minimum(jnp.minimum(i, j), LAGS - 1) + 1).astype(F32)
        half_tile = jnp.exp(-(lagged / (counts * (PTS * 0.25))))
        half_hi, half_lo = parts(half_tile, 2)
        my_half = pl.ds(pl.multiple_of(core * 256, 256), 256)
        kern_hi[my_half, :] = half_hi
        kern_lo[my_half, :] = half_lo
        swaps = [remote(ref.at[my_half, :], ref.at[my_half, :], core_send.at[n], core_recv.at[n], sibling)
                 for n, ref in enumerate((kern_hi, kern_lo))]

        @pl.when(core == 1)
        def _():
            for n, ref in enumerate((kern_hi, kern_lo)):
                send_pieces(4, ref.at[my_half, :], ref.at[my_half, :], core_send.at[n], core_recv.at[n], sibling)

        ones = jnp.ones((16, 512), BF16)
        deg_row[core, y] = (dot(ones, half_hi, ((1,), (1,))) + dot(ones, half_lo, ((1,), (1,))))[:8]
        deg_col[core, x] = (dot(ones[:, :256], half_hi, ((1,), (0,)))
                            + dot(ones[:, :256], half_lo, ((1,), (0,))))[:8]

        def degree_copies(k):
            row_view, col_view = deg_row.at[core, y], deg_col.at[core, x]
            return (remote(row_view, row_view, deg_send.at[0, k], deg_recv.at[0, core, k], along_y(k, 0)),
                    remote(col_view, col_view, deg_send.at[1, k], deg_recv.at[1, core, k], along_x(k, 0)))

        @pl.when(core == 1)
        def _():
            for k in (2, 1, 3, 0):
                for copy in degree_copies(k):
                    copy.start()
            for copy in swaps:
                copy.wait_send()
            for k in range(4):
                for copy in degree_copies(k):
                    copy.wait_send()

    @pl.when(iterates & (core == 0))
    def _():
        def degree_copy(n, c, k):
            ref = (deg_row, deg_col)[n].at[c, 0]
            return remote(ref, ref, deg_send.at[n, k], deg_recv.at[n, c, k], sibling)

        for k in (2, 1, 3):
            for n, ref, target in ((0, deg_row.at[0, y], along_y(k)), (1, deg_col.at[0, x], along_x(k))):
                remote(ref, ref, deg_send.at[n, k], deg_recv.at[n, 0, k], target).start()
        wide[...] = jnp.zeros_like(wide)

        def gram_of(block):
            wide[0:32, :] = block
            return dot(block, wide[...], ((1,), (1,)), HIGH)

        for k in range(4):
            @pl.when(row != 4 * y + k)
            def _():
                remote(start_ref, start.at[k], st_send.at[2], st_recv.at[k], sibling).wait_recv()
        mine = [start[k].T for k in range(4)]
        basis = [jnp.concatenate(mine[:2], axis=1), jnp.concatenate(mine[2:], axis=1)]
        other_half = pl.ds(256, 256)
        for n, ref in enumerate((kern_hi, kern_lo)):
            remote(ref.at[other_half, :], ref.at[other_half, :], core_send.at[n], core_recv.at[n], sibling).wait_recv()
        for n in (0, 1):
            for k in (1, 2, 3):
                degree_copy(n, 0, k).wait()
            for k in range(4):
                degree_copy(n, 1, k).wait_recv()
        row_sums = jnp.concatenate([four(deg_row.at[0]), four(deg_row.at[1])], axis=1)[0:1]
        scale_row = 1.0 / jnp.sqrt(row_sums)
        scale_col = 1.0 / jnp.sqrt((four(deg_col.at[0]) + four(deg_col.at[1]))[0:1])
        scale_row = scale_row[:, :256], scale_row[:, 256:]
        scale_col = scale_col[:, :256], scale_col[:, 256:]

        def term(over_y, n, m, block):
            n, m = pl.ds(n * 256, 256), pl.ds(m * 256, 256)
            at, dims = ((m, n), ((1,), (1,))) if over_y else ((n, m), ((1,), (0,)))
            high = dot(jnp.concatenate(block, axis=0), kern_hi[at], dims)
            low = dot(jnp.concatenate(block[:2], axis=0), kern_lo[at], dims)
            return high[:32] + ((high[32:64] + low[:32]) + (high[64:] + low[32:]))

        def arrived(step, n):
            for copy in copies[n]:
                copy.wait()
            block = four(income.at[step, n])
            return dot(inverse, block, ((1,), (0,)), HIGH) if step in (3, 5) else block

        inverse = None
        gram_copies = None
        copies = None
        for step in range(6):
            over_y = step % 2 == 0
            at = y if over_y else x
            scale_in, scale_out = (scale_col, scale_row) if over_y else (scale_row, scale_col)
            sums = None
            sent = []
            for n in (0, 1):
                if step:
                    basis[n] = arrived(step - 1, n)
                block = parts(basis[n] * scale_in[n], 3)
                if n == 0:
                    sums = [term(over_y, 0, m, block) for m in (0, 1)]
                    continue
                for m in (0, 1):
                    income[step, m, at] = (sums[m] + term(over_y, 1, m, block)) * scale_out[m]
                    view = income.at[step, m, at]
                    sent.append([send(view, view, step_send.at[step, m, k], step_recv.at[step, m, k],
                                      along_y(k) if over_y else along_x(k)) for k in (2, 1, 3)])
            copies = sent
            if step in (2, 4):
                n = step // 2 - 1
                grams[n, y] = gram_of(jnp.concatenate(basis, axis=1))
                gram_copies = [send(grams.at[n, y], grams.at[n, y], gram_send.at[n, k],
                                    gram_recv.at[n, k], along_y(k)) for k in (2, 1, 3)]
            if step in (3, 5):
                for copy in gram_copies:
                    copy.wait()
                inverse = inverse_factor(four(grams.at[step // 2 - 1]))
        basis = jnp.concatenate([arrived(5, 0), arrived(5, 1)], axis=1)

        owner = lax.div(y, 2) == lax.rem(group, 2)

        def row_copy(k, i, c):
            return remote(last.at[:, pl.ds((i * 2 + c) * 128, 128)], last_rows, row_send.at[k, i, c],
                          row_recv.at[0], device(x, lax.rem(y + k, 4), z_hi * 8 + 2 * y + i, c))

        def each_row_copy(do):
            for k in (2, 1, 3, 0):
                for i in (0, 1):
                    for c in (0, 1):
                        if k or c:
                            do(row_copy(k, i, c))
                        else:
                            @pl.when(z_lo != 2 * y + i)
                            def _():
                                do(row_copy(k, i, c))

        gram = gram_of(basis)
        last_grams[y] = jnp.concatenate([gram[8 * n:8 * n + 8, :32] for n in range(4)], axis=1)
        waits = []
        for k in (2, 1, 3, 0):
            for i in (2, 1, 3, 0):
                for c in (0, 1):
                    if k or i or c:
                        target = device(x, lax.rem(y + k, 4), group * 4 + lax.rem(1 + i, 4), c)
                        waits.append(send(last_grams.at[y], last_grams.at[y], fin_send.at[k, i, c],
                                          fin_recv.at[y], target))

        last[...] = basis

        @pl.when(owner)
        def _():
            each_row_copy(lambda copy: copy.start())
            for i in (0, 1):
                @pl.when(z_lo == 2 * y + i)
                def _():
                    last_rows[...] = last[:, i * 256:i * 256 + 128]

        for copy in waits:
            copy.wait_send()

        @pl.when(owner)
        def _():
            each_row_copy(lambda copy: copy.wait_send())

    for q in range(4):
        @pl.when(jnp.logical_not(iterates & (core == 0) & (y == q)))
        def _():
            remote(last_grams.at[q], last_grams.at[q], fin_send.at[0, 0, 0], fin_recv.at[q], sibling).wait_recv()
    packed = four(last_grams)
    packed = jnp.concatenate([packed[:, 32 * n:32 * n + 32] for n in range(4)], axis=0)
    inverse = inverse_factor(jnp.concatenate([packed, jnp.zeros((32, 96), F32)], axis=1))

    @pl.when(jnp.logical_not(iterates & (core == 0) & (y == lax.div(z_lo, 2))))
    def _():
        remote(last_rows, last_rows, row_send.at[0, 0, 0], row_recv.at[0], sibling).wait_recv()

    out_ref[...] = dot(inverse, last_rows[...], ((1,), (0,)), HIGH) * math.sqrt(SNAPS)

    for n, t in enumerate((2, 10)):
        @pl.when(giver & (row != t))
        def _():
            basis_copy(n, t).wait_send()
    each_gather(lambda copy: remote(*copy).wait_send())


VMEM = pl.BlockSpec(memory_space=pltpu.VMEM)
ANY = pl.BlockSpec(memory_space=pl.ANY)
DMA = pltpu.SemaphoreType.DMA


def body(snapshots, start_block):
    out = pl.pallas_call(
        kernel,
        out_shape=jax.ShapeDtypeStruct((32, 128), F32),
        in_specs=[ANY, ANY],
        out_specs=VMEM,
        scratch_shapes=[
            pltpu.VMEM((2, 4, 8, 16, 128), BF16),
            pltpu.VMEM((2, 4, 8, 4, 16, 128), BF16),
            pltpu.VMEM((2, 4, 8, 4, 16, 128), BF16),
            pltpu.VMEM((2, 4, 4, 16, 512), F32),
            pltpu.VMEM((4, 4, 16, 512), F32),
            pltpu.VMEM((16, 16, 512), F32),
            pltpu.VMEM((4, 16, 512), F32),
            pltpu.VMEM((3, 16, 512), F32),
            pltpu.VMEM((6, 16, 512), F32),
            pltpu.VMEM((2, 16, 512), F32),
            pltpu.VMEM((2, 16, 512), F32),
            pltpu.VMEM((16, 512), F32),
            pltpu.VMEM((4, 128, 32), F32),
            pltpu.VMEM((384, 640), F32),
            pltpu.VMEM((512, 512), BF16),
            pltpu.VMEM((512, 512), BF16),
            pltpu.VMEM((2, 4, 8, 256), F32),
            pltpu.VMEM((2, 4, 8, 512), F32),
            pltpu.VMEM((128, 512), F32),
            pltpu.VMEM((6, 2, 4, 32, 256), F32),
            pltpu.VMEM((2, 4, 32, 128), F32),
            pltpu.VMEM((32, 512), F32),
            pltpu.VMEM((32, 128), F32),
            pltpu.VMEM((4, 8, 128), F32),
            DMA((3,)), DMA((2, 32)), DMA((2, 32)), DMA((2, 2, 4)), DMA((2, 2, 4)), DMA((2, 2, 4)), DMA((2, 2, 4)),
            DMA((4,)), DMA((4,)), DMA((5,)), DMA((5,)), DMA((4,)), DMA((1,)), DMA((3,)), DMA((4,)),
            DMA((3,)), DMA((3,)), DMA((2,)), DMA((2,)), DMA((2, 4)), DMA((2, 2, 4)),
            DMA((6, 2, 4)), DMA((6, 2, 4)), DMA((2, 4)), DMA((2, 4)), DMA((4, 4, 2)), DMA((4,)),
            DMA((4, 2, 2)), DMA((1,)),
        ],
        compiler_params=pltpu.CompilerParams(
            collective_id=1, has_side_effects=True, vmem_limit_bytes=48 << 20),
        name="subspace",
    )(snapshots, start_block)
    return out.T


def solution(mesh):
    placed = (P(("row", "col"), "feat"), P("row", None))
    return jax.shard_map(
        body, mesh=mesh, in_specs=placed, out_specs=P("row", None), check_vma=False
    )
```

```python
import math

import jax
import jax.numpy as jnp
from jax import lax
from jax.experimental import pallas as pl
from jax.experimental.pallas import tpu as pltpu
from jax.sharding import PartitionSpec as P

PTS = 32768
LAGS = 128
SNAPS = 2048
MESH = pl.DeviceIdType.MESH
HIGH = lax.Precision.HIGHEST
F32 = jnp.float32
BF16 = jnp.bfloat16


def device(x, y, z, core):
    return (lax.rem(z, 8) * 2 + core, lax.div(z, 8) * 4 + x, y)


def remote(src, dst, send_sem, recv_sem, target):
    return pltpu.make_async_remote_copy(
        src_ref=src, dst_ref=dst, send_sem=send_sem, recv_sem=recv_sem,
        device_id=target, device_id_type=MESH,
    )


def send(*args):
    copy = remote(*args)
    copy.start()
    return copy


def send_pieces(count, src, dst, send_sem, recv_sem, target):
    rows = src.shape[0] // count
    for n in range(count):
        piece = pl.ds(n * rows, rows)
        send(src.at[piece], dst.at[piece], send_sem, recv_sem, target)
    return remote(src, dst, send_sem, recv_sem, target)


def dot(a, b, dims, precision=None):
    return lax.dot_general(
        a, b, (dims, ((), ())), precision=precision, preferred_element_type=F32
    )


def parts(value, count):
    out = []
    for _ in range(count):
        out.append(value.astype(BF16))
        value = value - out[-1].astype(F32)
    return out


def inverse_factor(gram):
    rows = lax.broadcasted_iota(jnp.int32, (32, 128), 0)
    lanes = lax.broadcasted_iota(jnp.int32, (32, 128), 1)
    work = jnp.where(lanes < 32, gram, jnp.where(lanes - 32 == rows, 1.0, 0.0))
    for k in range(0, 32, 16):
        tops = [work[k + n:k + n + 1, :] for n in range(16)]
        columns = [jnp.broadcast_to(work[:, k + n:k + n + 1], (32, 128)) for n in range(16)]
        for n in range(16):
            at = k + n
            ratio = columns[n] * (1.0 / columns[n][at:at + 1, :])
            for m in range(n + 1, 16):
                tops[m] = tops[m] - ratio[k + m:k + m + 1, :] * tops[n]
                columns[m] = columns[m] - ratio * columns[m][at:at + 1, :]
            work = work - jnp.where(rows > at, ratio, 0.0) * tops[n]
    diagonal = jnp.sum(jnp.where(lanes == rows, work, 0.0), axis=1, keepdims=True)
    return work[:, 32:64] / jnp.sqrt(diagonal)


def four(ref):
    return (ref[0] + ref[1]) + (ref[2] + ref[3])


def kernel(
    x_ref, start_ref, out_ref,
    zbuf, abuf, bbuf, part, sib, own, rs_up, rs_down, rs_near, rs_sum, rs_last, total, start,
    ext, kern_hi, kern_lo, deg_row, deg_col, wide, income, grams, last, last_rows, last_grams,
    local_sem, z_send, z_recv, plane_send, plane_recv, gather_send, gather_recv,
    sib_send, sib_recv, rs_send, rs_recv, ag_send, ag_recv, st_send, st_recv,
    halo_send, halo_recv, core_send, core_recv, deg_send, deg_recv,
    step_send, step_recv, gram_send, gram_recv, fin_send, fin_recv, row_send, row_recv,
):
    row, col, y = lax.axis_index("row"), lax.axis_index("col"), lax.axis_index("feat")
    x, z_hi = lax.rem(col, 4), lax.div(col, 4)
    core, z_lo = lax.rem(row, 2), lax.div(row, 2)
    z = z_hi * 8 + z_lo
    me = z * 2 + core
    group = lax.div(z, 4)
    iterates = lax.rem(z, 4) == 1

    def line(t):
        return device(x, y, lax.div(t, 2), lax.rem(t, 2))

    def along_x(k, c=core):
        return device(lax.rem(x + k, 4), y, z, c)

    def along_y(k, c=core):
        return device(x, lax.rem(y + k, 4), z, c)

    sibling = device(x, y, z, 1 - core)
    barrier = pltpu.get_barrier_semaphore()
    far_first = sorted(range(1, 32), key=lambda o: -min(o, 32 - o))
    partners = ([line(lax.rem(me + o, 32)) for o in far_first]
                + [along_x(k) for k in (1, 2, 3)] + [along_y(k) for k in (1, 2, 3)])
    for target in partners:
        pl.semaphore_signal(barrier, inc=1, device_id=target, device_id_type=MESH)
    pl.semaphore_wait(barrier, len(partners))

    def columns(t, h):
        return pl.ds(pl.multiple_of(t * 256 + h * 128, 128), 128)

    big, small = lax.div(z_lo, 2), lax.rem(z_lo, 2) * 4 + core * 2 + z_hi
    def half_wait(h):
        sent = x_ref.at[:, pl.ds(0, 31 * 128)]
        return (remote(sent, sent, z_send.at[h], z_recv.at[h], sibling),
                remote(zbuf.at[h], zbuf.at[h], z_send.at[h], z_recv.at[h], sibling))

    for h in (0, 1):
        if h:
            half_wait(0)[0].wait_send()
        for o in far_first:
            t = lax.rem(me + o, 32)
            send(x_ref.at[:, columns(t, h)], zbuf.at[h, big, small], z_send.at[h], z_recv.at[h], line(t))
        pltpu.make_async_copy(x_ref.at[:, columns(me, h)], zbuf.at[h, big, small], z_recv.at[h]).start()

    giver = lax.div(row, 4) == y
    basis_slot = lax.rem(row, 4)

    def basis_copy(n, t):
        return remote(start_ref, start.at[basis_slot], st_send.at[n], st_recv.at[basis_slot],
                      (t, col, y))

    for n, t in enumerate((2, 10)):
        @pl.when(giver & (row != t))
        def _():
            basis_copy(n, t).start()

    @pl.when(giver)
    def _():
        copy = pltpu.make_async_copy(start_ref, start.at[basis_slot], local_sem.at[0])
        copy.start()
        copy.wait()

    first = []
    for h in (0, 1):
        half_wait(h)[1].wait_recv()
        if h:
            half_wait(1)[0].wait_send()
        pairs = []
        for k in (2, 1, 3):
            pairs.append((
                send(zbuf.at[h, lax.rem(x + k, 4)], abuf.at[h, y, :, x],
                     plane_send.at[h, 0, k], plane_recv.at[h, 0, k], along_x(k)),
                send(zbuf.at[h, lax.rem(y + k, 4)], bbuf.at[h, y, :, x],
                     plane_send.at[h, 1, k], plane_recv.at[h, 1, k], along_y(k))))
        first.append(pairs)
        abuf[h, y, :, x] = zbuf[h, x]
        bbuf[h, y, :, x] = zbuf[h, y]
    gathers = []
    for h in (0, 1):
        group_copies = []
        for copy, _ in first[h]:
            copy.wait()
        for k in (2, 1, 3):
            group_copies.append(send_pieces(4, abuf.at[h, y], abuf.at[h, y],
                                     gather_send.at[h, 0, k], gather_recv.at[h, 0, k], along_y(k)))
        for _, copy in first[h]:
            copy.wait()
        for k in (2, 1, 3):
            group_copies.append(send_pieces(4, bbuf.at[h, :, :, x], bbuf.at[h, :, :, x],
                                     gather_send.at[h, 1, k], gather_recv.at[h, 1, k], along_x(k)))
        gathers.append(group_copies)

    for h in (0, 1):
        for copy in gathers[h]:
            copy.wait()
        b = jnp.concatenate([bbuf[h, q].reshape(512, 128) for q in range(4)], axis=1)
        b_wide = b.astype(F32)
        ones = jnp.ones((16, 512), BF16)
        b_norm = sum(dot(ones, p, ((1,), (1,))) for p in parts(b_wide * b_wide, 2))[0:1]
        for half in (1 - core, core):
            a = jnp.concatenate(
                [abuf[h, q, pl.ds(half * 4, 4)].reshape(256, 128) for q in range(4)], axis=1)
            a_wide = a.astype(F32)
            a_norm = jnp.sum(a_wide * a_wide, axis=1, keepdims=True)
            value = (a_norm + b_norm - 2.0 * dot(a, b, ((1,), (1,)))).reshape(4, 4, 16, 512)
            if h == 1:
                value = value + part[half]
            part[half] = value
            if h == 1 and half is not core:
                core_sums = [send_pieces(2, part.at[half, n], sib.at[n], sib_send.at[n], sib_recv.at[n], sibling)
                             for n in range(4)]

    for n in range(4):
        core_sums[n].wait()
        own[pl.ds(n * 4, 4)] = part[core, n] + sib[n]

    def at_plane(o):
        return device(x, y, lax.rem(z + o + 16, 16), core)

    for d in (8, 7, 6, 5):
        send(own.at[lax.rem(z + d, 16)], rs_up.at[d - 5], rs_send.at[0], rs_recv.at[0], at_plane(d - 4))
        if d < 8:
            send(own.at[lax.rem(z + 16 - d, 16)], rs_down.at[d - 5], rs_send.at[1], rs_recv.at[1], at_plane(4 - d))
    for d in (3, 2, 1):
        send(own.at[lax.rem(z + d, 16)], rs_near.at[d - 1], rs_send.at[2], rs_recv.at[2], at_plane(d))
        send(own.at[lax.rem(z + 16 - d, 16)], rs_near.at[d + 2], rs_send.at[2], rs_recv.at[2], at_plane(-d))
    remote(rs_up, rs_up, rs_send.at[0], rs_recv.at[0], sibling).wait_recv()
    rs_sum[0] = own[lax.rem(z + 4, 16)] + four(rs_up)
    last_up = send(rs_sum.at[0], rs_last.at[0], rs_send.at[3], rs_recv.at[3], at_plane(4))
    remote(rs_down, rs_down, rs_send.at[1], rs_recv.at[1], sibling).wait_recv()
    rs_sum[1] = own[lax.rem(z + 12, 16)] + (rs_down[0] + rs_down[1] + rs_down[2])
    last_down = send(rs_sum.at[1], rs_last.at[1], rs_send.at[4], rs_recv.at[4], at_plane(-4))
    remote(rs_near, rs_near, rs_send.at[2], rs_recv.at[2], sibling).wait()
    near = own[z] + ((rs_near[0] + rs_near[1]) + (rs_near[2] + rs_near[3]) + (rs_near[4] + rs_near[5]))
    last_up.wait()
    last_down.wait()
    total[...] = near + (rs_last[0] + rs_last[1])
    remote(rs_up, rs_up, rs_send.at[0], rs_recv.at[0], sibling).wait_send()
    remote(rs_down, rs_down, rs_send.at[1], rs_recv.at[1], sibling).wait_send()

    my_rows = pl.ds(pl.multiple_of(128 + z * 16, 16), 16)

    def gather(n, p):
        return (total, ext.at[my_rows, pl.ds(128, 512)], ag_send.at[n], ag_recv.at[0],
                device(x, y, p, core))

    def each_gather(do):
        for n in (2, 1, 3):
            do(gather(n, lax.rem(group + n, 4) * 4 + 1))

        @pl.when(jnp.logical_not(iterates))
        def _():
            do(gather(0, group * 4 + 1))

    each_gather(lambda copy: send_pieces(2, *copy))

    @pl.when(iterates)
    def _():
        ext[my_rows, 128:640] = total[...]
        view = ext.at[pl.ds(0, 240), pl.ds(128, 512)]
        remote(view, view, ag_send.at[0], ag_recv.at[0], sibling).wait_recv()

        x_next, y_next = lax.rem(x + core, 4), lax.rem(y + 1, 4)
        below, right, both = (
            device(x_next, y, z, 1 - core), device(x, y_next, z, core), device(x_next, y_next, z, 1 - core))
        bottom, inner, edge = pl.ds(256, 128), pl.ds(128, 512), pl.ds(512, 128)
        halo = [
            send_pieces(4, ext.at[bottom, inner], ext.at[pl.ds(0, 128), inner],
                        halo_send.at[0], halo_recv.at[0], below),
            send_pieces(2, ext.at[bottom, edge], ext.at[pl.ds(0, 128), pl.ds(0, 128)],
                        halo_send.at[2], halo_recv.at[2], both),
            send_pieces(4, ext.at[pl.ds(128, 256), edge], ext.at[pl.ds(128, 256), pl.ds(0, 128)],
                        halo_send.at[1], halo_recv.at[1], right),
        ]
        for copy in halo:
            copy.wait()
        rows = lax.broadcasted_iota(jnp.int32, (384, 640), 0)
        lanes = lax.broadcasted_iota(jnp.int32, (384, 640), 1)
        first_row = jnp.where(2 * x + core == 0, 128, 0)
        first_lane = jnp.where(y == 0, 128, 0)
        run = jnp.where((rows >= first_row) & (lanes >= first_lane), ext[...], 0.0)
        stride = LAGS // 2
        while stride >= 1:
            turned = pltpu.roll(run, stride, 1)
            if stride >= 8:
                run = run[stride:] + turned[:-stride]
            else:
                run = run + pltpu.roll(turned, stride, 0)
            stride //= 2
        lagged = run[8:, 128:]
        i = lax.broadcasted_iota(jnp.int32, (256, 512), 0) + (x * 512 + core * 256)
        j = lax.broadcasted_iota(jnp.int32, (256, 512), 1) + y * 512
        counts = (jnp.minimum(jnp.minimum(i, j), LAGS - 1) + 1).astype(F32)
        half_tile = jnp.exp(-(lagged / (counts * (PTS * 0.25))))
        half_hi, half_lo = parts(half_tile, 2)
        my_half = pl.ds(pl.multiple_of(core * 256, 256), 256)
        kern_hi[my_half, :] = half_hi
        kern_lo[my_half, :] = half_lo
        swaps = [remote(ref.at[my_half, :], ref.at[my_half, :], core_send.at[n], core_recv.at[n], sibling)
                 for n, ref in enumerate((kern_hi, kern_lo))]

        @pl.when(core == 1)
        def _():
            for n, ref in enumerate((kern_hi, kern_lo)):
                send_pieces(4, ref.at[my_half, :], ref.at[my_half, :], core_send.at[n], core_recv.at[n], sibling)

        ones = jnp.ones((16, 512), BF16)
        deg_row[core, y] = (dot(ones, half_hi, ((1,), (1,))) + dot(ones, half_lo, ((1,), (1,))))[:8]
        deg_col[core, x] = (dot(ones[:, :256], half_hi, ((1,), (0,)))
                            + dot(ones[:, :256], half_lo, ((1,), (0,))))[:8]

        def degree_copies(k):
            row_view, col_view = deg_row.at[core, y], deg_col.at[core, x]
            return (remote(row_view, row_view, deg_send.at[0, k], deg_recv.at[0, core, k], along_y(k, 0)),
                    remote(col_view, col_view, deg_send.at[1, k], deg_recv.at[1, core, k], along_x(k, 0)))

        @pl.when(core == 1)
        def _():
            for k in (2, 1, 3, 0):
                for copy in degree_copies(k):
                    copy.start()
            for copy in swaps:
                copy.wait_send()
            for k in range(4):
                for copy in degree_copies(k):
                    copy.wait_send()

    @pl.when(iterates & (core == 0))
    def _():
        def degree_copy(n, c, k):
            ref = (deg_row, deg_col)[n].at[c, 0]
            return remote(ref, ref, deg_send.at[n, k], deg_recv.at[n, c, k], sibling)

        for k in (2, 1, 3):
            for n, ref, target in ((0, deg_row.at[0, y], along_y(k)), (1, deg_col.at[0, x], along_x(k))):
                remote(ref, ref, deg_send.at[n, k], deg_recv.at[n, 0, k], target).start()
        wide[...] = jnp.zeros_like(wide)

        def gram_of(block):
            wide[0:32, :] = block
            return dot(block, wide[...], ((1,), (1,)), HIGH)

        for k in range(4):
            @pl.when(row != 4 * y + k)
            def _():
                remote(start_ref, start.at[k], st_send.at[2], st_recv.at[k], sibling).wait_recv()
        mine = [start[k].T for k in range(4)]
        basis = [jnp.concatenate(mine[:2], axis=1), jnp.concatenate(mine[2:], axis=1)]
        other_half = pl.ds(256, 256)
        for n, ref in enumerate((kern_hi, kern_lo)):
            remote(ref.at[other_half, :], ref.at[other_half, :], core_send.at[n], core_recv.at[n], sibling).wait_recv()
        for n in (0, 1):
            for k in (1, 2, 3):
                degree_copy(n, 0, k).wait()
            for k in range(4):
                degree_copy(n, 1, k).wait_recv()
        row_sums = jnp.concatenate([four(deg_row.at[0]), four(deg_row.at[1])], axis=1)[0:1]
        scale_row = 1.0 / jnp.sqrt(row_sums)
        scale_col = 1.0 / jnp.sqrt((four(deg_col.at[0]) + four(deg_col.at[1]))[0:1])
        scale_row = scale_row[:, :256], scale_row[:, 256:]
        scale_col = scale_col[:, :256], scale_col[:, 256:]

        def term(over_y, n, m, block):
            n, m = pl.ds(n * 256, 256), pl.ds(m * 256, 256)
            at, dims = ((m, n), ((1,), (1,))) if over_y else ((n, m), ((1,), (0,)))
            high = dot(jnp.concatenate(block, axis=0), kern_hi[at], dims)
            low = dot(jnp.concatenate(block[:2], axis=0), kern_lo[at], dims)
            return high[:32] + ((high[32:64] + low[:32]) + (high[64:] + low[32:]))

        def product_wait(step, n):
            three = income.at[step, n, pl.ds(0, 3)]
            return remote(three, three, step_send.at[step, n], step_recv.at[step, n], sibling)

        def arrived(step, n):
            product_wait(step, n).wait_recv()
            block = four(income.at[step, n])
            return dot(inverse, block, ((1,), (0,)), HIGH) if step in (3, 5) else block

        inverse = None
        gram_copies = None
        for step in range(6):
            over_y = step % 2 == 0
            at = y if over_y else x
            scale_in, scale_out = (scale_col, scale_row) if over_y else (scale_row, scale_col)
            sums = None
            for n in (0, 1):
                if step:
                    basis[n] = arrived(step - 1, n)
                block = parts(basis[n] * scale_in[n], 3)
                if n == 0:
                    sums = [term(over_y, 0, m, block) for m in (0, 1)]
                    continue
                for m in (0, 1):
                    income[step, m, at] = (sums[m] + term(over_y, 1, m, block)) * scale_out[m]
                    view = income.at[step, m, at]
                    for k in (2, 1, 3):
                        send(view, view, step_send.at[step, m], step_recv.at[step, m],
                             along_y(k) if over_y else along_x(k))
            if step:
                for m in (0, 1):
                    product_wait(step - 1, m).wait_send()
            if step in (2, 4):
                n = step // 2 - 1
                grams[n, y] = gram_of(jnp.concatenate(basis, axis=1))
                gram_copies = [send(grams.at[n, y], grams.at[n, y], gram_send.at[n, k],
                                    gram_recv.at[n, k], along_y(k)) for k in (2, 1, 3)]
            if step in (3, 5):
                for copy in gram_copies:
                    copy.wait()
                inverse = inverse_factor(four(grams.at[step // 2 - 1]))
        basis = jnp.concatenate([arrived(5, 0), arrived(5, 1)], axis=1)

        owner = lax.div(y, 2) == lax.rem(group, 2)

        def row_copy(k, i, c):
            return remote(last.at[:, pl.ds((i * 2 + c) * 128, 128)], last_rows, row_send.at[k, i, c],
                          row_recv.at[0], device(x, lax.rem(y + k, 4), z_hi * 8 + 2 * y + i, c))

        def each_row_copy(do):
            for k in (2, 1, 3, 0):
                for i in (0, 1):
                    for c in (0, 1):
                        if k or c:
                            do(row_copy(k, i, c))
                        else:
                            @pl.when(z_lo != 2 * y + i)
                            def _():
                                do(row_copy(k, i, c))

        gram = gram_of(basis)
        last_grams[y] = jnp.concatenate([gram[8 * n:8 * n + 8, :32] for n in range(4)], axis=1)
        waits = []
        for k in (2, 1, 3, 0):
            for i in (2, 1, 3, 0):
                for c in (0, 1):
                    if k or i or c:
                        target = device(x, lax.rem(y + k, 4), group * 4 + lax.rem(1 + i, 4), c)
                        waits.append(send(last_grams.at[y], last_grams.at[y], fin_send.at[k, i, c],
                                          fin_recv.at[y], target))

        last[...] = basis

        @pl.when(owner)
        def _():
            each_row_copy(lambda copy: copy.start())
            for i in (0, 1):
                @pl.when(z_lo == 2 * y + i)
                def _():
                    last_rows[...] = last[:, i * 256:i * 256 + 128]

        for m in (0, 1):
            product_wait(5, m).wait_send()
        for copy in waits:
            copy.wait_send()

        @pl.when(owner)
        def _():
            each_row_copy(lambda copy: copy.wait_send())

    for q in range(4):
        @pl.when(jnp.logical_not(iterates & (core == 0) & (y == q)))
        def _():
            remote(last_grams.at[q], last_grams.at[q], fin_send.at[0, 0, 0], fin_recv.at[q], sibling).wait_recv()
    packed = four(last_grams)
    packed = jnp.concatenate([packed[:, 32 * n:32 * n + 32] for n in range(4)], axis=0)
    inverse = inverse_factor(jnp.concatenate([packed, jnp.zeros((32, 96), F32)], axis=1))

    @pl.when(jnp.logical_not(iterates & (core == 0) & (y == lax.div(z_lo, 2))))
    def _():
        remote(last_rows, last_rows, row_send.at[0, 0, 0], row_recv.at[0], sibling).wait_recv()

    out_ref[...] = dot(inverse, last_rows[...], ((1,), (0,)), HIGH) * math.sqrt(SNAPS)

    for n, t in enumerate((2, 10)):
        @pl.when(giver & (row != t))
        def _():
            basis_copy(n, t).wait_send()
    each_gather(lambda copy: remote(*copy).wait_send())


VMEM = pl.BlockSpec(memory_space=pltpu.VMEM)
ANY = pl.BlockSpec(memory_space=pl.ANY)
DMA = pltpu.SemaphoreType.DMA


def body(snapshots, start_block):
    out = pl.pallas_call(
        kernel,
        out_shape=jax.ShapeDtypeStruct((32, 128), F32),
        in_specs=[ANY, ANY],
        out_specs=VMEM,
        scratch_shapes=[
            pltpu.VMEM((2, 4, 8, 16, 128), BF16),
            pltpu.VMEM((2, 4, 8, 4, 16, 128), BF16),
            pltpu.VMEM((2, 4, 8, 4, 16, 128), BF16),
            pltpu.VMEM((2, 4, 4, 16, 512), F32),
            pltpu.VMEM((4, 4, 16, 512), F32),
            pltpu.VMEM((16, 16, 512), F32),
            pltpu.VMEM((4, 16, 512), F32),
            pltpu.VMEM((3, 16, 512), F32),
            pltpu.VMEM((6, 16, 512), F32),
            pltpu.VMEM((2, 16, 512), F32),
            pltpu.VMEM((2, 16, 512), F32),
            pltpu.VMEM((16, 512), F32),
            pltpu.VMEM((4, 128, 32), F32),
            pltpu.VMEM((384, 640), F32),
            pltpu.VMEM((512, 512), BF16),
            pltpu.VMEM((512, 512), BF16),
            pltpu.VMEM((2, 4, 8, 256), F32),
            pltpu.VMEM((2, 4, 8, 512), F32),
            pltpu.VMEM((128, 512), F32),
            pltpu.VMEM((6, 2, 4, 32, 256), F32),
            pltpu.VMEM((2, 4, 32, 128), F32),
            pltpu.VMEM((32, 512), F32),
            pltpu.VMEM((32, 128), F32),
            pltpu.VMEM((4, 8, 128), F32),
            DMA((1,)), DMA((2,)), DMA((2,)), DMA((2, 2, 4)), DMA((2, 2, 4)), DMA((2, 2, 4)), DMA((2, 2, 4)),
            DMA((4,)), DMA((4,)), DMA((5,)), DMA((5,)), DMA((4,)), DMA((1,)), DMA((3,)), DMA((4,)),
            DMA((3,)), DMA((3,)), DMA((2,)), DMA((2,)), DMA((2, 4)), DMA((2, 2, 4)),
            DMA((6, 2)), DMA((6, 2)), DMA((2, 4)), DMA((2, 4)), DMA((4, 4, 2)), DMA((4,)),
            DMA((4, 2, 2)), DMA((1,)),
        ],
        compiler_params=pltpu.CompilerParams(
            collective_id=1, has_side_effects=True, vmem_limit_bytes=48 << 20),
        name="subspace",
    )(snapshots, start_block)
    return out.T


def solution(mesh):
    placed = (P(("row", "col"), "feat"), P("row", None))
    return jax.shard_map(
        body, mesh=mesh, in_specs=placed, out_specs=P("row", None), check_vma=False
    )
```

```python
import math

import jax
import jax.numpy as jnp
from jax import lax
from jax.experimental import pallas as pl
from jax.experimental.pallas import tpu as pltpu
from jax.sharding import PartitionSpec as P

PTS = 32768
LAGS = 128
SNAPS = 2048
MESH = pl.DeviceIdType.MESH
HIGH = lax.Precision.HIGHEST
F32 = jnp.float32
BF16 = jnp.bfloat16


def device(x, y, z, core):
    return (lax.rem(z, 8) * 2 + core, lax.div(z, 8) * 4 + x, y)


def remote(src, dst, send_sem, recv_sem, target):
    return pltpu.make_async_remote_copy(
        src_ref=src, dst_ref=dst, send_sem=send_sem, recv_sem=recv_sem,
        device_id=target, device_id_type=MESH,
    )


def send(*args):
    copy = remote(*args)
    copy.start()
    return copy


def send_pieces(count, src, dst, send_sem, recv_sem, target):
    rows = src.shape[0] // count
    for n in range(count):
        piece = pl.ds(n * rows, rows)
        send(src.at[piece], dst.at[piece], send_sem, recv_sem, target)
    return remote(src, dst, send_sem, recv_sem, target)


def dot(a, b, dims, precision=None):
    return lax.dot_general(
        a, b, (dims, ((), ())), precision=precision, preferred_element_type=F32
    )


def parts(value, count):
    out = []
    for _ in range(count):
        out.append(value.astype(BF16))
        value = value - out[-1].astype(F32)
    return out


def inverse_factor(gram):
    rows = lax.broadcasted_iota(jnp.int32, (32, 128), 0)
    lanes = lax.broadcasted_iota(jnp.int32, (32, 128), 1)
    work = jnp.where(lanes < 32, gram, jnp.where(lanes - 32 == rows, 1.0, 0.0))
    for k in range(0, 32, 16):
        tops = [work[k + n:k + n + 1, :] for n in range(16)]
        columns = [jnp.broadcast_to(work[:, k + n:k + n + 1], (32, 128)) for n in range(16)]
        for n in range(16):
            at = k + n
            ratio = columns[n] * (1.0 / columns[n][at:at + 1, :])
            for m in range(n + 1, 16):
                tops[m] = tops[m] - ratio[k + m:k + m + 1, :] * tops[n]
                columns[m] = columns[m] - ratio * columns[m][at:at + 1, :]
            work = work - jnp.where(rows > at, ratio, 0.0) * tops[n]
    diagonal = jnp.sum(jnp.where(lanes == rows, work, 0.0), axis=1, keepdims=True)
    return work[:, 32:64] / jnp.sqrt(diagonal)


def four(ref):
    return (ref[0] + ref[1]) + (ref[2] + ref[3])


def kernel(
    x_ref, start_ref, out_ref,
    zbuf, abuf, bbuf, part, sib, own, rs_up, rs_down, rs_near, rs_sum, rs_last, total, start,
    ext, kern_hi, kern_lo, deg_row, deg_col, wide, income, grams, last, last_rows, last_grams,
    local_sem, z_send, z_recv, plane_send, plane_recv, gather_send, gather_recv,
    sib_send, sib_recv, rs_send, rs_recv, ag_send, ag_recv, st_send, st_recv,
    halo_send, halo_recv, core_send, core_recv, deg_send, deg_recv,
    step_send, step_recv, gram_send, gram_recv, fin_send, fin_recv, row_send, row_recv,
):
    row, col, y = lax.axis_index("row"), lax.axis_index("col"), lax.axis_index("feat")
    x, z_hi = lax.rem(col, 4), lax.div(col, 4)
    core, z_lo = lax.rem(row, 2), lax.div(row, 2)
    z = z_hi * 8 + z_lo
    me = z * 2 + core
    group = lax.div(z, 4)
    iterates = lax.rem(z, 4) == 1

    def line(t):
        return device(x, y, lax.div(t, 2), lax.rem(t, 2))

    def along_x(k, c=core):
        return device(lax.rem(x + k, 4), y, z, c)

    def along_y(k, c=core):
        return device(x, lax.rem(y + k, 4), z, c)

    sibling = device(x, y, z, 1 - core)
    barrier = pltpu.get_barrier_semaphore()
    far_first = sorted(range(1, 32), key=lambda o: -min(o, 32 - o))
    partners = ([line(lax.rem(me + o, 32)) for o in far_first]
                + [along_x(k) for k in (1, 2, 3)] + [along_y(k) for k in (1, 2, 3)])
    for target in partners:
        pl.semaphore_signal(barrier, inc=1, device_id=target, device_id_type=MESH)
    pl.semaphore_wait(barrier, len(partners))

    def columns(t, h):
        return pl.ds(pl.multiple_of(t * 256 + h * 128, 128), 128)

    big, small = lax.div(z_lo, 2), lax.rem(z_lo, 2) * 4 + core * 2 + z_hi
    def half_wait(h):
        sent = x_ref.at[:, pl.ds(0, 31 * 128)]
        return (remote(sent, sent, z_send.at[h], z_recv.at[h], sibling),
                remote(zbuf.at[h], zbuf.at[h], z_send.at[h], z_recv.at[h], sibling))

    for h in (0, 1):
        if h:
            half_wait(0)[0].wait_send()
        for o in far_first:
            t = lax.rem(me + o, 32)
            send(x_ref.at[:, columns(t, h)], zbuf.at[h, big, small], z_send.at[h], z_recv.at[h], line(t))
        pltpu.make_async_copy(x_ref.at[:, columns(me, h)], zbuf.at[h, big, small], z_recv.at[h]).start()

    giver = lax.div(row, 4) == y
    basis_slot = lax.rem(row, 4)

    def basis_copy(n, t):
        return remote(start_ref, start.at[basis_slot], st_send.at[n], st_recv.at[basis_slot],
                      (t, col, y))

    for n, t in enumerate((2, 10)):
        @pl.when(giver & (row != t))
        def _():
            basis_copy(n, t).start()

    @pl.when(giver)
    def _():
        copy = pltpu.make_async_copy(start_ref, start.at[basis_slot], local_sem.at[0])
        copy.start()
        copy.wait()

    def three(ref, h, sems, n):
        view = ref.at[h, pl.ds(0, 3)]
        return remote(view, view, sems[0].at[h, n], sems[1].at[h, n], sibling)

    plane, gathered = (plane_send, plane_recv), (gather_send, gather_recv)
    for h in (0, 1):
        half_wait(h)[1].wait_recv()
        for k in (2, 1, 3):
            send(zbuf.at[h, lax.rem(x + k, 4)], abuf.at[h, y, :, x],
                 plane_send.at[h, 0], plane_recv.at[h, 0], along_x(k))
            send(zbuf.at[h, lax.rem(y + k, 4)], bbuf.at[h, y, :, x],
                 plane_send.at[h, 1], plane_recv.at[h, 1], along_y(k))
        abuf[h, y, :, x] = zbuf[h, x]
        bbuf[h, y, :, x] = zbuf[h, y]
    half_wait(1)[0].wait_send()
    for h in (0, 1):
        three(zbuf, h, plane, 0).wait_recv()
        for k in (2, 1, 3):
            send_pieces(4, abuf.at[h, y], abuf.at[h, y], gather_send.at[h, 0], gather_recv.at[h, 0], along_y(k))
        three(zbuf, h, plane, 1).wait_recv()
        for k in (2, 1, 3):
            send_pieces(4, bbuf.at[h, :, :, x], bbuf.at[h, :, :, x],
                        gather_send.at[h, 1], gather_recv.at[h, 1], along_x(k))
    for h in (0, 1):
        for n in (0, 1):
            three(zbuf, h, plane, n).wait_send()

    for h in (0, 1):
        three(abuf, h, gathered, 0).wait()
        three(bbuf, h, gathered, 1).wait()
        b = jnp.concatenate([bbuf[h, q].reshape(512, 128) for q in range(4)], axis=1)
        b_wide = b.astype(F32)
        ones = jnp.ones((16, 512), BF16)
        b_norm = sum(dot(ones, p, ((1,), (1,))) for p in parts(b_wide * b_wide, 2))[0:1]
        for half in (1 - core, core):
            a = jnp.concatenate(
                [abuf[h, q, pl.ds(half * 4, 4)].reshape(256, 128) for q in range(4)], axis=1)
            a_wide = a.astype(F32)
            a_norm = jnp.sum(a_wide * a_wide, axis=1, keepdims=True)
            value = (a_norm + b_norm - 2.0 * dot(a, b, ((1,), (1,)))).reshape(4, 4, 16, 512)
            if h == 1:
                value = value + part[half]
            part[half] = value
            if h == 1 and half is not core:
                core_sums = [send_pieces(2, part.at[half, n], sib.at[n], sib_send.at[n], sib_recv.at[n], sibling)
                             for n in range(4)]

    for n in range(4):
        core_sums[n].wait()
        own[pl.ds(n * 4, 4)] = part[core, n] + sib[n]

    def at_plane(o):
        return device(x, y, lax.rem(z + o + 16, 16), core)

    for d in (8, 7, 6, 5):
        send(own.at[lax.rem(z + d, 16)], rs_up.at[d - 5], rs_send.at[0], rs_recv.at[0], at_plane(d - 4))
        if d < 8:
            send(own.at[lax.rem(z + 16 - d, 16)], rs_down.at[d - 5], rs_send.at[1], rs_recv.at[1], at_plane(4 - d))
    for d in (3, 2, 1):
        send(own.at[lax.rem(z + d, 16)], rs_near.at[d - 1], rs_send.at[2], rs_recv.at[2], at_plane(d))
        send(own.at[lax.rem(z + 16 - d, 16)], rs_near.at[d + 2], rs_send.at[2], rs_recv.at[2], at_plane(-d))
    remote(rs_up, rs_up, rs_send.at[0], rs_recv.at[0], sibling).wait_recv()
    rs_sum[0] = own[lax.rem(z + 4, 16)] + four(rs_up)
    last_up = send(rs_sum.at[0], rs_last.at[0], rs_send.at[3], rs_recv.at[3], at_plane(4))
    remote(rs_down, rs_down, rs_send.at[1], rs_recv.at[1], sibling).wait_recv()
    rs_sum[1] = own[lax.rem(z + 12, 16)] + (rs_down[0] + rs_down[1] + rs_down[2])
    last_down = send(rs_sum.at[1], rs_last.at[1], rs_send.at[4], rs_recv.at[4], at_plane(-4))
    remote(rs_near, rs_near, rs_send.at[2], rs_recv.at[2], sibling).wait()
    near = own[z] + ((rs_near[0] + rs_near[1]) + (rs_near[2] + rs_near[3]) + (rs_near[4] + rs_near[5]))
    last_up.wait()
    last_down.wait()
    total[...] = near + (rs_last[0] + rs_last[1])
    remote(rs_up, rs_up, rs_send.at[0], rs_recv.at[0], sibling).wait_send()
    remote(rs_down, rs_down, rs_send.at[1], rs_recv.at[1], sibling).wait_send()

    my_rows = pl.ds(pl.multiple_of(128 + z * 16, 16), 16)

    def gather(n, p):
        return (total, ext.at[my_rows, pl.ds(128, 512)], ag_send.at[n], ag_recv.at[0],
                device(x, y, p, core))

    def each_gather(do):
        for n in (2, 1, 3):
            do(gather(n, lax.rem(group + n, 4) * 4 + 1))

        @pl.when(jnp.logical_not(iterates))
        def _():
            do(gather(0, group * 4 + 1))

    each_gather(lambda copy: send_pieces(2, *copy))

    @pl.when(iterates)
    def _():
        ext[my_rows, 128:640] = total[...]
        view = ext.at[pl.ds(0, 240), pl.ds(128, 512)]
        remote(view, view, ag_send.at[0], ag_recv.at[0], sibling).wait_recv()

        x_next, y_next = lax.rem(x + core, 4), lax.rem(y + 1, 4)
        below, right, both = (
            device(x_next, y, z, 1 - core), device(x, y_next, z, core), device(x_next, y_next, z, 1 - core))
        bottom, inner, edge = pl.ds(256, 128), pl.ds(128, 512), pl.ds(512, 128)
        halo = [
            send_pieces(4, ext.at[bottom, inner], ext.at[pl.ds(0, 128), inner],
                        halo_send.at[0], halo_recv.at[0], below),
            send_pieces(2, ext.at[bottom, edge], ext.at[pl.ds(0, 128), pl.ds(0, 128)],
                        halo_send.at[2], halo_recv.at[2], both),
            send_pieces(4, ext.at[pl.ds(128, 256), edge], ext.at[pl.ds(128, 256), pl.ds(0, 128)],
                        halo_send.at[1], halo_recv.at[1], right),
        ]
        for copy in halo:
            copy.wait()
        rows = lax.broadcasted_iota(jnp.int32, (384, 640), 0)
        lanes = lax.broadcasted_iota(jnp.int32, (384, 640), 1)
        first_row = jnp.where(2 * x + core == 0, 128, 0)
        first_lane = jnp.where(y == 0, 128, 0)
        run = jnp.where((rows >= first_row) & (lanes >= first_lane), ext[...], 0.0)
        stride = LAGS // 2
        while stride >= 1:
            turned = pltpu.roll(run, stride, 1)
            if stride >= 8:
                run = run[stride:] + turned[:-stride]
            else:
                run = run + pltpu.roll(turned, stride, 0)
            stride //= 2
        lagged = run[8:, 128:]
        i = lax.broadcasted_iota(jnp.int32, (256, 512), 0) + (x * 512 + core * 256)
        j = lax.broadcasted_iota(jnp.int32, (256, 512), 1) + y * 512
        counts = (jnp.minimum(jnp.minimum(i, j), LAGS - 1) + 1).astype(F32)
        half_tile = jnp.exp(-(lagged / (counts * (PTS * 0.25))))
        half_hi, half_lo = parts(half_tile, 2)
        my_half = pl.ds(pl.multiple_of(core * 256, 256), 256)
        kern_hi[my_half, :] = half_hi
        kern_lo[my_half, :] = half_lo
        swaps = [remote(ref.at[my_half, :], ref.at[my_half, :], core_send.at[n], core_recv.at[n], sibling)
                 for n, ref in enumerate((kern_hi, kern_lo))]

        @pl.when(core == 1)
        def _():
            for n, ref in enumerate((kern_hi, kern_lo)):
                send_pieces(4, ref.at[my_half, :], ref.at[my_half, :], core_send.at[n], core_recv.at[n], sibling)

        ones = jnp.ones((16, 512), BF16)
        deg_row[core * 4 + y] = (dot(ones, half_hi, ((1,), (1,))) + dot(ones, half_lo, ((1,), (1,))))[:8]
        deg_col[core * 4 + x] = (dot(ones[:, :256], half_hi, ((1,), (0,)))
                            + dot(ones[:, :256], half_lo, ((1,), (0,))))[:8]

        def degree_copies(k):
            row_view, col_view = deg_row.at[core * 4 + y], deg_col.at[core * 4 + x]
            return (remote(row_view, row_view, deg_send.at[0], deg_recv.at[0], along_y(k, 0)),
                    remote(col_view, col_view, deg_send.at[1], deg_recv.at[1], along_x(k, 0)))

        @pl.when(core == 1)
        def _():
            for k in (2, 1, 3, 0):
                for copy in degree_copies(k):
                    copy.start()
            for copy in swaps:
                copy.wait_send()
            for n, ref in enumerate((deg_row, deg_col)):
                view = ref.at[pl.ds(0, 4)]
                remote(view, view, deg_send.at[n], deg_recv.at[n], sibling).wait_send()

    @pl.when(iterates & (core == 0))
    def _():
        for k in (2, 1, 3):
            for n, ref, target in ((0, deg_row.at[y], along_y(k)), (1, deg_col.at[x], along_x(k))):
                send(ref, ref, deg_send.at[n], deg_recv.at[n], target)
        wide[...] = jnp.zeros_like(wide)

        def gram_of(block):
            wide[0:32, :] = block
            return dot(block, wide[...], ((1,), (1,)), HIGH)

        for k in range(4):
            @pl.when(row != 4 * y + k)
            def _():
                remote(start_ref, start.at[k], st_send.at[2], st_recv.at[k], sibling).wait_recv()
        mine = [start[k].T for k in range(4)]
        basis = [jnp.concatenate(mine[:2], axis=1), jnp.concatenate(mine[2:], axis=1)]
        other_half = pl.ds(256, 256)
        for n, ref in enumerate((kern_hi, kern_lo)):
            remote(ref.at[other_half, :], ref.at[other_half, :], core_send.at[n], core_recv.at[n], sibling).wait_recv()
        for n, ref in enumerate((deg_row, deg_col)):
            sent, arriving = ref.at[pl.ds(0, 3)], ref.at[pl.ds(0, 7)]
            remote(arriving, arriving, deg_send.at[n], deg_recv.at[n], sibling).wait_recv()
            remote(sent, sent, deg_send.at[n], deg_recv.at[n], sibling).wait_send()
        low_half, high_half = pl.ds(0, 4), pl.ds(4, 4)
        row_sums = jnp.concatenate([four(deg_row.at[low_half]), four(deg_row.at[high_half])], axis=1)[0:1]
        scale_row = 1.0 / jnp.sqrt(row_sums)
        scale_col = 1.0 / jnp.sqrt((four(deg_col.at[low_half]) + four(deg_col.at[high_half]))[0:1])
        scale_row = scale_row[:, :256], scale_row[:, 256:]
        scale_col = scale_col[:, :256], scale_col[:, 256:]

        def term(over_y, n, m, block):
            n, m = pl.ds(n * 256, 256), pl.ds(m * 256, 256)
            at, dims = ((m, n), ((1,), (1,))) if over_y else ((n, m), ((1,), (0,)))
            high = dot(jnp.concatenate(block, axis=0), kern_hi[at], dims)
            low = dot(jnp.concatenate(block[:2], axis=0), kern_lo[at], dims)
            return high[:32] + ((high[32:64] + low[:32]) + (high[64:] + low[32:]))

        def product_wait(step, n):
            three = income.at[step, n, pl.ds(0, 3)]
            return remote(three, three, step_send.at[step, n], step_recv.at[step, n], sibling)

        def arrived(step, n):
            product_wait(step, n).wait_recv()
            block = four(income.at[step, n])
            return dot(inverse, block, ((1,), (0,)), HIGH) if step in (3, 5) else block

        inverse = None
        gram_copies = None
        for step in range(6):
            over_y = step % 2 == 0
            at = y if over_y else x
            scale_in, scale_out = (scale_col, scale_row) if over_y else (scale_row, scale_col)
            sums = None
            for n in (0, 1):
                if step:
                    basis[n] = arrived(step - 1, n)
                block = parts(basis[n] * scale_in[n], 3)
                if n == 0:
                    sums = [term(over_y, 0, m, block) for m in (0, 1)]
                    continue
                for m in (0, 1):
                    income[step, m, at] = (sums[m] + term(over_y, 1, m, block)) * scale_out[m]
                    view = income.at[step, m, at]
                    for k in (2, 1, 3):
                        send(view, view, step_send.at[step, m], step_recv.at[step, m],
                             along_y(k) if over_y else along_x(k))
            if step:
                for m in (0, 1):
                    product_wait(step - 1, m).wait_send()
            if step in (2, 4):
                n = step // 2 - 1
                grams[n, y] = gram_of(jnp.concatenate(basis, axis=1))
                gram_copies = [send(grams.at[n, y], grams.at[n, y], gram_send.at[n, k],
                                    gram_recv.at[n, k], along_y(k)) for k in (2, 1, 3)]
            if step in (3, 5):
                for copy in gram_copies:
                    copy.wait()
                inverse = inverse_factor(four(grams.at[step // 2 - 1]))
        basis = jnp.concatenate([arrived(5, 0), arrived(5, 1)], axis=1)

        owner = lax.div(y, 2) == lax.rem(group, 2)

        def row_copy(k, i, c):
            return remote(last.at[:, pl.ds((i * 2 + c) * 128, 128)], last_rows, row_send.at[k, i, c],
                          row_recv.at[0], device(x, lax.rem(y + k, 4), z_hi * 8 + 2 * y + i, c))

        def each_row_copy(do):
            for k in (2, 1, 3, 0):
                for i in (0, 1):
                    for c in (0, 1):
                        if k or c:
                            do(row_copy(k, i, c))
                        else:
                            @pl.when(z_lo != 2 * y + i)
                            def _():
                                do(row_copy(k, i, c))

        gram = gram_of(basis)
        last_grams[y] = jnp.concatenate([gram[8 * n:8 * n + 8, :32] for n in range(4)], axis=1)
        waits = []
        for k in (2, 1, 3, 0):
            for i in (2, 1, 3, 0):
                for c in (0, 1):
                    if k or i or c:
                        target = device(x, lax.rem(y + k, 4), group * 4 + lax.rem(1 + i, 4), c)
                        waits.append(send(last_grams.at[y], last_grams.at[y], fin_send.at[k, i, c],
                                          fin_recv.at[y], target))

        last[...] = basis

        @pl.when(owner)
        def _():
            each_row_copy(lambda copy: copy.start())
            for i in (0, 1):
                @pl.when(z_lo == 2 * y + i)
                def _():
                    last_rows[...] = last[:, i * 256:i * 256 + 128]

        for m in (0, 1):
            product_wait(5, m).wait_send()
        for copy in waits:
            copy.wait_send()

        @pl.when(owner)
        def _():
            each_row_copy(lambda copy: copy.wait_send())

    for q in range(4):
        @pl.when(jnp.logical_not(iterates & (core == 0) & (y == q)))
        def _():
            remote(last_grams.at[q], last_grams.at[q], fin_send.at[0, 0, 0], fin_recv.at[q], sibling).wait_recv()
    packed = four(last_grams)
    packed = jnp.concatenate([packed[:, 32 * n:32 * n + 32] for n in range(4)], axis=0)
    inverse = inverse_factor(jnp.concatenate([packed, jnp.zeros((32, 96), F32)], axis=1))

    @pl.when(jnp.logical_not(iterates & (core == 0) & (y == lax.div(z_lo, 2))))
    def _():
        remote(last_rows, last_rows, row_send.at[0, 0, 0], row_recv.at[0], sibling).wait_recv()

    out_ref[...] = dot(inverse, last_rows[...], ((1,), (0,)), HIGH) * math.sqrt(SNAPS)

    for n, t in enumerate((2, 10)):
        @pl.when(giver & (row != t))
        def _():
            basis_copy(n, t).wait_send()
    each_gather(lambda copy: remote(*copy).wait_send())


VMEM = pl.BlockSpec(memory_space=pltpu.VMEM)
ANY = pl.BlockSpec(memory_space=pl.ANY)
DMA = pltpu.SemaphoreType.DMA


def body(snapshots, start_block):
    out = pl.pallas_call(
        kernel,
        out_shape=jax.ShapeDtypeStruct((32, 128), F32),
        in_specs=[ANY, ANY],
        out_specs=VMEM,
        scratch_shapes=[
            pltpu.VMEM((2, 4, 8, 16, 128), BF16),
            pltpu.VMEM((2, 4, 8, 4, 16, 128), BF16),
            pltpu.VMEM((2, 4, 8, 4, 16, 128), BF16),
            pltpu.VMEM((2, 4, 4, 16, 512), F32),
            pltpu.VMEM((4, 4, 16, 512), F32),
            pltpu.VMEM((16, 16, 512), F32),
            pltpu.VMEM((4, 16, 512), F32),
            pltpu.VMEM((3, 16, 512), F32),
            pltpu.VMEM((6, 16, 512), F32),
            pltpu.VMEM((2, 16, 512), F32),
            pltpu.VMEM((2, 16, 512), F32),
            pltpu.VMEM((16, 512), F32),
            pltpu.VMEM((4, 128, 32), F32),
            pltpu.VMEM((384, 640), F32),
            pltpu.VMEM((512, 512), BF16),
            pltpu.VMEM((512, 512), BF16),
            pltpu.VMEM((8, 8, 256), F32),
            pltpu.VMEM((8, 8, 512), F32),
            pltpu.VMEM((128, 512), F32),
            pltpu.VMEM((6, 2, 4, 32, 256), F32),
            pltpu.VMEM((2, 4, 32, 128), F32),
            pltpu.VMEM((32, 512), F32),
            pltpu.VMEM((32, 128), F32),
            pltpu.VMEM((4, 8, 128), F32),
            DMA((1,)), DMA((2,)), DMA((2,)), DMA((2, 2)), DMA((2, 2)), DMA((2, 2)), DMA((2, 2)),
            DMA((4,)), DMA((4,)), DMA((5,)), DMA((5,)), DMA((4,)), DMA((1,)), DMA((3,)), DMA((4,)),
            DMA((3,)), DMA((3,)), DMA((2,)), DMA((2,)), DMA((2,)), DMA((2,)),
            DMA((6, 2)), DMA((6, 2)), DMA((2, 4)), DMA((2, 4)), DMA((4, 4, 2)), DMA((4,)),
            DMA((4, 2, 2)), DMA((1,)),
        ],
        compiler_params=pltpu.CompilerParams(
            collective_id=1, has_side_effects=True, vmem_limit_bytes=48 << 20),
        name="subspace",
    )(snapshots, start_block)
    return out.T


def solution(mesh):
    placed = (P(("row", "col"), "feat"), P("row", None))
    return jax.shard_map(
        body, mesh=mesh, in_specs=placed, out_specs=P("row", None), check_vma=False
    )
```

```python
import math

import jax
import jax.numpy as jnp
from jax import lax
from jax.experimental import pallas as pl
from jax.experimental.pallas import tpu as pltpu
from jax.sharding import PartitionSpec as P

PTS = 32768
LAGS = 128
SNAPS = 2048
MESH = pl.DeviceIdType.MESH
HIGH = lax.Precision.HIGHEST
F32 = jnp.float32
BF16 = jnp.bfloat16


def device(x, y, z, core):
    return (lax.rem(z, 8) * 2 + core, lax.div(z, 8) * 4 + x, y)


def remote(src, dst, send_sem, recv_sem, target):
    return pltpu.make_async_remote_copy(
        src_ref=src, dst_ref=dst, send_sem=send_sem, recv_sem=recv_sem,
        device_id=target, device_id_type=MESH,
    )


def send(*args):
    copy = remote(*args)
    copy.start()
    return copy


def send_pieces(count, src, dst, send_sem, recv_sem, target):
    rows = src.shape[0] // count
    for n in range(count):
        piece = pl.ds(n * rows, rows)
        send(src.at[piece], dst.at[piece], send_sem, recv_sem, target)
    return remote(src, dst, send_sem, recv_sem, target)


def dot(a, b, dims, precision=None):
    return lax.dot_general(
        a, b, (dims, ((), ())), precision=precision, preferred_element_type=F32
    )


def parts(value, count):
    out = []
    for _ in range(count):
        out.append(value.astype(BF16))
        value = value - out[-1].astype(F32)
    return out


def inverse_factor(gram):
    rows = lax.broadcasted_iota(jnp.int32, (32, 128), 0)
    lanes = lax.broadcasted_iota(jnp.int32, (32, 128), 1)
    work = jnp.where(lanes < 32, gram, jnp.where(lanes - 32 == rows, 1.0, 0.0))
    for k in range(0, 32, 16):
        tops = [work[k + n:k + n + 1, :] for n in range(16)]
        columns = [jnp.broadcast_to(work[:, k + n:k + n + 1], (32, 128)) for n in range(16)]
        for n in range(16):
            at = k + n
            ratio = columns[n] * (1.0 / columns[n][at:at + 1, :])
            for m in range(n + 1, 16):
                tops[m] = tops[m] - ratio[k + m:k + m + 1, :] * tops[n]
                columns[m] = columns[m] - ratio * columns[m][at:at + 1, :]
            work = work - jnp.where(rows > at, ratio, 0.0) * tops[n]
    diagonal = jnp.sum(jnp.where(lanes == rows, work, 0.0), axis=1, keepdims=True)
    return work[:, 32:64] / jnp.sqrt(diagonal)


def four(ref):
    return (ref[0] + ref[1]) + (ref[2] + ref[3])


def kernel(
    x_ref, start_ref, out_ref,
    zbuf, abuf, bbuf, part, sib, own, rs_up, rs_down, rs_near, rs_sum, rs_last, total, start,
    ext, kern_hi, kern_lo, deg_row, deg_col, wide, income, grams, last, last_rows, last_grams,
    local_sem, z_send, z_recv, plane_send, plane_recv, gather_send, gather_recv,
    sib_send, sib_recv, rs_send, rs_recv, ag_send, ag_recv, st_send, st_recv,
    halo_send, halo_recv, core_send, core_recv, deg_send, deg_recv,
    step_send, step_recv, gram_send, gram_recv, fin_send, fin_recv, row_send, row_recv,
):
    row, col, y = lax.axis_index("row"), lax.axis_index("col"), lax.axis_index("feat")
    x, z_hi = lax.rem(col, 4), lax.div(col, 4)
    core, z_lo = lax.rem(row, 2), lax.div(row, 2)
    z = z_hi * 8 + z_lo
    me = z * 2 + core
    group = lax.div(z, 4)
    iterates = lax.rem(z, 4) == 1

    def line(t):
        return device(x, y, lax.div(t, 2), lax.rem(t, 2))

    def along_x(k, c=core):
        return device(lax.rem(x + k, 4), y, z, c)

    def along_y(k, c=core):
        return device(x, lax.rem(y + k, 4), z, c)

    sibling = device(x, y, z, 1 - core)
    barrier = pltpu.get_barrier_semaphore()
    far_first = sorted(range(1, 32), key=lambda o: -min(o, 32 - o))
    partners = ([line(lax.rem(me + o, 32)) for o in far_first]
                + [along_x(k) for k in (1, 2, 3)] + [along_y(k) for k in (1, 2, 3)])
    for target in partners:
        pl.semaphore_signal(barrier, inc=1, device_id=target, device_id_type=MESH)
    pl.semaphore_wait(barrier, len(partners))

    def columns(t, h):
        return pl.ds(pl.multiple_of(t * 256 + h * 128, 128), 128)

    big, small = lax.div(z_lo, 2), lax.rem(z_lo, 2) * 4 + core * 2 + z_hi
    def half_wait(h):
        sent = x_ref.at[:, pl.ds(0, 31 * 128)]
        return (remote(sent, sent, z_send.at[h], z_recv.at[h], sibling),
                remote(zbuf.at[h], zbuf.at[h], z_send.at[h], z_recv.at[h], sibling))

    for h in (0, 1):
        if h:
            half_wait(0)[0].wait_send()
        for o in far_first:
            t = lax.rem(me + o, 32)
            send(x_ref.at[:, columns(t, h)], zbuf.at[h, big, small], z_send.at[h], z_recv.at[h], line(t))
        pltpu.make_async_copy(x_ref.at[:, columns(me, h)], zbuf.at[h, big, small], z_recv.at[h]).start()

    giver = lax.div(row, 4) == y
    basis_slot = lax.rem(row, 4)

    def basis_copy(n, t):
        return remote(start_ref, start.at[basis_slot], st_send.at[n], st_recv.at[basis_slot],
                      (t, col, y))

    for n, t in enumerate((2, 10)):
        @pl.when(giver & (row != t))
        def _():
            basis_copy(n, t).start()

    @pl.when(giver)
    def _():
        copy = pltpu.make_async_copy(start_ref, start.at[basis_slot], local_sem.at[0])
        copy.start()
        copy.wait()

    def three(ref, h, sems, n):
        view = ref.at[h, pl.ds(0, 3)]
        return remote(view, view, sems[0].at[h, n], sems[1].at[h, n], sibling)

    plane, gathered = (plane_send, plane_recv), (gather_send, gather_recv)
    for h in (0, 1):
        half_wait(h)[1].wait_recv()
        for k in (2, 1, 3):
            send(zbuf.at[h, lax.rem(x + k, 4)], abuf.at[h, y, :, x],
                 plane_send.at[h, 0], plane_recv.at[h, 0], along_x(k))
            send(zbuf.at[h, lax.rem(y + k, 4)], bbuf.at[h, y, :, x],
                 plane_send.at[h, 1], plane_recv.at[h, 1], along_y(k))
        abuf[h, y, :, x] = zbuf[h, x]
        bbuf[h, y, :, x] = zbuf[h, y]
    half_wait(1)[0].wait_send()
    for h in (0, 1):
        three(zbuf, h, plane, 0).wait_recv()
        for k in (2, 1, 3):
            send_pieces(4, abuf.at[h, y], abuf.at[h, y], gather_send.at[h, 0], gather_recv.at[h, 0], along_y(k))
        three(zbuf, h, plane, 1).wait_recv()
        for k in (2, 1, 3):
            send_pieces(4, bbuf.at[h, :, :, x], bbuf.at[h, :, :, x],
                        gather_send.at[h, 1], gather_recv.at[h, 1], along_x(k))
    for h in (0, 1):
        for n in (0, 1):
            three(zbuf, h, plane, n).wait_send()

    for h in (0, 1):
        three(abuf, h, gathered, 0).wait()
        three(bbuf, h, gathered, 1).wait()
        b = jnp.concatenate([bbuf[h, q].reshape(512, 128) for q in range(4)], axis=1)
        b_wide = b.astype(F32)
        ones = jnp.ones((16, 512), BF16)
        b_norm = sum(dot(ones, p, ((1,), (1,))) for p in parts(b_wide * b_wide, 2))[0:1]
        for half in (1 - core, core):
            a = jnp.concatenate(
                [abuf[h, q, pl.ds(half * 4, 4)].reshape(256, 128) for q in range(4)], axis=1)
            a_wide = a.astype(F32)
            a_norm = jnp.sum(a_wide * a_wide, axis=1, keepdims=True)
            value = (a_norm + b_norm - 2.0 * dot(a, b, ((1,), (1,)))).reshape(4, 4, 16, 512)
            if h == 1:
                value = value + part[half]
            part[half] = value
            if h == 1 and half is not core:
                core_sums = [send_pieces(2, part.at[half, n], sib.at[n], sib_send.at[n], sib_recv.at[n], sibling)
                             for n in range(4)]

    for n in range(4):
        core_sums[n].wait()
        own[pl.ds(n * 4, 4)] = part[core, n] + sib[n]

    def at_plane(o):
        return device(x, y, lax.rem(z + o + 16, 16), core)

    for d in (8, 7, 6, 5):
        send(own.at[lax.rem(z + d, 16)], rs_up.at[d - 5], rs_send.at[0], rs_recv.at[0], at_plane(d - 4))
        if d < 8:
            send(own.at[lax.rem(z + 16 - d, 16)], rs_down.at[d - 5], rs_send.at[1], rs_recv.at[1], at_plane(4 - d))
    for d in (3, 2, 1):
        send(own.at[lax.rem(z + d, 16)], rs_near.at[d - 1], rs_send.at[2], rs_recv.at[2], at_plane(d))
        send(own.at[lax.rem(z + 16 - d, 16)], rs_near.at[d + 2], rs_send.at[2], rs_recv.at[2], at_plane(-d))
    remote(rs_up, rs_up, rs_send.at[0], rs_recv.at[0], sibling).wait_recv()
    rs_sum[0] = own[lax.rem(z + 4, 16)] + four(rs_up)
    last_up = send(rs_sum.at[0], rs_last.at[0], rs_send.at[3], rs_recv.at[3], at_plane(4))
    remote(rs_down, rs_down, rs_send.at[1], rs_recv.at[1], sibling).wait_recv()
    rs_sum[1] = own[lax.rem(z + 12, 16)] + (rs_down[0] + rs_down[1] + rs_down[2])
    last_down = send(rs_sum.at[1], rs_last.at[1], rs_send.at[4], rs_recv.at[4], at_plane(-4))
    remote(rs_near, rs_near, rs_send.at[2], rs_recv.at[2], sibling).wait()
    near = own[z] + ((rs_near[0] + rs_near[1]) + (rs_near[2] + rs_near[3]) + (rs_near[4] + rs_near[5]))
    last_up.wait()
    last_down.wait()
    total[...] = near + (rs_last[0] + rs_last[1])
    remote(rs_up, rs_up, rs_send.at[0], rs_recv.at[0], sibling).wait_send()
    remote(rs_down, rs_down, rs_send.at[1], rs_recv.at[1], sibling).wait_send()

    my_rows = pl.ds(pl.multiple_of(128 + z * 16, 16), 16)

    def gather(n, p):
        return (total, ext.at[my_rows, pl.ds(128, 512)], ag_send.at[n], ag_recv.at[0],
                device(x, y, p, core))

    def each_gather(do):
        for n in (2, 1, 3):
            do(gather(n, lax.rem(group + n, 4) * 4 + 1))

        @pl.when(jnp.logical_not(iterates))
        def _():
            do(gather(0, group * 4 + 1))

    each_gather(lambda copy: send_pieces(2, *copy))

    @pl.when(iterates)
    def _():
        ext[my_rows, 128:640] = total[...]
        view = ext.at[pl.ds(0, 240), pl.ds(128, 512)]
        remote(view, view, ag_send.at[0], ag_recv.at[0], sibling).wait_recv()

        x_next, y_next = lax.rem(x + core, 4), lax.rem(y + 1, 4)
        below, right, both = (
            device(x_next, y, z, 1 - core), device(x, y_next, z, core), device(x_next, y_next, z, 1 - core))
        bottom, inner, edge = pl.ds(256, 128), pl.ds(128, 512), pl.ds(512, 128)
        halo = [
            send_pieces(4, ext.at[bottom, inner], ext.at[pl.ds(0, 128), inner],
                        halo_send.at[0], halo_recv.at[0], below),
            send_pieces(2, ext.at[bottom, edge], ext.at[pl.ds(0, 128), pl.ds(0, 128)],
                        halo_send.at[2], halo_recv.at[2], both),
            send_pieces(4, ext.at[pl.ds(128, 256), edge], ext.at[pl.ds(128, 256), pl.ds(0, 128)],
                        halo_send.at[1], halo_recv.at[1], right),
        ]
        for copy in halo:
            copy.wait()
        rows = lax.broadcasted_iota(jnp.int32, (384, 640), 0)
        lanes = lax.broadcasted_iota(jnp.int32, (384, 640), 1)
        first_row = jnp.where(2 * x + core == 0, 128, 0)
        first_lane = jnp.where(y == 0, 128, 0)
        run = jnp.where((rows >= first_row) & (lanes >= first_lane), ext[...], 0.0)
        run = jnp.concatenate(
            [pltpu.roll(run[r:r + 8], (640 - r) % 640, 1) for r in range(0, 384, 8)], axis=0)
        stride = LAGS // 2
        while stride >= 8:
            run = run[stride:] + run[:-stride]
            stride //= 2
        run = jnp.concatenate(
            [pltpu.roll(run[r:r + 8], r + 120, 1) for r in range(0, 264, 8)], axis=0)
        while stride >= 1:
            run = run + pltpu.roll(pltpu.roll(run, stride, 1), stride, 0)
            stride //= 2
        lagged = run[8:, 128:]
        i = lax.broadcasted_iota(jnp.int32, (256, 512), 0) + (x * 512 + core * 256)
        j = lax.broadcasted_iota(jnp.int32, (256, 512), 1) + y * 512
        counts = (jnp.minimum(jnp.minimum(i, j), LAGS - 1) + 1).astype(F32)
        half_tile = jnp.exp(-(lagged / (counts * (PTS * 0.25))))
        half_hi, half_lo = parts(half_tile, 2)
        my_half = pl.ds(pl.multiple_of(core * 256, 256), 256)
        kern_hi[my_half, :] = half_hi
        kern_lo[my_half, :] = half_lo
        swaps = [remote(ref.at[my_half, :], ref.at[my_half, :], core_send.at[n], core_recv.at[n], sibling)
                 for n, ref in enumerate((kern_hi, kern_lo))]

        @pl.when(core == 1)
        def _():
            for n, ref in enumerate((kern_hi, kern_lo)):
                send_pieces(4, ref.at[my_half, :], ref.at[my_half, :], core_send.at[n], core_recv.at[n], sibling)

        ones = jnp.ones((16, 512), BF16)
        deg_row[core * 4 + y] = (dot(ones, half_hi, ((1,), (1,))) + dot(ones, half_lo, ((1,), (1,))))[:8]
        deg_col[core * 4 + x] = (dot(ones[:, :256], half_hi, ((1,), (0,)))
                            + dot(ones[:, :256], half_lo, ((1,), (0,))))[:8]

        def degree_copies(k):
            row_view, col_view = deg_row.at[core * 4 + y], deg_col.at[core * 4 + x]
            return (remote(row_view, row_view, deg_send.at[0], deg_recv.at[0], along_y(k, 0)),
                    remote(col_view, col_view, deg_send.at[1], deg_recv.at[1], along_x(k, 0)))

        @pl.when(core == 1)
        def _():
            for k in (2, 1, 3, 0):
                for copy in degree_copies(k):
                    copy.start()
            for copy in swaps:
                copy.wait_send()
            for n, ref in enumerate((deg_row, deg_col)):
                view = ref.at[pl.ds(0, 4)]
                remote(view, view, deg_send.at[n], deg_recv.at[n], sibling).wait_send()

    @pl.when(iterates & (core == 0))
    def _():
        for k in (2, 1, 3):
            for n, ref, target in ((0, deg_row.at[y], along_y(k)), (1, deg_col.at[x], along_x(k))):
                send(ref, ref, deg_send.at[n], deg_recv.at[n], target)
        wide[...] = jnp.zeros_like(wide)

        def gram_of(block):
            wide[0:32, :] = block
            return dot(block, wide[...], ((1,), (1,)), HIGH)

        for k in range(4):
            @pl.when(row != 4 * y + k)
            def _():
                remote(start_ref, start.at[k], st_send.at[2], st_recv.at[k], sibling).wait_recv()
        mine = [start[k].T for k in range(4)]
        basis = [jnp.concatenate(mine[:2], axis=1), jnp.concatenate(mine[2:], axis=1)]
        other_half = pl.ds(256, 256)
        for n, ref in enumerate((kern_hi, kern_lo)):
            remote(ref.at[other_half, :], ref.at[other_half, :], core_send.at[n], core_recv.at[n], sibling).wait_recv()
        for n, ref in enumerate((deg_row, deg_col)):
            sent, arriving = ref.at[pl.ds(0, 3)], ref.at[pl.ds(0, 7)]
            remote(arriving, arriving, deg_send.at[n], deg_recv.at[n], sibling).wait_recv()
            remote(sent, sent, deg_send.at[n], deg_recv.at[n], sibling).wait_send()
        low_half, high_half = pl.ds(0, 4), pl.ds(4, 4)
        row_sums = jnp.concatenate([four(deg_row.at[low_half]), four(deg_row.at[high_half])], axis=1)[0:1]
        scale_row = 1.0 / jnp.sqrt(row_sums)
        scale_col = 1.0 / jnp.sqrt((four(deg_col.at[low_half]) + four(deg_col.at[high_half]))[0:1])
        scale_row = scale_row[:, :256], scale_row[:, 256:]
        scale_col = scale_col[:, :256], scale_col[:, 256:]

        def term(over_y, n, m, block):
            n, m = pl.ds(n * 256, 256), pl.ds(m * 256, 256)
            at, dims = ((m, n), ((1,), (1,))) if over_y else ((n, m), ((1,), (0,)))
            high = dot(jnp.concatenate(block, axis=0), kern_hi[at], dims)
            low = dot(jnp.concatenate(block[:2], axis=0), kern_lo[at], dims)
            return high[:32] + ((high[32:64] + low[:32]) + (high[64:] + low[32:]))

        def product_wait(step, n):
            three = income.at[step, n, pl.ds(0, 3)]
            return remote(three, three, step_send.at[step, n], step_recv.at[step, n], sibling)

        def arrived(step, n):
            product_wait(step, n).wait_recv()
            block = four(income.at[step, n])
            return dot(inverse, block, ((1,), (0,)), HIGH) if step in (3, 5) else block

        inverse = None
        gram_copies = None
        for step in range(6):
            over_y = step % 2 == 0
            at = y if over_y else x
            scale_in, scale_out = (scale_col, scale_row) if over_y else (scale_row, scale_col)
            sums = None
            for n in (0, 1):
                if step:
                    basis[n] = arrived(step - 1, n)
                block = parts(basis[n] * scale_in[n], 3)
                if n == 0:
                    sums = [term(over_y, 0, m, block) for m in (0, 1)]
                    continue
                for m in (0, 1):
                    income[step, m, at] = (sums[m] + term(over_y, 1, m, block)) * scale_out[m]
                    view = income.at[step, m, at]
                    for k in (2, 1, 3):
                        send(view, view, step_send.at[step, m], step_recv.at[step, m],
                             along_y(k) if over_y else along_x(k))
            if step:
                for m in (0, 1):
                    product_wait(step - 1, m).wait_send()
            if step in (2, 4):
                n = step // 2 - 1
                grams[n, y] = gram_of(jnp.concatenate(basis, axis=1))
                gram_copies = [send(grams.at[n, y], grams.at[n, y], gram_send.at[n, k],
                                    gram_recv.at[n, k], along_y(k)) for k in (2, 1, 3)]
            if step in (3, 5):
                for copy in gram_copies:
                    copy.wait()
                inverse = inverse_factor(four(grams.at[step // 2 - 1]))
        basis = jnp.concatenate([arrived(5, 0), arrived(5, 1)], axis=1)

        owner = lax.div(y, 2) == lax.rem(group, 2)

        def row_copy(k, i, c):
            return remote(last.at[:, pl.ds((i * 2 + c) * 128, 128)], last_rows, row_send.at[k, i, c],
                          row_recv.at[0], device(x, lax.rem(y + k, 4), z_hi * 8 + 2 * y + i, c))

        def each_row_copy(do):
            for k in (2, 1, 3, 0):
                for i in (0, 1):
                    for c in (0, 1):
                        if k or c:
                            do(row_copy(k, i, c))
                        else:
                            @pl.when(z_lo != 2 * y + i)
                            def _():
                                do(row_copy(k, i, c))

        gram = gram_of(basis)
        last_grams[y] = jnp.concatenate([gram[8 * n:8 * n + 8, :32] for n in range(4)], axis=1)
        waits = []
        for k in (2, 1, 3, 0):
            for i in (2, 1, 3, 0):
                for c in (0, 1):
                    if k or i or c:
                        target = device(x, lax.rem(y + k, 4), group * 4 + lax.rem(1 + i, 4), c)
                        waits.append(send(last_grams.at[y], last_grams.at[y], fin_send.at[k, i, c],
                                          fin_recv.at[y], target))

        last[...] = basis

        @pl.when(owner)
        def _():
            each_row_copy(lambda copy: copy.start())
            for i in (0, 1):
                @pl.when(z_lo == 2 * y + i)
                def _():
                    last_rows[...] = last[:, i * 256:i * 256 + 128]

        for m in (0, 1):
            product_wait(5, m).wait_send()
        for copy in waits:
            copy.wait_send()

        @pl.when(owner)
        def _():
            each_row_copy(lambda copy: copy.wait_send())

    for q in range(4):
        @pl.when(jnp.logical_not(iterates & (core == 0) & (y == q)))
        def _():
            remote(last_grams.at[q], last_grams.at[q], fin_send.at[0, 0, 0], fin_recv.at[q], sibling).wait_recv()
    packed = four(last_grams)
    packed = jnp.concatenate([packed[:, 32 * n:32 * n + 32] for n in range(4)], axis=0)
    inverse = inverse_factor(jnp.concatenate([packed, jnp.zeros((32, 96), F32)], axis=1))

    @pl.when(jnp.logical_not(iterates & (core == 0) & (y == lax.div(z_lo, 2))))
    def _():
        remote(last_rows, last_rows, row_send.at[0, 0, 0], row_recv.at[0], sibling).wait_recv()

    out_ref[...] = dot(inverse, last_rows[...], ((1,), (0,)), HIGH) * math.sqrt(SNAPS)

    for n, t in enumerate((2, 10)):
        @pl.when(giver & (row != t))
        def _():
            basis_copy(n, t).wait_send()
    each_gather(lambda copy: remote(*copy).wait_send())


VMEM = pl.BlockSpec(memory_space=pltpu.VMEM)
ANY = pl.BlockSpec(memory_space=pl.ANY)
DMA = pltpu.SemaphoreType.DMA


def body(snapshots, start_block):
    out = pl.pallas_call(
        kernel,
        out_shape=jax.ShapeDtypeStruct((32, 128), F32),
        in_specs=[ANY, ANY],
        out_specs=VMEM,
        scratch_shapes=[
            pltpu.VMEM((2, 4, 8, 16, 128), BF16),
            pltpu.VMEM((2, 4, 8, 4, 16, 128), BF16),
            pltpu.VMEM((2, 4, 8, 4, 16, 128), BF16),
            pltpu.VMEM((2, 4, 4, 16, 512), F32),
            pltpu.VMEM((4, 4, 16, 512), F32),
            pltpu.VMEM((16, 16, 512), F32),
            pltpu.VMEM((4, 16, 512), F32),
            pltpu.VMEM((3, 16, 512), F32),
            pltpu.VMEM((6, 16, 512), F32),
            pltpu.VMEM((2, 16, 512), F32),
            pltpu.VMEM((2, 16, 512), F32),
            pltpu.VMEM((16, 512), F32),
            pltpu.VMEM((4, 128, 32), F32),
            pltpu.VMEM((384, 640), F32),
            pltpu.VMEM((512, 512), BF16),
            pltpu.VMEM((512, 512), BF16),
            pltpu.VMEM((8, 8, 256), F32),
            pltpu.VMEM((8, 8, 512), F32),
            pltpu.VMEM((128, 512), F32),
            pltpu.VMEM((6, 2, 4, 32, 256), F32),
            pltpu.VMEM((2, 4, 32, 128), F32),
            pltpu.VMEM((32, 512), F32),
            pltpu.VMEM((32, 128), F32),
            pltpu.VMEM((4, 8, 128), F32),
            DMA((1,)), DMA((2,)), DMA((2,)), DMA((2, 2)), DMA((2, 2)), DMA((2, 2)), DMA((2, 2)),
            DMA((4,)), DMA((4,)), DMA((5,)), DMA((5,)), DMA((4,)), DMA((1,)), DMA((3,)), DMA((4,)),
            DMA((3,)), DMA((3,)), DMA((2,)), DMA((2,)), DMA((2,)), DMA((2,)),
            DMA((6, 2)), DMA((6, 2)), DMA((2, 4)), DMA((2, 4)), DMA((4, 4, 2)), DMA((4,)),
            DMA((4, 2, 2)), DMA((1,)),
        ],
        compiler_params=pltpu.CompilerParams(
            collective_id=1, has_side_effects=True, vmem_limit_bytes=48 << 20),
        name="subspace",
    )(snapshots, start_block)
    return out.T


def solution(mesh):
    placed = (P(("row", "col"), "feat"), P("row", None))
    return jax.shard_map(
        body, mesh=mesh, in_specs=placed, out_specs=P("row", None), check_vma=False
    )
```

```python
import math

import jax
import jax.numpy as jnp
from jax import lax
from jax.experimental import pallas as pl
from jax.experimental.pallas import tpu as pltpu
from jax.sharding import PartitionSpec as P

PTS = 32768
LAGS = 128
SNAPS = 2048
MESH = pl.DeviceIdType.MESH
HIGH = lax.Precision.HIGHEST
F32 = jnp.float32
BF16 = jnp.bfloat16


def device(x, y, z, core):
    return (lax.rem(z, 8) * 2 + core, lax.div(z, 8) * 4 + x, y)


def remote(src, dst, send_sem, recv_sem, target):
    return pltpu.make_async_remote_copy(
        src_ref=src, dst_ref=dst, send_sem=send_sem, recv_sem=recv_sem,
        device_id=target, device_id_type=MESH,
    )


def send(*args):
    copy = remote(*args)
    copy.start()
    return copy


def send_pieces(count, src, dst, send_sem, recv_sem, target):
    rows = src.shape[0] // count
    for n in range(count):
        piece = pl.ds(n * rows, rows)
        send(src.at[piece], dst.at[piece], send_sem, recv_sem, target)
    return remote(src, dst, send_sem, recv_sem, target)


def dot(a, b, dims, precision=None):
    return lax.dot_general(
        a, b, (dims, ((), ())), precision=precision, preferred_element_type=F32
    )


def parts(value, count):
    out = []
    for _ in range(count):
        out.append(value.astype(BF16))
        value = value - out[-1].astype(F32)
    return out


def inverse_factor(gram):
    rows = lax.broadcasted_iota(jnp.int32, (32, 128), 0)
    lanes = lax.broadcasted_iota(jnp.int32, (32, 128), 1)
    work = jnp.where(lanes < 32, gram, jnp.where(lanes - 32 == rows, 1.0, 0.0))
    for k in range(0, 32, 16):
        tops = [work[k + n:k + n + 1, :] for n in range(16)]
        columns = [jnp.broadcast_to(work[:, k + n:k + n + 1], (32, 128)) for n in range(16)]
        for n in range(16):
            at = k + n
            ratio = columns[n] * (1.0 / columns[n][at:at + 1, :])
            for m in range(n + 1, 16):
                tops[m] = tops[m] - ratio[k + m:k + m + 1, :] * tops[n]
                columns[m] = columns[m] - ratio * columns[m][at:at + 1, :]
            work = work - jnp.where(rows > at, ratio, 0.0) * tops[n]
    diagonal = jnp.sum(jnp.where(lanes == rows, work, 0.0), axis=1, keepdims=True)
    return work[:, 32:64] / jnp.sqrt(diagonal)


def four(ref):
    return (ref[0] + ref[1]) + (ref[2] + ref[3])


def kernel(
    x_ref, start_ref, out_ref,
    zbuf, abuf, bbuf, part, sib, own, rs_up, rs_down, rs_near, rs_sum, rs_last, total, start,
    ext, kern_hi, kern_lo, deg_row, deg_col, wide, income, grams, last, last_rows, last_grams,
    local_sem, z_send, z_recv, plane_send, plane_recv, gather_send, gather_recv,
    sib_send, sib_recv, rs_send, rs_recv, ag_send, ag_recv, st_send, st_recv,
    halo_send, halo_recv, core_send, core_recv, deg_send, deg_recv,
    step_send, step_recv, gram_send, gram_recv, fin_send, fin_recv, row_send, row_recv,
):
    row, col, y = lax.axis_index("row"), lax.axis_index("col"), lax.axis_index("feat")
    x, z_hi = lax.rem(col, 4), lax.div(col, 4)
    core, z_lo = lax.rem(row, 2), lax.div(row, 2)
    z = z_hi * 8 + z_lo
    me = z * 2 + core
    group = lax.div(z, 4)
    iterates = lax.rem(z, 4) == 1

    def line(t):
        return device(x, y, lax.div(t, 2), lax.rem(t, 2))

    def along_x(k, c=core):
        return device(lax.rem(x + k, 4), y, z, c)

    def along_y(k, c=core):
        return device(x, lax.rem(y + k, 4), z, c)

    sibling = device(x, y, z, 1 - core)
    barrier = pltpu.get_barrier_semaphore()
    far_first = sorted(range(1, 32), key=lambda o: -min(o, 32 - o))
    partners = ([line(lax.rem(me + o, 32)) for o in far_first]
                + [along_x(k) for k in (1, 2, 3)] + [along_y(k) for k in (1, 2, 3)])
    for target in partners:
        pl.semaphore_signal(barrier, inc=1, device_id=target, device_id_type=MESH)
    pl.semaphore_wait(barrier, len(partners))

    def columns(t, h):
        return pl.ds(pl.multiple_of(t * 256 + h * 128, 128), 128)

    big, small = lax.div(z_lo, 2), lax.rem(z_lo, 2) * 4 + core * 2 + z_hi
    def half_wait(h):
        sent = x_ref.at[:, pl.ds(0, 31 * 128)]
        return (remote(sent, sent, z_send.at[h], z_recv.at[h], sibling),
                remote(zbuf.at[h], zbuf.at[h], z_send.at[h], z_recv.at[h], sibling))

    for h in (0, 1):
        if h:
            half_wait(0)[0].wait_send()
        for o in far_first:
            t = lax.rem(me + o, 32)
            send(x_ref.at[:, columns(t, h)], zbuf.at[h, big, small], z_send.at[h], z_recv.at[h], line(t))
        pltpu.make_async_copy(x_ref.at[:, columns(me, h)], zbuf.at[h, big, small], z_recv.at[h]).start()

    giver = lax.div(row, 4) == y
    basis_slot = lax.rem(row, 4)

    def basis_copy(n, t):
        return remote(start_ref, start.at[basis_slot], st_send.at[n], st_recv.at[basis_slot],
                      (t, col, y))

    for n, t in enumerate((2, 10)):
        @pl.when(giver & (row != t))
        def _():
            basis_copy(n, t).start()

    @pl.when(giver)
    def _():
        copy = pltpu.make_async_copy(start_ref, start.at[basis_slot], local_sem.at[0])
        copy.start()
        copy.wait()

    def three(ref, h, sems, n):
        view = ref.at[h, pl.ds(0, 3)]
        return remote(view, view, sems[0].at[h, n], sems[1].at[h, n], sibling)

    plane, gathered = (plane_send, plane_recv), (gather_send, gather_recv)
    for h in (0, 1):
        half_wait(h)[1].wait_recv()
        for k in (2, 1, 3):
            send(zbuf.at[h, lax.rem(x + k, 4)], abuf.at[h, y, :, x],
                 plane_send.at[h, 0], plane_recv.at[h, 0], along_x(k))
            send(zbuf.at[h, lax.rem(y + k, 4)], bbuf.at[h, y, :, x],
                 plane_send.at[h, 1], plane_recv.at[h, 1], along_y(k))
        abuf[h, y, :, x] = zbuf[h, x]
        bbuf[h, y, :, x] = zbuf[h, y]
    half_wait(1)[0].wait_send()
    for h in (0, 1):
        three(zbuf, h, plane, 0).wait_recv()
        for k in (2, 1, 3):
            send_pieces(4, abuf.at[h, y], abuf.at[h, y], gather_send.at[h, 0], gather_recv.at[h, 0], along_y(k))
        three(zbuf, h, plane, 1).wait_recv()
        for k in (2, 1, 3):
            send_pieces(4, bbuf.at[h, :, :, x], bbuf.at[h, :, :, x],
                        gather_send.at[h, 1], gather_recv.at[h, 1], along_x(k))
    for h in (0, 1):
        for n in (0, 1):
            three(zbuf, h, plane, n).wait_send()

    for h in (0, 1):
        three(abuf, h, gathered, 0).wait()
        three(bbuf, h, gathered, 1).wait()
        b = jnp.concatenate([bbuf[h, q].reshape(512, 128) for q in range(4)], axis=1)
        b_wide = b.astype(F32)
        ones = jnp.ones((16, 512), BF16)
        b_norm = sum(dot(ones, p, ((1,), (1,))) for p in parts(b_wide * b_wide, 2))[0:1]
        for half in (1 - core, core):
            a = jnp.concatenate(
                [abuf[h, q, pl.ds(half * 4, 4)].reshape(256, 128) for q in range(4)], axis=1)
            a_wide = a.astype(F32)
            a_norm = jnp.sum(a_wide * a_wide, axis=1, keepdims=True)
            value = (a_norm + b_norm - 2.0 * dot(a, b, ((1,), (1,)))).reshape(4, 4, 16, 512)
            if h == 1:
                value = value + part[half]
            part[half] = value
            if h == 1 and half is not core:
                core_sums = [send_pieces(2, part.at[half, n], sib.at[n], sib_send.at[n], sib_recv.at[n], sibling)
                             for n in range(4)]

    for n in range(4):
        core_sums[n].wait()
        own[pl.ds(n * 4, 4)] = part[core, n] + sib[n]

    def at_plane(o):
        return device(x, y, lax.rem(z + o + 16, 16), core)

    for d in (8, 7, 6, 5):
        send(own.at[lax.rem(z + d, 16)], rs_up.at[d - 5], rs_send.at[0], rs_recv.at[0], at_plane(d - 4))
        if d < 8:
            send(own.at[lax.rem(z + 16 - d, 16)], rs_down.at[d - 5], rs_send.at[1], rs_recv.at[1], at_plane(4 - d))
    remote(rs_up, rs_up, rs_send.at[0], rs_recv.at[0], sibling).wait_recv()
    rs_sum[0] = own[lax.rem(z + 4, 16)] + four(rs_up)
    last_up = send(rs_sum.at[0], rs_last.at[0], rs_send.at[3], rs_recv.at[3], at_plane(4))
    remote(rs_down, rs_down, rs_send.at[1], rs_recv.at[1], sibling).wait_recv()
    rs_sum[1] = own[lax.rem(z + 12, 16)] + (rs_down[0] + rs_down[1] + rs_down[2])
    last_down = send(rs_sum.at[1], rs_last.at[1], rs_send.at[4], rs_recv.at[4], at_plane(-4))
    for d in (3, 2, 1):
        send(own.at[lax.rem(z + d, 16)], rs_near.at[d - 1], rs_send.at[2], rs_recv.at[2], at_plane(d))
        send(own.at[lax.rem(z + 16 - d, 16)], rs_near.at[d + 2], rs_send.at[2], rs_recv.at[2], at_plane(-d))
    remote(rs_near, rs_near, rs_send.at[2], rs_recv.at[2], sibling).wait()
    near = own[z] + ((rs_near[0] + rs_near[1]) + (rs_near[2] + rs_near[3]) + (rs_near[4] + rs_near[5]))
    last_up.wait()
    last_down.wait()
    total[...] = near + (rs_last[0] + rs_last[1])
    remote(rs_up, rs_up, rs_send.at[0], rs_recv.at[0], sibling).wait_send()
    remote(rs_down, rs_down, rs_send.at[1], rs_recv.at[1], sibling).wait_send()

    my_rows = pl.ds(pl.multiple_of(128 + z * 16, 16), 16)

    def gather(n, p):
        return (total, ext.at[my_rows, pl.ds(128, 512)], ag_send.at[n], ag_recv.at[0],
                device(x, y, p, core))

    def each_gather(do):
        for n in (2, 1, 3):
            do(gather(n, lax.rem(group + n, 4) * 4 + 1))

        @pl.when(jnp.logical_not(iterates))
        def _():
            do(gather(0, group * 4 + 1))

    each_gather(lambda copy: send_pieces(2, *copy))

    @pl.when(iterates)
    def _():
        ext[my_rows, 128:640] = total[...]
        view = ext.at[pl.ds(0, 240), pl.ds(128, 512)]
        remote(view, view, ag_send.at[0], ag_recv.at[0], sibling).wait_recv()

        x_next, y_next = lax.rem(x + core, 4), lax.rem(y + 1, 4)
        below, right, both = (
            device(x_next, y, z, 1 - core), device(x, y_next, z, core), device(x_next, y_next, z, 1 - core))
        bottom, inner, edge = pl.ds(256, 128), pl.ds(128, 512), pl.ds(512, 128)
        halo = [
            send_pieces(4, ext.at[bottom, inner], ext.at[pl.ds(0, 128), inner],
                        halo_send.at[0], halo_recv.at[0], below),
            send_pieces(2, ext.at[bottom, edge], ext.at[pl.ds(0, 128), pl.ds(0, 128)],
                        halo_send.at[2], halo_recv.at[2], both),
            send_pieces(4, ext.at[pl.ds(128, 256), edge], ext.at[pl.ds(128, 256), pl.ds(0, 128)],
                        halo_send.at[1], halo_recv.at[1], right),
        ]
        for copy in halo:
            copy.wait()
        rows = lax.broadcasted_iota(jnp.int32, (384, 640), 0)
        lanes = lax.broadcasted_iota(jnp.int32, (384, 640), 1)
        first_row = jnp.where(2 * x + core == 0, 128, 0)
        first_lane = jnp.where(y == 0, 128, 0)
        run = jnp.where((rows >= first_row) & (lanes >= first_lane), ext[...], 0.0)
        run = jnp.concatenate(
            [pltpu.roll(run[r:r + 8], (640 - r) % 640, 1) for r in range(0, 384, 8)], axis=0)
        stride = LAGS // 2
        while stride >= 8:
            run = run[stride:] + run[:-stride]
            stride //= 2
        run = jnp.concatenate(
            [pltpu.roll(run[r:r + 8], r + 120, 1) for r in range(0, 264, 8)], axis=0)
        while stride >= 1:
            run = run + pltpu.roll(pltpu.roll(run, stride, 1), stride, 0)
            stride //= 2
        lagged = run[8:, 128:]
        i = lax.broadcasted_iota(jnp.int32, (256, 512), 0) + (x * 512 + core * 256)
        j = lax.broadcasted_iota(jnp.int32, (256, 512), 1) + y * 512
        counts = (jnp.minimum(jnp.minimum(i, j), LAGS - 1) + 1).astype(F32)
        half_tile = jnp.exp(-(lagged / (counts * (PTS * 0.25))))
        half_hi, half_lo = parts(half_tile, 2)
        my_half = pl.ds(pl.multiple_of(core * 256, 256), 256)
        kern_hi[my_half, :] = half_hi
        kern_lo[my_half, :] = half_lo
        swaps = [remote(ref.at[my_half, :], ref.at[my_half, :], core_send.at[n], core_recv.at[n], sibling)
                 for n, ref in enumerate((kern_hi, kern_lo))]

        @pl.when(core == 1)
        def _():
            for n, ref in enumerate((kern_hi, kern_lo)):
                send_pieces(4, ref.at[my_half, :], ref.at[my_half, :], core_send.at[n], core_recv.at[n], sibling)

        ones = jnp.ones((16, 512), BF16)
        deg_row[core * 4 + y] = (dot(ones, half_hi, ((1,), (1,))) + dot(ones, half_lo, ((1,), (1,))))[:8]
        deg_col[core * 4 + x] = (dot(ones[:, :256], half_hi, ((1,), (0,)))
                            + dot(ones[:, :256], half_lo, ((1,), (0,))))[:8]

        def degree_copies(k):
            row_view, col_view = deg_row.at[core * 4 + y], deg_col.at[core * 4 + x]
            return (remote(row_view, row_view, deg_send.at[0], deg_recv.at[0], along_y(k, 0)),
                    remote(col_view, col_view, deg_send.at[1], deg_recv.at[1], along_x(k, 0)))

        @pl.when(core == 1)
        def _():
            for k in (2, 1, 3, 0):
                for copy in degree_copies(k):
                    copy.start()
            for copy in swaps:
                copy.wait_send()
            for n, ref in enumerate((deg_row, deg_col)):
                view = ref.at[pl.ds(0, 4)]
                remote(view, view, deg_send.at[n], deg_recv.at[n], sibling).wait_send()

    @pl.when(iterates & (core == 0))
    def _():
        for k in (2, 1, 3):
            for n, ref, target in ((0, deg_row.at[y], along_y(k)), (1, deg_col.at[x], along_x(k))):
                send(ref, ref, deg_send.at[n], deg_recv.at[n], target)
        wide[...] = jnp.zeros_like(wide)

        def gram_of(block):
            wide[0:32, :] = block
            return dot(block, wide[...], ((1,), (1,)), HIGH)

        for k in range(4):
            @pl.when(row != 4 * y + k)
            def _():
                remote(start_ref, start.at[k], st_send.at[2], st_recv.at[k], sibling).wait_recv()
        mine = [start[k].T for k in range(4)]
        basis = [jnp.concatenate(mine[:2], axis=1), jnp.concatenate(mine[2:], axis=1)]
        other_half = pl.ds(256, 256)
        for n, ref in enumerate((kern_hi, kern_lo)):
            remote(ref.at[other_half, :], ref.at[other_half, :], core_send.at[n], core_recv.at[n], sibling).wait_recv()
        for n, ref in enumerate((deg_row, deg_col)):
            sent, arriving = ref.at[pl.ds(0, 3)], ref.at[pl.ds(0, 7)]
            remote(arriving, arriving, deg_send.at[n], deg_recv.at[n], sibling).wait_recv()
            remote(sent, sent, deg_send.at[n], deg_recv.at[n], sibling).wait_send()
        low_half, high_half = pl.ds(0, 4), pl.ds(4, 4)
        row_sums = jnp.concatenate([four(deg_row.at[low_half]), four(deg_row.at[high_half])], axis=1)[0:1]
        scale_row = 1.0 / jnp.sqrt(row_sums)
        scale_col = 1.0 / jnp.sqrt((four(deg_col.at[low_half]) + four(deg_col.at[high_half]))[0:1])
        scale_row = scale_row[:, :256], scale_row[:, 256:]
        scale_col = scale_col[:, :256], scale_col[:, 256:]

        def term(over_y, n, m, block):
            n, m = pl.ds(n * 256, 256), pl.ds(m * 256, 256)
            at, dims = ((m, n), ((1,), (1,))) if over_y else ((n, m), ((1,), (0,)))
            high = dot(jnp.concatenate(block, axis=0), kern_hi[at], dims)
            low = dot(jnp.concatenate(block[:2], axis=0), kern_lo[at], dims)
            return high[:32] + ((high[32:64] + low[:32]) + (high[64:] + low[32:]))

        def product_wait(step, n):
            three = income.at[step, n, pl.ds(0, 3)]
            return remote(three, three, step_send.at[step, n], step_recv.at[step, n], sibling)

        def arrived(step, n):
            product_wait(step, n).wait_recv()
            block = four(income.at[step, n])
            return dot(inverse, block, ((1,), (0,)), HIGH) if step in (3, 5) else block

        inverse = None
        gram_copies = None
        for step in range(6):
            over_y = step % 2 == 0
            at = y if over_y else x
            scale_in, scale_out = (scale_col, scale_row) if over_y else (scale_row, scale_col)
            sums = None
            for n in (0, 1):
                if step:
                    basis[n] = arrived(step - 1, n)
                block = parts(basis[n] * scale_in[n], 3)
                if n == 0:
                    sums = [term(over_y, 0, m, block) for m in (0, 1)]
                    continue
                for m in (0, 1):
                    income[step, m, at] = (sums[m] + term(over_y, 1, m, block)) * scale_out[m]
                    view = income.at[step, m, at]
                    for k in (2, 1, 3):
                        send(view, view, step_send.at[step, m], step_recv.at[step, m],
                             along_y(k) if over_y else along_x(k))
            if step:
                for m in (0, 1):
                    product_wait(step - 1, m).wait_send()
            if step in (2, 4):
                n = step // 2 - 1
                grams[n, y] = gram_of(jnp.concatenate(basis, axis=1))
                gram_copies = [send(grams.at[n, y], grams.at[n, y], gram_send.at[n, k],
                                    gram_recv.at[n, k], along_y(k)) for k in (2, 1, 3)]
            if step in (3, 5):
                for copy in gram_copies:
                    copy.wait()
                inverse = inverse_factor(four(grams.at[step // 2 - 1]))
        basis = jnp.concatenate([arrived(5, 0), arrived(5, 1)], axis=1)

        owner = lax.div(y, 2) == lax.rem(group, 2)

        def row_copy(k, i, c):
            return remote(last.at[:, pl.ds((i * 2 + c) * 128, 128)], last_rows, row_send.at[k, i, c],
                          row_recv.at[0], device(x, lax.rem(y + k, 4), z_hi * 8 + 2 * y + i, c))

        def each_row_copy(do):
            for k in (2, 1, 3, 0):
                for i in (0, 1):
                    for c in (0, 1):
                        if k or c:
                            do(row_copy(k, i, c))
                        else:
                            @pl.when(z_lo != 2 * y + i)
                            def _():
                                do(row_copy(k, i, c))

        gram = gram_of(basis)
        last_grams[y] = jnp.concatenate([gram[8 * n:8 * n + 8, :32] for n in range(4)], axis=1)
        waits = []
        for k in (2, 1, 3, 0):
            for i in (2, 1, 3, 0):
                for c in (0, 1):
                    if k or i or c:
                        target = device(x, lax.rem(y + k, 4), group * 4 + lax.rem(1 + i, 4), c)
                        waits.append(send(last_grams.at[y], last_grams.at[y], fin_send.at[k, i, c],
                                          fin_recv.at[y], target))

        last[...] = basis

        @pl.when(owner)
        def _():
            each_row_copy(lambda copy: copy.start())
            for i in (0, 1):
                @pl.when(z_lo == 2 * y + i)
                def _():
                    last_rows[...] = last[:, i * 256:i * 256 + 128]

        for m in (0, 1):
            product_wait(5, m).wait_send()
        for copy in waits:
            copy.wait_send()

        @pl.when(owner)
        def _():
            each_row_copy(lambda copy: copy.wait_send())

    for q in range(4):
        @pl.when(jnp.logical_not(iterates & (core == 0) & (y == q)))
        def _():
            remote(last_grams.at[q], last_grams.at[q], fin_send.at[0, 0, 0], fin_recv.at[q], sibling).wait_recv()
    packed = four(last_grams)
    packed = jnp.concatenate([packed[:, 32 * n:32 * n + 32] for n in range(4)], axis=0)
    inverse = inverse_factor(jnp.concatenate([packed, jnp.zeros((32, 96), F32)], axis=1))

    @pl.when(jnp.logical_not(iterates & (core == 0) & (y == lax.div(z_lo, 2))))
    def _():
        remote(last_rows, last_rows, row_send.at[0, 0, 0], row_recv.at[0], sibling).wait_recv()

    out_ref[...] = dot(inverse, last_rows[...], ((1,), (0,)), HIGH) * math.sqrt(SNAPS)

    for n, t in enumerate((2, 10)):
        @pl.when(giver & (row != t))
        def _():
            basis_copy(n, t).wait_send()
    each_gather(lambda copy: remote(*copy).wait_send())


VMEM = pl.BlockSpec(memory_space=pltpu.VMEM)
ANY = pl.BlockSpec(memory_space=pl.ANY)
DMA = pltpu.SemaphoreType.DMA


def body(snapshots, start_block):
    out = pl.pallas_call(
        kernel,
        out_shape=jax.ShapeDtypeStruct((32, 128), F32),
        in_specs=[ANY, ANY],
        out_specs=VMEM,
        scratch_shapes=[
            pltpu.VMEM((2, 4, 8, 16, 128), BF16),
            pltpu.VMEM((2, 4, 8, 4, 16, 128), BF16),
            pltpu.VMEM((2, 4, 8, 4, 16, 128), BF16),
            pltpu.VMEM((2, 4, 4, 16, 512), F32),
            pltpu.VMEM((4, 4, 16, 512), F32),
            pltpu.VMEM((16, 16, 512), F32),
            pltpu.VMEM((4, 16, 512), F32),
            pltpu.VMEM((3, 16, 512), F32),
            pltpu.VMEM((6, 16, 512), F32),
            pltpu.VMEM((2, 16, 512), F32),
            pltpu.VMEM((2, 16, 512), F32),
            pltpu.VMEM((16, 512), F32),
            pltpu.VMEM((4, 128, 32), F32),
            pltpu.VMEM((384, 640), F32),
            pltpu.VMEM((512, 512), BF16),
            pltpu.VMEM((512, 512), BF16),
            pltpu.VMEM((8, 8, 256), F32),
            pltpu.VMEM((8, 8, 512), F32),
            pltpu.VMEM((128, 512), F32),
            pltpu.VMEM((6, 2, 4, 32, 256), F32),
            pltpu.VMEM((2, 4, 32, 128), F32),
            pltpu.VMEM((32, 512), F32),
            pltpu.VMEM((32, 128), F32),
            pltpu.VMEM((4, 8, 128), F32),
            DMA((1,)), DMA((2,)), DMA((2,)), DMA((2, 2)), DMA((2, 2)), DMA((2, 2)), DMA((2, 2)),
            DMA((4,)), DMA((4,)), DMA((5,)), DMA((5,)), DMA((4,)), DMA((1,)), DMA((3,)), DMA((4,)),
            DMA((3,)), DMA((3,)), DMA((2,)), DMA((2,)), DMA((2,)), DMA((2,)),
            DMA((6, 2)), DMA((6, 2)), DMA((2, 4)), DMA((2, 4)), DMA((4, 4, 2)), DMA((4,)),
            DMA((4, 2, 2)), DMA((1,)),
        ],
        compiler_params=pltpu.CompilerParams(
            collective_id=1, has_side_effects=True, vmem_limit_bytes=48 << 20),
        name="subspace",
    )(snapshots, start_block)
    return out.T


def solution(mesh):
    placed = (P(("row", "col"), "feat"), P("row", None))
    return jax.shard_map(
        body, mesh=mesh, in_specs=placed, out_specs=P("row", None), check_vma=False
    )
```
